32 devices in a mesh: grp: 2 (over y), gx: 4 (over z), gy: 2 (over x), gz: 2 (over core).
Axes of the slice: x: 2, y: 2, z: 4, core: 2. Of those that a mesh axis runs over, the one named last changes fastest.
Arguments:
- innovation: float32 [10, 4, 64, 216], P('grp', 'gz', 'gx', 'gy'), parts along dimension 0, may hold values from -36 to 36
- obs_precision: float32 [10, 4, 64, 216], P('grp', 'gz', 'gx', 'gy'), parts along dimension 0, may hold values from 0.3 to 3
- error_scale: float32 [5, 4, 64, 216], P(None, 'gz', 'gx', 'gy'), may hold values from 0.3 to 3
- kappa_x: float32 [4, 64, 216], P('gz', 'gx', 'gy'), may hold values from 0.04 to 0.24
- kappa_y: float32 [4, 64, 216], P('gz', 'gx', 'gy'), may hold values from 0.04 to 0.24
- sea_mask: int32 [4, 64, 216], P('gz', 'gx', 'gy'), may hold values 0 or 1
- members: float32 [32, 5, 4, 64, 216], P('grp', None, 'gz', 'gx', 'gy'), parts along dimension 0, may hold values from -6 to 6
- vertical: float32 [5, 4, 4], replicated, may hold values from -3 to 3
- diffusion_steps: int32 [5], replicated, may hold values from 5 to 10, as said below
Outputs:
- control_field: float32 [10, 4, 64, 216], P('grp', 'gz', 'gx', 'gy'), parts along dimension 0
- control_weights: float32 [32], P('grp'), parts along dimension 0
- residual_field: float32 [10, 4, 64, 216], P('grp', 'gz', 'gx', 'gy'), parts along dimension 0
The draws below stay inside these ranges and needn't reach their ends.
There are 2 independent parts, one for each index of `grp`. The reference program is written for one: setup_inputs(seed, part) draws one part's arguments, and reference() takes and returns one part's arrays. A program takes and returns all parts, laid end to end along the dimension named above; an argument that names none is the same for every part. Nothing has to cross between parts.
Inputs may be any that keep to these rules, and one draw needn't show every extreme that they name: `diffusion_steps`: each field's number of diffusion steps; at least one field takes all 10.
All inputs are finite; a program needn't handle non-finite values. No bound on the sum of `sea_mask` on one device may be relied on, other than what follows from the above.
Results may differ from the reference program's by a relative error of at most 0.0004.
Values sent between devices are 32-bit elements; how exact they have to be, the bound alone decides.
No kernel may reach another device: no remote copies, remote signals or barrier semaphores. Data moves between devices by JAX's collectives and lax.ppermute only.
A program may use at most 64 MiB of HBM per device.

```python
import math
import jax
import jax.numpy as jnp
from jax import lax

F = 5
LEV = 4
M = 16
KMAX = 10
ITERS = 2
NX = 64
NY = 216


def draw_innovation(key, part):
    key = jax.random.fold_in(key, 11)
    x_position = jnp.arange(NX, dtype=jnp.float32) / NX
    y_position = jnp.arange(NY, dtype=jnp.float32) / NY
    growth = jnp.exp(math.log(3.0) * (x_position[:, None] + y_position[None, :]))
    values = jnp.clip(jax.random.normal(key, (F, LEV, NX, NY), jnp.float32), -4.0, 4.0)
    return (values * growth).astype(jnp.float32)


def draw_diffusion_steps(key, part):
    key = jax.random.fold_in(key, 5)
    step_counts = jax.random.randint(key, (F,), KMAX // 2, KMAX + 1)
    chosen = jax.random.randint(jax.random.fold_in(key, 1), (), 0, F)
    return jnp.where(jnp.arange(F) == chosen, KMAX, step_counts).astype(jnp.int32)


def place_ends(entries, rng, least, largest):
    longest = entries.shape.index(max(entries.shape))
    spots = []
    for shift in (0, 1):
        where = [jax.random.randint(jax.random.fold_in(rng, axis), (), 0, length) for axis, length in enumerate(entries.shape)]
        where[longest] = (where[longest] + shift) % entries.shape[longest]
        spots.append(tuple(where))
    return entries.at[spots[0]].set(least).at[spots[1]].set(largest)


def steps_of(own_key, shape, pieces, smallest, top_value):
    def one(position, shards_of):
        steps = jax.random.uniform(jax.random.fold_in(jax.random.fold_in(own_key, 6), position), (shards_of,), jnp.float32, smallest / len(pieces), top_value / len(pieces))
        return jnp.repeat(jnp.exp(steps), shape[position] // shards_of).reshape((-1,) + (1,) * (len(shape) - position - 1))

    level = one(*pieces[0])
    for cut in pieces[1:]:
        level = level * one(*cut)
    return level


def centred(stream_key, extent, scale, bound, shards=(), held_as=jnp.bfloat16):
    level = steps_of(stream_key, extent, shards, -0.22, 0.18) if shards else 1.0
    result = jax.random.normal(stream_key, extent, jnp.float32) * scale * level
    return jnp.minimum(jnp.maximum(result, -bound), bound).astype(held_as)


def setup_inputs(seed: int = 0, part: int = 0) -> dict:
    key_list = jax.random.split(jax.random.key(seed), 10)
    own_keys = jax.random.split(jax.random.fold_in(key_list[9], part), 10)
    return {
        "innovation": draw_innovation(jax.random.fold_in(jax.random.fold_in(key_list[9], part), 71), part),
        "obs_precision": jnp.clip(jnp.exp(math.log(3.0) - 2.3025851 * jax.random.uniform(own_keys[1], (F, LEV, NX, NY), jnp.float32) ** steps_of(own_keys[1], (F, LEV, NX, NY), ((1, 2), (2, 4), (3, 2)), -0.2, 0.2)), 0.3, 3.0),
        "error_scale": jnp.clip(jnp.exp(math.log(3.0) - 2.3025851 * jax.random.uniform(key_list[2], (F, LEV, NX, NY), jnp.float32) ** steps_of(key_list[2], (F, LEV, NX, NY), ((1, 2), (2, 4), (3, 2)), -0.2, 0.2)), 0.3, 3.0),
        "kappa_x": jnp.clip(0.04 + 0.19999999552965164 * jax.random.uniform(key_list[3], (LEV, NX, NY), jnp.float32) ** steps_of(key_list[3], (LEV, NX, NY), ((0, 2), (1, 4), (2, 2)), -0.2, 0.2), 0.04, 0.24),
        "kappa_y": jnp.clip(0.04 + 0.19999999552965164 * jax.random.uniform(key_list[4], (LEV, NX, NY), jnp.float32) ** steps_of(key_list[4], (LEV, NX, NY), ((0, 2), (1, 4), (2, 2)), -0.2, 0.2), 0.04, 0.24),
        "sea_mask": place_ends((jax.random.randint(key_list[5], (LEV, NX, NY), 0, 4) < 3).astype(jnp.int32), jax.random.fold_in(key_list[5], 1), 0, 1),
        "members": centred(own_keys[6], (M, F, LEV, NX, NY), 1.0, 6.0, ((2, 2), (3, 4), (4, 2)), jnp.float32),
        "vertical": centred(key_list[7], (F, LEV, LEV), 0.5, 3.0, (), jnp.float32),
        "diffusion_steps": draw_diffusion_steps(jax.random.fold_in(key_list[9], 71), part),
    }


static_share = 0.6
ensemble_share = 0.4

def level_mix(source, mixing):
    return jnp.einsum('flk,fkxy->flxy', mixing, source, precision=lax.Precision.HIGHEST)

def diffuse(source, east_coef, north_coef, step_counts):
    current = source
    for number in range(KMAX):
        active = (step_counts > number).astype(jnp.float32)[:, None, None, None]
        flux_east = east_coef * (jnp.roll(current, -1, axis=2) - current)
        shifted_north = jnp.concatenate([current[:, :, :, 1:], jnp.zeros_like(current[:, :, :, :1])], axis=3)
        flux_north = north_coef * (shifted_north - current)
        div_east = flux_east - jnp.roll(flux_east, 1, axis=2)
        div_north = flux_north - jnp.concatenate([jnp.zeros_like(flux_north[:, :, :, :1]), flux_north[:, :, :, :-1]], axis=3)
        current = current + active * (div_east + div_north)
    return current

def reference(innovation, obs_precision, error_scale, kappa_x, kappa_y, sea_mask, members, vertical, diffusion_steps):
    wet_cells = sea_mask.astype(jnp.float32)
    wet_next_x = jnp.roll(wet_cells, -1, axis=1)
    east_coef = kappa_x * wet_cells * wet_next_x
    wet_next_y = jnp.concatenate([wet_cells[:, :, 1:], jnp.zeros_like(wet_cells[:, :, :1])], axis=2)
    north_coef = kappa_y * wet_cells * wet_next_y
    transposed = jnp.swapaxes(vertical, 1, 2)
    sqrt_static = math.sqrt(static_share)
    ens_scale = math.sqrt(ensemble_share / (M - 1))

    def apply_forward(control, weights):
        static = error_scale * level_mix(diffuse(control, east_coef, north_coef, diffusion_steps), vertical)
        ensemble = jnp.einsum('m,mflxy->flxy', weights, members, precision=lax.Precision.HIGHEST)
        return wet_cells * (sqrt_static * static + ens_scale * ensemble)

    def apply_back(weighted):
        masked = wet_cells * weighted
        back_field = sqrt_static * diffuse(level_mix(error_scale * masked, transposed), east_coef, north_coef, diffusion_steps)
        back_weights = ens_scale * jnp.einsum('mflxy,flxy->m', members, masked, precision=lax.Precision.HIGHEST)
        return (back_field, back_weights)
    resid_field, resid_weights = apply_back(obs_precision * innovation)
    dir_field, dir_weights = (resid_field, resid_weights)
    control_field = jnp.zeros_like(resid_field)
    control_weights = jnp.zeros((M,), jnp.float32)
    norm_now = jnp.sum(resid_field * resid_field) + jnp.sum(resid_weights * resid_weights)
    for iteration in range(ITERS):
        observed = apply_forward(dir_field, dir_weights)
        back_field, back_weights = apply_back(obs_precision * observed)
        image_field = dir_field + back_field
        image_weights = dir_weights + back_weights
        curvature = jnp.sum(dir_field * image_field) + jnp.sum(dir_weights * image_weights)
        step_length = norm_now / curvature
        control_field = control_field + step_length * dir_field
        control_weights = control_weights + step_length * dir_weights
        resid_field = resid_field - step_length * image_field
        resid_weights = resid_weights - step_length * image_weights
        if iteration + 1 < ITERS:
            norm_next = jnp.sum(resid_field * resid_field) + jnp.sum(resid_weights * resid_weights)
            ratio_next = norm_next / norm_now
            dir_field = resid_field + ratio_next * dir_field
            dir_weights = resid_weights + ratio_next * dir_weights
            norm_now = norm_next
    return (control_field, control_weights, resid_field)
```

```python
import functools
import math


import jax
import jax.numpy as jnp
from jax import lax
from jax.experimental import pallas as pl
from jax.experimental.pallas import tpu as pltpu
from jax.sharding import PartitionSpec as P

KMAX = 10
ITERS = 2


static_share = 0.6
ensemble_share = 0.4


def extended(cells, sides, width):
    for axis, dim in sides:
        count = lax.axis_size(axis)
        head = lax.slice_in_dim(cells, 0, width, axis=dim)
        tail = lax.slice_in_dim(cells, cells.shape[dim] - width, cells.shape[dim], axis=dim)
        cells = jnp.concatenate(
            [
                lax.ppermute(tail, axis, [(i, (i + 1) % count) for i in range(count)]),
                cells,
                lax.ppermute(head, axis, [((i + 1) % count, i) for i in range(count)]),
            ],
            axis=dim,
        )
    return cells


def level_mix(source, mixing):
    local_levels = source.shape[1]
    gathered = lax.all_gather(source, "gz", axis=1, tiled=True)
    own_rows = lax.dynamic_slice_in_dim(
        mixing, lax.axis_index("gz") * local_levels, local_levels, 1
    )
    return jnp.einsum("flk,fkxy->flxy", own_rows, gathered, precision=lax.Precision.HIGHEST)


def diffuse(source, padded, step_counts, halo_depth):
    current = source
    for segment in range(KMAX // halo_depth):
        current = extended(current, (("gx", 2), ("gy", 3)), halo_depth)
        for substep in range(halo_depth):
            number = segment * halo_depth + substep
            offset = KMAX - halo_depth + substep
            rows_now = current.shape[2]
            cols_now = current.shape[3]
            window = padded[:, :, offset : offset + rows_now, offset : offset + cols_now]
            east_kappa = window[0]
            north_kappa = window[1]
            wet_window = window[2]
            east_coef = east_kappa[:, :-1, :] * wet_window[:, :-1, :] * wet_window[:, 1:, :]
            flux_east = east_coef * (current[:, :, 1:, :] - current[:, :, :-1, :])
            div_east = (flux_east[:, :, 1:, :] - flux_east[:, :, :-1, :])[:, :, :, 1:-1]
            north_coef = north_kappa[:, :, :-1] * wet_window[:, :, :-1] * wet_window[:, :, 1:]
            flux_north = north_coef * (current[:, :, :, 1:] - current[:, :, :, :-1])
            div_north = (flux_north[:, :, :, 1:] - flux_north[:, :, :, :-1])[:, :, 1:-1, :]
            active = (step_counts > number).astype(jnp.float32)[:, None, None, None]
            current = current[:, :, 1:-1, 1:-1] + active * (div_east + div_north)
    return current


def both_sums(terms, partial_value):
    return lax.psum((terms, partial_value), ("gx", "gy", "gz"))


def squares(resid_field):
    return lax.psum(jnp.sum(resid_field * resid_field), ("gx", "gy", "gz"))


def shards_any(
    innovation,
    obs_precision,
    error_scale,
    kappa_x,
    kappa_y,
    sea_mask,
    members,
    vertical,
    diffusion_steps,
):
    wet_cells = sea_mask.astype(jnp.float32)
    coefficients = jnp.stack([kappa_x, kappa_y, wet_cells])
    padded = extended(coefficients, (("gx", 2), ("gy", 3)), KMAX)
    cols_dev = wet_cells.shape[2]
    y_position = (
        lax.axis_index("gy") * cols_dev + jnp.arange(cols_dev + 2 * KMAX, dtype=jnp.int32) - KMAX
    )
    inside = ((y_position >= 0) & (y_position < cols_dev * lax.axis_size("gy"))).astype(jnp.float32)
    padded = jnp.stack([padded[0], padded[1], padded[2] * inside[None, None, :]])
    halo_depth = 2
    transposed = jnp.swapaxes(vertical, 1, 2)
    sqrt_static = math.sqrt(static_share)
    ens_scale = math.sqrt(ensemble_share / (members.shape[0] - 1))

    def static_back(masked):
        return sqrt_static * diffuse(
            level_mix(error_scale * masked, transposed), padded, diffusion_steps, halo_depth
        )

    def ensemble_terms(masked):
        return jnp.einsum("mflxy,flxy->m", members, masked, precision=lax.Precision.HIGHEST)

    masked = wet_cells * (obs_precision * innovation)
    resid_field = static_back(masked)
    ens_sum, field_norm = both_sums(ensemble_terms(masked), jnp.sum(resid_field * resid_field))
    resid_weights = ens_scale * ens_sum
    norm_now = field_norm + jnp.sum(resid_weights * resid_weights)
    dir_field, dir_weights = (resid_field, resid_weights)
    control_field = jnp.zeros_like(resid_field)
    control_weights = jnp.zeros(resid_weights.shape, jnp.float32)
    for iteration in range(ITERS):
        static = error_scale * level_mix(
            diffuse(dir_field, padded, diffusion_steps, halo_depth), vertical
        )
        ensemble = jnp.einsum(
            "m,mflxy->flxy", dir_weights, members, precision=lax.Precision.HIGHEST
        )
        observed = wet_cells * (sqrt_static * static + ens_scale * ensemble)
        weighted = obs_precision * observed
        masked = wet_cells * weighted
        image_field = dir_field + static_back(masked)
        ens_sum, curve_part = both_sums(ensemble_terms(masked), jnp.sum(dir_field * image_field))
        image_weights = dir_weights + ens_scale * ens_sum
        curvature = curve_part + jnp.sum(dir_weights * image_weights)
        step_length = norm_now / curvature
        control_field = control_field + step_length * dir_field
        control_weights = control_weights + step_length * dir_weights
        resid_field = resid_field - step_length * image_field
        resid_weights = resid_weights - step_length * image_weights
        if iteration + 1 < ITERS:
            norm_next = squares(resid_field) + jnp.sum(resid_weights * resid_weights)
            ratio_next = norm_next / norm_now
            dir_field = resid_field + ratio_next * dir_field
            dir_weights = resid_weights + ratio_next * dir_weights
            norm_now = norm_next
    return (control_field, control_weights, resid_field)

ROWS = 16
WIN = 56
LANES = 128
DEPTH = 2 * KMAX
GROUP = LANES // DEPTH
SUMS = 8
AXES = ("gx", "gy", "gz")
VMEM = pl.BlockSpec(memory_space=pltpu.VMEM)
SMEM = pl.BlockSpec(memory_space=pltpu.SMEM)
SQRT_STATIC = math.sqrt(static_share)


def f32(*shape):
    return jax.ShapeDtypeStruct(shape, jnp.float32)


def call(kernel, outs, specs, args, scratch=()):
    return pl.pallas_call(
        kernel,
        out_shape=outs,
        in_specs=specs,
        out_specs=[VMEM] * len(outs),
        scratch_shapes=list(scratch),
        compiler_params=pltpu.CompilerParams(vmem_limit_bytes=32 * 1024 * 1024),
    )(*args)


def lanes_of(shape):
    return lax.broadcasted_iota(jnp.int32, shape, len(shape) - 1)


def tile(ref, index, size=ROWS):
    return ref[index * size : (index + 1) * size, :]


def pack_edges(out_ref, planes, cols):
    first = jnp.where(lax.axis_index("gy") == 0, cols - DEPTH, 0)
    lane = lanes_of((ROWS, LANES))
    for group in range(-(-len(planes) // GROUP)):
        packed = jnp.zeros((ROWS, LANES), jnp.float32)
        for slot, plane in enumerate(planes[group * GROUP : (group + 1) * GROUP]):
            moved = pltpu.roll(plane, lax.rem(DEPTH * slot - first + LANES, LANES), 1)
            packed = jnp.where((lane >= DEPTH * slot) & (lane < DEPTH * (slot + 1)), moved, packed)
        out_ref[group * ROWS : (group + 1) * ROWS, :] = packed


def with_edge(own, edge_ref, index, cols):
    group, slot = divmod(index, GROUP)
    moved = pltpu.roll(tile(edge_ref, group), (cols - DEPTH * slot) % LANES, 1)
    return jnp.where(lanes_of(own.shape) < cols, own, moved)


def over_rows(values):
    return jnp.sum(values, axis=0, keepdims=True)


def observe(first, planes, levels, cols, members_count, with_weights):
    ens_scale = math.sqrt(ensemble_share / (members_count - 1))
    base = planes * ROWS

    def kernel(*refs):
        if first:
            innov, prec, scale, mask, kx, ky, members, out_z, out_e, coef = refs
        elif with_weights:
            own, other, weights, sums, vert, prec, scale, mask, members, out_z, out_e, out_q = refs
        else:
            own, other, weights, sums, vert, prec, scale, mask, members, seen, out_z, out_e = refs
        out_z[...] = jnp.zeros(out_z.shape, jnp.float32)
        totals = [jnp.zeros((ROWS, cols), jnp.float32) for _ in range(members_count)]
        energy = jnp.zeros((ROWS, cols), jnp.float32)
        cross = jnp.zeros((ROWS, cols), jnp.float32)
        here = lax.axis_index("gz") * levels
        there = (1 - lax.axis_index("gz")) * levels
        for plane in range(planes):
            field, level = divmod(plane, levels)
            wet = mask[level].astype(jnp.float32)
            if first:
                weighted = wet * (prec[plane] * innov[plane])
            else:
                static = jnp.zeros((ROWS, cols), jnp.float32)
                for k in range(levels):
                    row = (field * 2 * levels + here + level) * 2 * levels
                    static += vert[row + here + k] * tile(own, field * levels + k)[:, :cols]
                    static += vert[row + there + k] * tile(other, field * levels + k)[:, :cols]
                ensemble = jnp.zeros((ROWS, cols), jnp.float32)
                for m in range(members_count):
                    ensemble += weights[m : m + 1, :cols] * members[m, plane]
                seen_now = wet * (SQRT_STATIC * (scale[plane] * static) + ens_scale * ensemble)
                weighted = wet * (prec[plane] * seen_now)
                energy += seen_now * weighted
                if with_weights:
                    out_q[plane] = weighted
                else:
                    cross += seen_now * seen[plane]
            if with_weights:
                for m in range(members_count):
                    totals[m] += members[m, plane] * weighted
            out_z[plane * ROWS : (plane + 1) * ROWS, :cols] = scale[plane] * weighted
        if with_weights:
            for m in range(members_count):
                out_z[base + m : base + m + 1, :cols] = ens_scale * over_rows(totals[m])
        if not first:
            sums_at = base + ROWS * with_weights
            out_z[sums_at : sums_at + SUMS, :] = sums[...]
            out_z[sums_at : sums_at + 1, :cols] = over_rows(energy)
            if not with_weights:
                out_z[sums_at + 1 : sums_at + 2, :cols] = over_rows(cross)
        edges = [tile(out_z, plane) for plane in range(planes)]
        if first:
            coef[...] = jnp.zeros(coef.shape, jnp.float32)
            for level in range(levels):
                for kind, source in enumerate((kx, ky, mask)):
                    at = (kind * levels + level) * ROWS
                    coef[at : at + ROWS, :cols] = source[level].astype(jnp.float32)
            edges += [tile(coef, index) for index in range(3 * levels)]
        packed = -(-len(edges) // GROUP) * ROWS
        pack_edges(out_e, edges, cols)
        out_e[packed:, :] = out_z[base:, :]

    tail = (ROWS * with_weights) + (0 if first else SUMS)
    edge_rows = -(-(planes + (3 * levels if first else 0)) // GROUP) * ROWS + tail
    outs = [f32(base + tail, LANES), f32(edge_rows, LANES)]
    if first:
        outs.append(f32(3 * levels * ROWS, LANES))
    elif with_weights:
        outs.append(f32(planes, ROWS, cols))
    return kernel, outs


def mix_back(first, planes, levels, cols, tail):
    base = planes * ROWS
    coefs = 3 * levels if first else 0
    fields = planes // levels

    def kernel(*refs):
        if first:
            own, other, edge, edge_other, vert, coef, out_all, out_near = refs
        else:
            own, other, edge, edge_other, vert, out_all, out_near = refs
        here = lax.axis_index("gz") * levels
        there = (1 - lax.axis_index("gz")) * levels
        upper = lax.broadcasted_iota(jnp.int32, (8, LANES), 0) < 4

        def put(index, values):
            out_all[index * ROWS : (index + 1) * ROWS, :] = values
            out_near[index * 8 : (index + 1) * 8, :] = jnp.where(upper, values[:8], values[8:])

        for field in range(fields):
            mine = [with_edge(tile(own, field * levels + l), edge, field * levels + l, cols) for l in range(levels)]
            theirs = [
                with_edge(tile(other, field * levels + l), edge_other, field * levels + l, cols) for l in range(levels)
            ]
            for k in range(levels):
                mixed = jnp.zeros((ROWS, LANES), jnp.float32)
                for l in range(levels):
                    block = field * 2 * levels
                    mixed += vert[(block + here + l) * 2 * levels + here + k] * mine[l]
                    mixed += vert[(block + there + l) * 2 * levels + here + k] * theirs[l]
                put(field * levels + k, mixed)
        for index in range(coefs):
            put(planes + index, with_edge(tile(coef, index), edge, planes + index, cols))
        packed = -(-(planes + coefs) // GROUP) * ROWS
        total = (own[base:, :] + other[base:, :]) + (edge[packed:, :] + edge_other[packed:, :])
        out_all[(planes + coefs) * ROWS :, :] = total
        out_near[(planes + coefs) * 8 :, :] = total

    count = planes + coefs
    return kernel, [f32(count * ROWS + tail, LANES), f32(count * 8 + tail, LANES)]


def window(target, index, own, after, near, before, slot):
    target[index, 0:16, :] = tile(own, slot)
    target[index, 16:32, :] = tile(after, slot)
    target[index, 32:40, :] = tile(near, slot, 8)
    target[index, 40:56, :] = tile(before, slot)


def run_steps(start, other, coef, steps, planes, levels):
    def one(number, source, target):
        for level in range(levels):
            for field in range(planes // levels):
                plane = field * levels + level
                u = source[plane]
                rows = u.shape[0]
                change = (
                    coef[0, level] * pltpu.roll(u, rows - 1, 0)
                    + coef[1, level] * pltpu.roll(u, 1, 0)
                    + coef[2, level] * pltpu.roll(u, LANES - 1, 1)
                    + coef[3, level] * pltpu.roll(u, 1, 1)
                    - coef[4, level] * u
                )
                active = jnp.where(steps[field] > number, 1.0, 0.0).astype(jnp.float32)
                target[plane] = u + active * change

    def pair(index, carry):
        one(2 * index, start, other)
        one(2 * index + 1, other, start)
        return carry

    lax.fori_loop(0, KMAX // 2, pair, 0)


def make_coefs(coef, kinds, levels, cols):
    lane = lanes_of((WIN, LANES))
    last = jnp.where(lax.axis_index("gy") == 0, LANES - 1, cols - 1)
    for level in range(levels):
        kx, ky, wet = (kinds[kind * levels + level] for kind in range(3))
        east = kx * wet * pltpu.roll(wet, WIN - 1, 0)
        north = ky * wet * pltpu.roll(wet, LANES - 1, 1)
        north = jnp.where(lane == last, 0.0, north)
        west = pltpu.roll(east, 1, 0)
        south = pltpu.roll(north, 1, 1)
        for index, values in enumerate((east, west, north, south, (east + west) + (north + south))):
            coef[index, level] = values


def own_sum(values, cols):
    own = values[:ROWS]
    return over_rows(jnp.where(lanes_of(own.shape) < cols, own, 0.0))


def spread(values):
    return jnp.broadcast_to(jnp.sum(values, axis=1, keepdims=True), values.shape)


def first_diffuse(planes, levels, cols):
    coefs = 3 * levels

    def kernel(own, after, near, before, steps, coef, resid, weights, sums, out_g, buf, kinds):
        for plane in range(planes):
            window(buf, plane, own, after, near, before, plane)
        for index in range(coefs):
            window(kinds, index, own, after, near, before, planes + index)
        make_coefs(coef, kinds, levels, cols)
        at, near_at = (planes + coefs) * ROWS, (planes + coefs) * 8
        weights[...] = spread((own[at:, :] + after[at:, :]) + (near[near_at:, :] + before[at:, :]))
        run_steps(buf, resid, coef, steps, planes, levels)
        squares = jnp.zeros((ROWS, LANES), jnp.float32)
        for plane in range(planes):
            value = SQRT_STATIC * buf[plane]
            resid[plane] = value
            buf[plane] = value
            squares += value[:ROWS] * value[:ROWS]
        sums[...] = jnp.zeros(sums.shape, jnp.float32)
        sums[2:3, :] = own_sum(squares, cols)
        run_steps(buf, kinds, coef, steps, planes, levels)
        for plane in range(planes):
            out_g[plane * ROWS : (plane + 1) * ROWS, :] = buf[plane, :ROWS, :]

    outs = [
        f32(5, levels, WIN, LANES),
        f32(planes, WIN, LANES),
        f32(ROWS, LANES),
        f32(SUMS, LANES),
        f32(planes * ROWS, LANES),
    ]
    scratch = [pltpu.VMEM((planes, WIN, LANES), jnp.float32)] * 2
    return kernel, outs, scratch


def second_diffuse(planes, levels, cols):
    def kernel(own, after, near, before, steps, coef, resid, weights, image, new, new_w, sums, facts, out_g, buf, spare):
        for plane in range(planes):
            window(buf, plane, own, after, near, before, plane)
        at, near_at = planes * ROWS, planes * 8
        total = spread((own[at:, :] + after[at:, :]) + (near[near_at:, :] + before[at:, :]))
        energy = total[ROWS : ROWS + 1]
        rr = total[ROWS + 2 : ROWS + 3] + over_rows(weights[...] * weights[...])
        curvature = rr + energy
        step = rr / curvature
        new_weights = weights[...] - step * (weights[...] + total[:ROWS])
        new_w[...] = new_weights
        facts[...] = jnp.zeros(facts.shape, jnp.float32)
        facts[0:1, :] = rr
        facts[1:2, :] = energy
        facts[2:3, :] = step
        run_steps(buf, spare, coef, steps, planes, levels)
        squares = jnp.zeros((ROWS, LANES), jnp.float32)
        cross = jnp.zeros((ROWS, LANES), jnp.float32)
        for plane in range(planes):
            direction = resid[plane]
            image_now = direction + SQRT_STATIC * buf[plane]
            value = direction - step * image_now
            image[plane * ROWS : (plane + 1) * ROWS, :] = image_now[:ROWS]
            new[plane * ROWS : (plane + 1) * ROWS, :] = value[:ROWS]
            buf[plane] = value
            squares += value[:ROWS] * value[:ROWS]
            cross += value[:ROWS] * direction[:ROWS]
        sums[...] = jnp.zeros(sums.shape, jnp.float32)
        sums[2:3, :] = own_sum(squares, cols)
        sums[3:4, :] = own_sum(cross, cols)
        run_steps(buf, spare, coef, steps, planes, levels)
        for plane in range(planes):
            out_g[plane * ROWS : (plane + 1) * ROWS, :] = buf[plane, :ROWS, :]

    block = f32(planes * ROWS, LANES)
    outs = [block, block, f32(ROWS, LANES), f32(SUMS, LANES), f32(SUMS, LANES), block]
    scratch = [pltpu.VMEM((planes, WIN, LANES), jnp.float32)] * 2
    return kernel, outs, scratch


def last_diffuse(planes, levels, cols):
    def kernel(
        own, after, near, before, steps, coef, resid, weights, image, new, new_w, facts, control, control_w, final, buf, spare
    ):
        for plane in range(planes):
            window(buf, plane, own, after, near, before, plane)
        at, near_at = planes * ROWS, planes * 8
        total = spread((own[at:, :] + after[at:, :]) + (near[near_at:, :] + before[at:, :]))
        rr, energy, step = facts[0:1, :], facts[1:2, :], facts[2:3, :]
        new_energy, cross_energy = total[0:1], total[1:2]
        new_rr = total[2:3] + over_rows(new_w[...] * new_w[...])
        cross_rr = total[3:4] + over_rows(new_w[...] * weights[...])
        ratio = new_rr / rr
        squares = new_rr + ratio * (2.0 * cross_rr + ratio * rr)
        curvature = squares + (new_energy + ratio * (2.0 * cross_energy + ratio * energy))
        new_step = new_rr / curvature
        control_w[...] = step * weights[...] + new_step * (new_w[...] + ratio * weights[...])
        run_steps(buf, spare, coef, steps, planes, levels)
        for plane in range(planes):
            value = tile(new, plane)
            direction = resid[plane, :ROWS, :]
            new_direction = value + ratio * direction
            new_image = (value + SQRT_STATIC * buf[plane, :ROWS, :]) + ratio * tile(image, plane)
            control[plane] = (step * direction + new_step * new_direction)[:, :cols]
            final[plane] = (value - new_step * new_image)[:, :cols]

    outs = [f32(planes, ROWS, cols), f32(ROWS, LANES), f32(planes, ROWS, cols)]
    scratch = [pltpu.VMEM((planes, WIN, LANES), jnp.float32)] * 2
    return kernel, outs, scratch


def moved_to(values, dx, dy, dz):
    sizes = [lax.axis_size(axis) for axis in AXES]
    pairs = []
    for x in range(sizes[0]):
        for y in range(sizes[1]):
            for z in range(sizes[2]):
                to = ((x + dx) % sizes[0] * sizes[1] + (y + dy) % sizes[1]) * sizes[2] + (z + dz) % sizes[2]
                pairs.append(((x * sizes[1] + y) * sizes[2] + z, to))
    return lax.ppermute(values, AXES, pairs)


def across(kernel_of, out_z, out_e, vert, extra):
    other = moved_to(out_z, 0, 0, 1)
    edge = moved_to(out_e, 0, 1, 0)
    edge_other = moved_to(out_e, 0, 1, 1)
    kernel, outs = kernel_of
    specs = [VMEM] * 4 + [SMEM] + [VMEM] * len(extra)
    own, near = call(kernel, outs, specs, (out_z, other, edge, edge_other, vert, *extra))
    return own, moved_to(own, -1, 0, 0), moved_to(near, 2, 0, 0), moved_to(own, 1, 0, 0)


def shards_small(
    innovation, obs_precision, error_scale, kappa_x, kappa_y, sea_mask, members, vertical, diffusion_steps
):
    fields, levels, rows, cols = innovation.shape
    count = members.shape[0]
    planes = fields * levels
    block = (planes, rows, cols)
    innov, prec, scale = (a.reshape(block) for a in (innovation, obs_precision, error_scale))
    ens = members.reshape((count,) + block)
    vert = vertical.reshape(-1)

    kernel, outs = observe(True, planes, levels, cols, count, True)
    out_z, out_e, coef_own = call(kernel, outs, [VMEM] * 7, (innov, prec, scale, sea_mask, kappa_x, kappa_y, ens))
    parts = across(mix_back(True, planes, levels, cols, ROWS), out_z, out_e, vert, (coef_own,))
    kernel, outs, scratch = first_diffuse(planes, levels, cols)
    specs = [VMEM] * 4 + [SMEM]
    coef, resid, weights, sums, out_g = call(kernel, outs, specs, (*parts, diffusion_steps), scratch)

    kernel, outs = observe(False, planes, levels, cols, count, True)
    specs = [VMEM] * 4 + [SMEM] + [VMEM] * 4
    args = (out_g, moved_to(out_g, 0, 0, 1), weights, sums, vert, prec, scale, sea_mask, ens)
    out_z, out_e, seen = call(kernel, outs, specs, args)
    parts = across(mix_back(False, planes, levels, cols, ROWS + SUMS), out_z, out_e, vert, ())
    kernel, outs, scratch = second_diffuse(planes, levels, cols)
    specs = [VMEM] * 4 + [SMEM] + [VMEM] * 3
    image, new, new_w, sums, facts, out_g = call(
        kernel, outs, specs, (*parts, diffusion_steps, coef, resid, weights), scratch
    )

    kernel, outs = observe(False, planes, levels, cols, count, False)
    specs = [VMEM] * 4 + [SMEM] + [VMEM] * 5
    args = (out_g, moved_to(out_g, 0, 0, 1), new_w, sums, vert, prec, scale, sea_mask, ens, seen)
    out_z, out_e = call(kernel, outs, specs, args)
    parts = across(mix_back(False, planes, levels, cols, SUMS), out_z, out_e, vert, ())
    kernel, outs, scratch = last_diffuse(planes, levels, cols)
    specs = [VMEM] * 4 + [SMEM] + [VMEM] * 7
    control, control_w, final = call(
        kernel, outs, specs, (*parts, diffusion_steps, coef, resid, weights, image, new, new_w, facts), scratch
    )
    return control.reshape(innovation.shape), control_w[:, 0], final.reshape(innovation.shape)


def shards(innovation, obs_precision, error_scale, kappa_x, kappa_y, sea_mask, members, vertical, diffusion_steps):
    arrays = (innovation, obs_precision, error_scale, kappa_x, kappa_y, sea_mask, members, vertical, diffusion_steps)
    sizes = tuple(lax.axis_size(axis) for axis in AXES)
    rows, cols = innovation.shape[2:]
    fits = rows == ROWS and members.shape[0] == ROWS and DEPTH <= cols <= LANES - DEPTH and ITERS == 2
    if sizes == (4, 2, 2) and fits:
        return shards_small(*arrays)
    return shards_any(*arrays)


def solution(mesh):
    placed = (
        P("grp", "gz", "gx", "gy"),
        P("grp", "gz", "gx", "gy"),
        P(None, "gz", "gx", "gy"),
        P("gz", "gx", "gy"),
        P("gz", "gx", "gy"),
        P("gz", "gx", "gy"),
        P("grp", None, "gz", "gx", "gy"),
        P(),
        P(),
    )
    return jax.shard_map(
        shards,
        mesh=mesh,
        in_specs=placed,
        out_specs=(P("grp", "gz", "gx", "gy"), P("grp"), P("grp", "gz", "gx", "gy")),
        check_vma=False,
    )
```

```python
import functools
import math


import jax
import jax.numpy as jnp
from jax import lax
from jax.experimental import pallas as pl
from jax.experimental.pallas import tpu as pltpu
from jax.sharding import PartitionSpec as P

KMAX = 10
ITERS = 2


static_share = 0.6
ensemble_share = 0.4


def extended(cells, sides, width):
    for axis, dim in sides:
        count = lax.axis_size(axis)
        head = lax.slice_in_dim(cells, 0, width, axis=dim)
        tail = lax.slice_in_dim(cells, cells.shape[dim] - width, cells.shape[dim], axis=dim)
        cells = jnp.concatenate(
            [
                lax.ppermute(tail, axis, [(i, (i + 1) % count) for i in range(count)]),
                cells,
                lax.ppermute(head, axis, [((i + 1) % count, i) for i in range(count)]),
            ],
            axis=dim,
        )
    return cells


def level_mix(source, mixing):
    local_levels = source.shape[1]
    gathered = lax.all_gather(source, "gz", axis=1, tiled=True)
    own_rows = lax.dynamic_slice_in_dim(
        mixing, lax.axis_index("gz") * local_levels, local_levels, 1
    )
    return jnp.einsum("flk,fkxy->flxy", own_rows, gathered, precision=lax.Precision.HIGHEST)


def diffuse(source, padded, step_counts, halo_depth):
    current = source
    for segment in range(KMAX // halo_depth):
        current = extended(current, (("gx", 2), ("gy", 3)), halo_depth)
        for substep in range(halo_depth):
            number = segment * halo_depth + substep
            offset = KMAX - halo_depth + substep
            rows_now = current.shape[2]
            cols_now = current.shape[3]
            window = padded[:, :, offset : offset + rows_now, offset : offset + cols_now]
            east_kappa = window[0]
            north_kappa = window[1]
            wet_window = window[2]
            east_coef = east_kappa[:, :-1, :] * wet_window[:, :-1, :] * wet_window[:, 1:, :]
            flux_east = east_coef * (current[:, :, 1:, :] - current[:, :, :-1, :])
            div_east = (flux_east[:, :, 1:, :] - flux_east[:, :, :-1, :])[:, :, :, 1:-1]
            north_coef = north_kappa[:, :, :-1] * wet_window[:, :, :-1] * wet_window[:, :, 1:]
            flux_north = north_coef * (current[:, :, :, 1:] - current[:, :, :, :-1])
            div_north = (flux_north[:, :, :, 1:] - flux_north[:, :, :, :-1])[:, :, 1:-1, :]
            active = (step_counts > number).astype(jnp.float32)[:, None, None, None]
            current = current[:, :, 1:-1, 1:-1] + active * (div_east + div_north)
    return current


def both_sums(terms, partial_value):
    return lax.psum((terms, partial_value), ("gx", "gy", "gz"))


def squares(resid_field):
    return lax.psum(jnp.sum(resid_field * resid_field), ("gx", "gy", "gz"))


def shards_any(
    innovation,
    obs_precision,
    error_scale,
    kappa_x,
    kappa_y,
    sea_mask,
    members,
    vertical,
    diffusion_steps,
):
    wet_cells = sea_mask.astype(jnp.float32)
    coefficients = jnp.stack([kappa_x, kappa_y, wet_cells])
    padded = extended(coefficients, (("gx", 2), ("gy", 3)), KMAX)
    cols_dev = wet_cells.shape[2]
    y_position = (
        lax.axis_index("gy") * cols_dev + jnp.arange(cols_dev + 2 * KMAX, dtype=jnp.int32) - KMAX
    )
    inside = ((y_position >= 0) & (y_position < cols_dev * lax.axis_size("gy"))).astype(jnp.float32)
    padded = jnp.stack([padded[0], padded[1], padded[2] * inside[None, None, :]])
    halo_depth = 2
    transposed = jnp.swapaxes(vertical, 1, 2)
    sqrt_static = math.sqrt(static_share)
    ens_scale = math.sqrt(ensemble_share / (members.shape[0] - 1))

    def static_back(masked):
        return sqrt_static * diffuse(
            level_mix(error_scale * masked, transposed), padded, diffusion_steps, halo_depth
        )

    def ensemble_terms(masked):
        return jnp.einsum("mflxy,flxy->m", members, masked, precision=lax.Precision.HIGHEST)

    masked = wet_cells * (obs_precision * innovation)
    resid_field = static_back(masked)
    ens_sum, field_norm = both_sums(ensemble_terms(masked), jnp.sum(resid_field * resid_field))
    resid_weights = ens_scale * ens_sum
    norm_now = field_norm + jnp.sum(resid_weights * resid_weights)
    dir_field, dir_weights = (resid_field, resid_weights)
    control_field = jnp.zeros_like(resid_field)
    control_weights = jnp.zeros(resid_weights.shape, jnp.float32)
    for iteration in range(ITERS):
        static = error_scale * level_mix(
            diffuse(dir_field, padded, diffusion_steps, halo_depth), vertical
        )
        ensemble = jnp.einsum(
            "m,mflxy->flxy", dir_weights, members, precision=lax.Precision.HIGHEST
        )
        observed = wet_cells * (sqrt_static * static + ens_scale * ensemble)
        weighted = obs_precision * observed
        masked = wet_cells * weighted
        image_field = dir_field + static_back(masked)
        ens_sum, curve_part = both_sums(ensemble_terms(masked), jnp.sum(dir_field * image_field))
        image_weights = dir_weights + ens_scale * ens_sum
        curvature = curve_part + jnp.sum(dir_weights * image_weights)
        step_length = norm_now / curvature
        control_field = control_field + step_length * dir_field
        control_weights = control_weights + step_length * dir_weights
        resid_field = resid_field - step_length * image_field
        resid_weights = resid_weights - step_length * image_weights
        if iteration + 1 < ITERS:
            norm_next = squares(resid_field) + jnp.sum(resid_weights * resid_weights)
            ratio_next = norm_next / norm_now
            dir_field = resid_field + ratio_next * dir_field
            dir_weights = resid_weights + ratio_next * dir_weights
            norm_now = norm_next
    return (control_field, control_weights, resid_field)

ROWS = 16
WIN = 56
LANES = 128
DEPTH = 2 * KMAX
GROUP = LANES // DEPTH
SUMS = 8
AXES = ("gx", "gy", "gz")
VMEM = pl.BlockSpec(memory_space=pltpu.VMEM)
HBM = pl.BlockSpec(memory_space=pltpu.HBM)
SQRT_STATIC = math.sqrt(static_share)


def f32(*shape):
    return jax.ShapeDtypeStruct(shape, jnp.float32)


def call(kernel, outs, specs, args, scratch=(), grant=32):
    return pl.pallas_call(
        kernel,
        out_shape=outs,
        in_specs=specs,
        out_specs=[VMEM] * len(outs),
        scratch_shapes=list(scratch),
        compiler_params=pltpu.CompilerParams(vmem_limit_bytes=grant * 1024 * 1024),
    )(*args)


def lanes_of(shape):
    return lax.broadcasted_iota(jnp.int32, shape, len(shape) - 1)


def tile(ref, index, size=ROWS):
    return ref[index * size : (index + 1) * size, :]


def pack_edges(out_ref, planes, cols):
    first = jnp.where(lax.axis_index("gy") == 0, cols - DEPTH, 0)
    lane = lanes_of((ROWS, LANES))
    for group in range(-(-len(planes) // GROUP)):
        packed = jnp.zeros((ROWS, LANES), jnp.float32)
        for slot, plane in enumerate(planes[group * GROUP : (group + 1) * GROUP]):
            moved = pltpu.roll(plane, lax.rem(DEPTH * slot - first + LANES, LANES), 1)
            packed = jnp.where((lane >= DEPTH * slot) & (lane < DEPTH * (slot + 1)), moved, packed)
        out_ref[group * ROWS : (group + 1) * ROWS, :] = packed


def with_edge(own, edge_ref, index, cols):
    group, slot = divmod(index, GROUP)
    moved = pltpu.roll(tile(edge_ref, group), (cols - DEPTH * slot) % LANES, 1)
    return jnp.where(lanes_of(own.shape) < cols, own, moved)


def over_rows(values):
    return jnp.sum(values, axis=0, keepdims=True)


def coefficient_planes(coef, sources, levels, cols):
    coef[...] = jnp.zeros(coef.shape, jnp.float32)
    for level in range(levels):
        for kind, source in enumerate(sources):
            at = (kind * levels + level) * ROWS
            coef[at : at + ROWS, :cols] = source[level].astype(jnp.float32)


def project(out_z, at, totals, scale):
    for m, total in enumerate(totals):
        out_z[at + m : at + m + 1, : total.shape[1]] = scale * over_rows(total)


def start(planes, levels, cols, count):
    ens_scale = math.sqrt(ensemble_share / (count - 1))
    base = planes * ROWS
    edge_rows = -(-(planes + 3 * levels) // GROUP) * ROWS

    def kernel(*refs):
        sources, (out_z, out_e, coef), copies, weighted, sems = refs[:7], refs[7:10], refs[10:17], refs[17], refs[18]
        moves = [pltpu.make_async_copy(a, b, sems.at[i]) for i, (a, b) in enumerate(zip(sources, copies, strict=True))]
        for move in moves:
            move.start()
        innov, prec, scale, mask, kx, ky, members = copies
        out_z[...] = jnp.zeros(out_z.shape, jnp.float32)
        for move in moves[:6]:
            move.wait()
        coefficient_planes(coef, (kx, ky, mask), levels, cols)
        for plane in range(planes):
            weighted[plane] = mask[plane % levels].astype(jnp.float32) * (prec[plane] * innov[plane])
            out_z[plane * ROWS : (plane + 1) * ROWS, :cols] = scale[plane] * weighted[plane]
        edges = [tile(out_z, plane) for plane in range(planes)]
        pack_edges(out_e, edges + [tile(coef, index) for index in range(3 * levels)], cols)
        moves[6].wait()
        totals = [jnp.zeros((ROWS, cols), jnp.float32) for _ in range(count)]
        for plane in range(planes):
            for m in range(count):
                totals[m] += members[m, plane] * weighted[plane]
        project(out_z, base, totals, ens_scale)
        out_e[edge_rows:, :] = out_z[base:, :]

    outs = [f32(base + ROWS, LANES), f32(edge_rows + ROWS, LANES), f32(3 * levels * ROWS, LANES)]
    field, flat = (planes, ROWS, cols), (levels, ROWS, cols)
    kept = [(field, jnp.float32)] * 3 + [(flat, jnp.int32)] + [(flat, jnp.float32)] * 2 + [((count,) + field, jnp.float32)]
    scratch = [pltpu.VMEM(*one) for one in kept] + [pltpu.VMEM(field, jnp.float32), pltpu.SemaphoreType.DMA((7,))]
    return kernel, outs, scratch


def observe(planes, levels, cols, count, with_weights):
    ens_scale = math.sqrt(ensemble_share / (count - 1))
    base = planes * ROWS
    edge_rows = -(-planes // GROUP) * ROWS
    sums_at = base + ROWS * with_weights

    def kernel(*refs):
        own, other, weights, sums, vert, prec, scale, mask, members = refs[:9]
        if with_weights:
            out_z, out_e, out_q = refs[9:]
        else:
            seen, out_z, out_e = refs[9:]
        out_z[...] = jnp.zeros(out_z.shape, jnp.float32)
        totals = [jnp.zeros((ROWS, cols), jnp.float32) for _ in range(count)]
        energy = jnp.zeros((ROWS, cols), jnp.float32)
        cross = jnp.zeros((ROWS, cols), jnp.float32)
        here = lax.axis_index("gz") * levels
        there = (1 - lax.axis_index("gz")) * levels
        for plane in range(planes):
            field, level = divmod(plane, levels)
            wet = mask[level].astype(jnp.float32)
            static = jnp.zeros((ROWS, cols), jnp.float32)
            for k in range(levels):
                row = (field * 2 * levels + here + level) * 2 * levels
                static += vert[pl.ds(row + here + k, 1), :cols] * tile(own, field * levels + k)[:, :cols]
                static += vert[pl.ds(row + there + k, 1), :cols] * tile(other, field * levels + k)[:, :cols]
            ensemble = jnp.zeros((ROWS, cols), jnp.float32)
            for m in range(count):
                ensemble += weights[m : m + 1, :cols] * members[m, plane]
            seen_now = wet * (SQRT_STATIC * (scale[plane] * static) + ens_scale * ensemble)
            weighted = wet * (prec[plane] * seen_now)
            energy += seen_now * weighted
            if with_weights:
                out_q[plane] = weighted
                for m in range(count):
                    totals[m] += members[m, plane] * weighted
            else:
                cross += seen_now * seen[plane]
            out_z[plane * ROWS : (plane + 1) * ROWS, :cols] = scale[plane] * weighted
        if with_weights:
            project(out_z, base, totals, ens_scale)
        out_z[sums_at : sums_at + SUMS, :] = sums[...]
        out_z[sums_at : sums_at + 1, :cols] = over_rows(energy)
        if not with_weights:
            out_z[sums_at + 1 : sums_at + 2, :cols] = over_rows(cross)
        pack_edges(out_e, [tile(out_z, plane) for plane in range(planes)], cols)
        out_e[edge_rows:, :] = out_z[base:, :]

    tail = (ROWS * with_weights) + SUMS
    outs = [f32(base + tail, LANES), f32(edge_rows + tail, LANES)]
    if with_weights:
        outs.append(f32(planes, ROWS, cols))
    return kernel, outs


def mix_back(first, planes, levels, cols, tail):
    base = planes * ROWS
    coefs = 3 * levels if first else 0
    fields = planes // levels

    def kernel(*refs):
        if first:
            own, other, edge, edge_other, vert, coef, out_all, out_near = refs
        else:
            own, other, edge, edge_other, vert, out_all, out_near = refs
        here = lax.axis_index("gz") * levels
        there = (1 - lax.axis_index("gz")) * levels
        upper = lax.broadcasted_iota(jnp.int32, (8, LANES), 0) < 4

        def put(index, values):
            out_all[index * ROWS : (index + 1) * ROWS, :] = values
            out_near[index * 8 : (index + 1) * 8, :] = jnp.where(upper, values[:8], values[8:])

        for field in range(fields):
            mine = [with_edge(tile(own, field * levels + l), edge, field * levels + l, cols) for l in range(levels)]
            theirs = [
                with_edge(tile(other, field * levels + l), edge_other, field * levels + l, cols) for l in range(levels)
            ]
            for k in range(levels):
                mixed = jnp.zeros((ROWS, LANES), jnp.float32)
                for l in range(levels):
                    block = field * 2 * levels
                    mixed += vert[pl.ds((block + here + l) * 2 * levels + here + k, 1), :] * mine[l]
                    mixed += vert[pl.ds((block + there + l) * 2 * levels + here + k, 1), :] * theirs[l]
                put(field * levels + k, mixed)
        for index in range(coefs):
            put(planes + index, with_edge(tile(coef, index), edge, planes + index, cols))
        packed = -(-(planes + coefs) // GROUP) * ROWS
        total = (own[base:, :] + other[base:, :]) + (edge[packed:, :] + edge_other[packed:, :])
        out_all[(planes + coefs) * ROWS :, :] = total
        out_near[(planes + coefs) * 8 :, :] = total

    count = planes + coefs
    return kernel, [f32(count * ROWS + tail, LANES), f32(count * 8 + tail, LANES)]


def window(target, index, own, first, near, third, slot):
    even = lax.rem(lax.axis_index("gx"), 2) == 0
    one, three = tile(first, slot), tile(third, slot)
    target[index, 0:16, :] = tile(own, slot)
    target[index, 16:32, :] = jnp.where(even, one, three)
    target[index, 32:40, :] = tile(near, slot, 8)
    target[index, 40:56, :] = jnp.where(even, three, one)


def run_steps(start, other, coef, steps, planes, levels):
    def one(number, source, target):
        number = number.astype(jnp.float32)
        for level in range(levels):
            for field in range(planes // levels):
                plane = field * levels + level
                u = source[plane]
                rows = u.shape[0]
                change = (
                    coef[0, level] * pltpu.roll(u, rows - 1, 0)
                    + coef[1, level] * pltpu.roll(u, 1, 0)
                    + coef[2, level] * pltpu.roll(u, LANES - 1, 1)
                    + coef[3, level] * pltpu.roll(u, 1, 1)
                    - coef[4, level] * u
                )
                active = jnp.where(steps[field : field + 1, :] > number, 1.0, 0.0).astype(jnp.float32)
                target[plane] = u + active * change

    def pair(index, carry):
        one(2 * index, start, other)
        one(2 * index + 1, other, start)
        return carry

    lax.fori_loop(0, KMAX // 2, pair, 0)


def make_coefs(coef, kinds, levels, cols):
    lane = lanes_of((WIN, LANES))
    last = jnp.where(lax.axis_index("gy") == 0, LANES - 1, cols - 1)
    for level in range(levels):
        kx, ky, wet = (kinds[kind * levels + level] for kind in range(3))
        east = kx * wet * pltpu.roll(wet, WIN - 1, 0)
        north = ky * wet * pltpu.roll(wet, LANES - 1, 1)
        north = jnp.where(lane == last, 0.0, north)
        west = pltpu.roll(east, 1, 0)
        south = pltpu.roll(north, 1, 1)
        for index, values in enumerate((east, west, north, south, (east + west) + (north + south))):
            coef[index, level] = values


def own_sum(values, cols):
    own = values[:ROWS]
    return over_rows(jnp.where(lanes_of(own.shape) < cols, own, 0.0))


def spread(values):
    return jnp.broadcast_to(jnp.sum(values, axis=1, keepdims=True), values.shape)


def first_diffuse(planes, levels, cols):
    coefs = 3 * levels

    def kernel(own, first, near, third, steps, coef, resid, weights, sums, out_g, buf, kinds):
        for plane in range(planes):
            window(buf, plane, own, first, near, third, plane)
        for index in range(coefs):
            window(kinds, index, own, first, near, third, planes + index)
        make_coefs(coef, kinds, levels, cols)
        at, near_at = (planes + coefs) * ROWS, (planes + coefs) * 8
        weights[...] = spread((own[at:, :] + first[at:, :]) + (near[near_at:, :] + third[at:, :]))
        run_steps(buf, resid, coef, steps, planes, levels)
        squares = jnp.zeros((ROWS, LANES), jnp.float32)
        for plane in range(planes):
            value = SQRT_STATIC * buf[plane]
            resid[plane] = value
            buf[plane] = value
            squares += value[:ROWS] * value[:ROWS]
        sums[...] = jnp.zeros(sums.shape, jnp.float32)
        sums[2:3, :] = own_sum(squares, cols)
        run_steps(buf, kinds, coef, steps, planes, levels)
        for plane in range(planes):
            out_g[plane * ROWS : (plane + 1) * ROWS, :] = buf[plane, :ROWS, :]

    outs = [
        f32(5, levels, WIN, LANES),
        f32(planes, WIN, LANES),
        f32(ROWS, LANES),
        f32(SUMS, LANES),
        f32(planes * ROWS, LANES),
    ]
    scratch = [pltpu.VMEM((planes, WIN, LANES), jnp.float32)] * 2
    return kernel, outs, scratch


def second_diffuse(planes, levels, cols):
    def kernel(own, first, near, third, steps, coef, resid, weights, image, new, new_w, sums, facts, out_g, buf, spare):
        for plane in range(planes):
            window(buf, plane, own, first, near, third, plane)
        at, near_at = planes * ROWS, planes * 8
        total = spread((own[at:, :] + first[at:, :]) + (near[near_at:, :] + third[at:, :]))
        energy = total[ROWS : ROWS + 1]
        rr = total[ROWS + 2 : ROWS + 3] + over_rows(weights[...] * weights[...])
        curvature = rr + energy
        step = rr / curvature
        new_weights = weights[...] - step * (weights[...] + total[:ROWS])
        new_w[...] = new_weights
        facts[...] = jnp.zeros(facts.shape, jnp.float32)
        facts[0:1, :] = rr
        facts[1:2, :] = energy
        facts[2:3, :] = step
        run_steps(buf, spare, coef, steps, planes, levels)
        squares = jnp.zeros((ROWS, LANES), jnp.float32)
        cross = jnp.zeros((ROWS, LANES), jnp.float32)
        for plane in range(planes):
            direction = resid[plane]
            image_now = direction + SQRT_STATIC * buf[plane]
            value = direction - step * image_now
            image[plane * ROWS : (plane + 1) * ROWS, :] = image_now[:ROWS]
            new[plane * ROWS : (plane + 1) * ROWS, :] = value[:ROWS]
            buf[plane] = value
            squares += value[:ROWS] * value[:ROWS]
            cross += value[:ROWS] * direction[:ROWS]
        sums[...] = jnp.zeros(sums.shape, jnp.float32)
        sums[2:3, :] = own_sum(squares, cols)
        sums[3:4, :] = own_sum(cross, cols)
        run_steps(buf, spare, coef, steps, planes, levels)
        for plane in range(planes):
            out_g[plane * ROWS : (plane + 1) * ROWS, :] = buf[plane, :ROWS, :]

    block = f32(planes * ROWS, LANES)
    outs = [block, block, f32(ROWS, LANES), f32(SUMS, LANES), f32(SUMS, LANES), block]
    scratch = [pltpu.VMEM((planes, WIN, LANES), jnp.float32)] * 2
    return kernel, outs, scratch


def last_diffuse(planes, levels, cols):
    def kernel(
        own, first, near, third, steps, coef, resid, weights, image, new, new_w, facts, control, control_w, final, buf, spare
    ):
        for plane in range(planes):
            window(buf, plane, own, first, near, third, plane)
        at, near_at = planes * ROWS, planes * 8
        total = spread((own[at:, :] + first[at:, :]) + (near[near_at:, :] + third[at:, :]))
        rr, energy, step = facts[0:1, :], facts[1:2, :], facts[2:3, :]
        new_energy, cross_energy = total[0:1], total[1:2]
        new_rr = total[2:3] + over_rows(new_w[...] * new_w[...])
        cross_rr = total[3:4] + over_rows(new_w[...] * weights[...])
        ratio = new_rr / rr
        squares = new_rr + ratio * (2.0 * cross_rr + ratio * rr)
        curvature = squares + (new_energy + ratio * (2.0 * cross_energy + ratio * energy))
        new_step = new_rr / curvature
        combined = step * weights[...] + new_step * (new_w[...] + ratio * weights[...])
        diagonal = lax.broadcasted_iota(jnp.int32, combined.shape, 0) == lanes_of(combined.shape)
        control_w[...] = over_rows(jnp.where(diagonal, combined, 0.0))[:, :ROWS]
        run_steps(buf, spare, coef, steps, planes, levels)
        for plane in range(planes):
            value = tile(new, plane)
            direction = resid[plane, :ROWS, :]
            new_direction = value + ratio * direction
            new_image = (value + SQRT_STATIC * buf[plane, :ROWS, :]) + ratio * tile(image, plane)
            control[plane] = (step * direction + new_step * new_direction)[:, :cols]
            final[plane] = (value - new_step * new_image)[:, :cols]

    outs = [f32(planes, ROWS, cols), f32(1, ROWS), f32(planes, ROWS, cols)]
    scratch = [pltpu.VMEM((planes, WIN, LANES), jnp.float32)] * 2
    return kernel, outs, scratch


def moved_to(values, x, y, z):
    sizes = [lax.axis_size(axis) for axis in AXES]
    here = [(a, b, c) for a in range(sizes[0]) for b in range(sizes[1]) for c in range(sizes[2])]
    number = {place: index for index, place in enumerate(here)}
    return lax.ppermute(values, AXES, [(number[a, b, c], number[a ^ x, b ^ y, c ^ z]) for a, b, c in here])


def across(kernel_of, out_z, out_e, vert, extra):
    other = moved_to(out_z, 0, 0, 1)
    edge = moved_to(out_e, 0, 1, 0)
    edge_other = moved_to(out_e, 0, 1, 1)
    kernel, outs = kernel_of
    own, near = call(kernel, outs, [VMEM] * (5 + len(extra)), (out_z, other, edge, edge_other, vert, *extra))
    return own, moved_to(own, 1, 0, 0), moved_to(near, 2, 0, 0), moved_to(own, 3, 0, 0)


def shards_small(
    innovation, obs_precision, error_scale, kappa_x, kappa_y, sea_mask, members, vertical, diffusion_steps
):
    fields, levels, rows, cols = innovation.shape
    count = members.shape[0]
    planes = fields * levels
    block = (planes, rows, cols)
    innov, prec, scale = (a.reshape(block) for a in (innovation, obs_precision, error_scale))
    ens = members.reshape((count,) + block)
    vert = jnp.broadcast_to(vertical.reshape(-1, 1), (vertical.size, LANES))
    steps = jnp.broadcast_to(diffusion_steps.astype(jnp.float32)[:, None], (fields, LANES))

    kernel, outs, scratch = start(planes, levels, cols, count)
    args = (innov, prec, scale, sea_mask, kappa_x, kappa_y, ens)
    out_z, out_e, coef_own = call(kernel, outs, [HBM] * 7, args, scratch, 56)
    parts = across(mix_back(True, planes, levels, cols, ROWS), out_z, out_e, vert, (coef_own,))
    kernel, outs, scratch = first_diffuse(planes, levels, cols)
    coef, resid, weights, sums, out_g = call(kernel, outs, [VMEM] * 5, (*parts, steps), scratch)

    kernel, outs = observe(planes, levels, cols, count, True)
    args = (out_g, moved_to(out_g, 0, 0, 1), weights, sums, vert, prec, scale, sea_mask, ens)
    out_z, out_e, seen = call(kernel, outs, [VMEM] * 9, args)
    parts = across(mix_back(False, planes, levels, cols, ROWS + SUMS), out_z, out_e, vert, ())
    kernel, outs, scratch = second_diffuse(planes, levels, cols)
    args = (*parts, steps, coef, resid, weights)
    image, new, new_w, sums, facts, out_g = call(kernel, outs, [VMEM] * 8, args, scratch)

    kernel, outs = observe(planes, levels, cols, count, False)
    args = (out_g, moved_to(out_g, 0, 0, 1), new_w, sums, vert, prec, scale, sea_mask, ens, seen)
    out_z, out_e = call(kernel, outs, [VMEM] * 10, args)
    parts = across(mix_back(False, planes, levels, cols, SUMS), out_z, out_e, vert, ())
    kernel, outs, scratch = last_diffuse(planes, levels, cols)
    args = (*parts, steps, coef, resid, weights, image, new, new_w, facts)
    control, control_w, final = call(kernel, outs, [VMEM] * 12, args, scratch)
    return control.reshape(innovation.shape), control_w.reshape(count), final.reshape(innovation.shape)


def shards(innovation, obs_precision, error_scale, kappa_x, kappa_y, sea_mask, members, vertical, diffusion_steps):
    arrays = (innovation, obs_precision, error_scale, kappa_x, kappa_y, sea_mask, members, vertical, diffusion_steps)
    sizes = tuple(lax.axis_size(axis) for axis in AXES)
    rows, cols = innovation.shape[2:]
    fits = rows == ROWS and members.shape[0] == ROWS and DEPTH <= cols <= LANES - DEPTH and ITERS == 2
    if sizes == (4, 2, 2) and fits:
        return shards_small(*arrays)
    return shards_any(*arrays)


def solution(mesh):
    placed = (
        P("grp", "gz", "gx", "gy"),
        P("grp", "gz", "gx", "gy"),
        P(None, "gz", "gx", "gy"),
        P("gz", "gx", "gy"),
        P("gz", "gx", "gy"),
        P("gz", "gx", "gy"),
        P("grp", None, "gz", "gx", "gy"),
        P(),
        P(),
    )
    return jax.shard_map(
        shards,
        mesh=mesh,
        in_specs=placed,
        out_specs=(P("grp", "gz", "gx", "gy"), P("grp"), P("grp", "gz", "gx", "gy")),
        check_vma=False,
    )
```

```python
import functools
import math


import jax
import jax.numpy as jnp
from jax import lax
from jax.experimental import pallas as pl
from jax.experimental.pallas import tpu as pltpu
from jax.sharding import PartitionSpec as P

KMAX = 10
ITERS = 2


static_share = 0.6
ensemble_share = 0.4


def extended(cells, sides, width):
    for axis, dim in sides:
        count = lax.axis_size(axis)
        head = lax.slice_in_dim(cells, 0, width, axis=dim)
        tail = lax.slice_in_dim(cells, cells.shape[dim] - width, cells.shape[dim], axis=dim)
        cells = jnp.concatenate(
            [
                lax.ppermute(tail, axis, [(i, (i + 1) % count) for i in range(count)]),
                cells,
                lax.ppermute(head, axis, [((i + 1) % count, i) for i in range(count)]),
            ],
            axis=dim,
        )
    return cells


def level_mix(source, mixing):
    local_levels = source.shape[1]
    gathered = lax.all_gather(source, "gz", axis=1, tiled=True)
    own_rows = lax.dynamic_slice_in_dim(
        mixing, lax.axis_index("gz") * local_levels, local_levels, 1
    )
    return jnp.einsum("flk,fkxy->flxy", own_rows, gathered, precision=lax.Precision.HIGHEST)


def diffuse(source, padded, step_counts, halo_depth):
    current = source
    for segment in range(KMAX // halo_depth):
        current = extended(current, (("gx", 2), ("gy", 3)), halo_depth)
        for substep in range(halo_depth):
            number = segment * halo_depth + substep
            offset = KMAX - halo_depth + substep
            rows_now = current.shape[2]
            cols_now = current.shape[3]
            window = padded[:, :, offset : offset + rows_now, offset : offset + cols_now]
            east_kappa = window[0]
            north_kappa = window[1]
            wet_window = window[2]
            east_coef = east_kappa[:, :-1, :] * wet_window[:, :-1, :] * wet_window[:, 1:, :]
            flux_east = east_coef * (current[:, :, 1:, :] - current[:, :, :-1, :])
            div_east = (flux_east[:, :, 1:, :] - flux_east[:, :, :-1, :])[:, :, :, 1:-1]
            north_coef = north_kappa[:, :, :-1] * wet_window[:, :, :-1] * wet_window[:, :, 1:]
            flux_north = north_coef * (current[:, :, :, 1:] - current[:, :, :, :-1])
            div_north = (flux_north[:, :, :, 1:] - flux_north[:, :, :, :-1])[:, :, 1:-1, :]
            active = (step_counts > number).astype(jnp.float32)[:, None, None, None]
            current = current[:, :, 1:-1, 1:-1] + active * (div_east + div_north)
    return current


def both_sums(terms, partial_value):
    return lax.psum((terms, partial_value), ("gx", "gy", "gz"))


def squares(resid_field):
    return lax.psum(jnp.sum(resid_field * resid_field), ("gx", "gy", "gz"))


def shards_any(
    innovation,
    obs_precision,
    error_scale,
    kappa_x,
    kappa_y,
    sea_mask,
    members,
    vertical,
    diffusion_steps,
):
    wet_cells = sea_mask.astype(jnp.float32)
    coefficients = jnp.stack([kappa_x, kappa_y, wet_cells])
    padded = extended(coefficients, (("gx", 2), ("gy", 3)), KMAX)
    cols_dev = wet_cells.shape[2]
    y_position = (
        lax.axis_index("gy") * cols_dev + jnp.arange(cols_dev + 2 * KMAX, dtype=jnp.int32) - KMAX
    )
    inside = ((y_position >= 0) & (y_position < cols_dev * lax.axis_size("gy"))).astype(jnp.float32)
    padded = jnp.stack([padded[0], padded[1], padded[2] * inside[None, None, :]])
    halo_depth = 2
    transposed = jnp.swapaxes(vertical, 1, 2)
    sqrt_static = math.sqrt(static_share)
    ens_scale = math.sqrt(ensemble_share / (members.shape[0] - 1))

    def static_back(masked):
        return sqrt_static * diffuse(
            level_mix(error_scale * masked, transposed), padded, diffusion_steps, halo_depth
        )

    def ensemble_terms(masked):
        return jnp.einsum("mflxy,flxy->m", members, masked, precision=lax.Precision.HIGHEST)

    masked = wet_cells * (obs_precision * innovation)
    resid_field = static_back(masked)
    ens_sum, field_norm = both_sums(ensemble_terms(masked), jnp.sum(resid_field * resid_field))
    resid_weights = ens_scale * ens_sum
    norm_now = field_norm + jnp.sum(resid_weights * resid_weights)
    dir_field, dir_weights = (resid_field, resid_weights)
    control_field = jnp.zeros_like(resid_field)
    control_weights = jnp.zeros(resid_weights.shape, jnp.float32)
    for iteration in range(ITERS):
        static = error_scale * level_mix(
            diffuse(dir_field, padded, diffusion_steps, halo_depth), vertical
        )
        ensemble = jnp.einsum(
            "m,mflxy->flxy", dir_weights, members, precision=lax.Precision.HIGHEST
        )
        observed = wet_cells * (sqrt_static * static + ens_scale * ensemble)
        weighted = obs_precision * observed
        masked = wet_cells * weighted
        image_field = dir_field + static_back(masked)
        ens_sum, curve_part = both_sums(ensemble_terms(masked), jnp.sum(dir_field * image_field))
        image_weights = dir_weights + ens_scale * ens_sum
        curvature = curve_part + jnp.sum(dir_weights * image_weights)
        step_length = norm_now / curvature
        control_field = control_field + step_length * dir_field
        control_weights = control_weights + step_length * dir_weights
        resid_field = resid_field - step_length * image_field
        resid_weights = resid_weights - step_length * image_weights
        if iteration + 1 < ITERS:
            norm_next = squares(resid_field) + jnp.sum(resid_weights * resid_weights)
            ratio_next = norm_next / norm_now
            dir_field = resid_field + ratio_next * dir_field
            dir_weights = resid_weights + ratio_next * dir_weights
            norm_now = norm_next
    return (control_field, control_weights, resid_field)

ROWS = 16
WIN = 56
TILES = WIN // 8
LANES = 128
DEPTH = 2 * KMAX
GROUP = LANES // DEPTH
SUMS = 8
AXES = ("gx", "gy", "gz")
VMEM = pl.BlockSpec(memory_space=pltpu.VMEM)
HBM = pl.BlockSpec(memory_space=pltpu.HBM)
SQRT_STATIC = math.sqrt(static_share)


def f32(*shape):
    return jax.ShapeDtypeStruct(shape, jnp.float32)


def call(kernel, outs, specs, args, scratch=(), grant=32):
    return pl.pallas_call(
        kernel,
        out_shape=outs,
        in_specs=specs,
        out_specs=[VMEM] * len(outs),
        scratch_shapes=list(scratch),
        compiler_params=pltpu.CompilerParams(vmem_limit_bytes=grant * 1024 * 1024),
    )(*args)


def lanes_of(shape):
    return lax.broadcasted_iota(jnp.int32, shape, len(shape) - 1)


def tile(ref, index, size=ROWS):
    return ref[index * size : (index + 1) * size, :]


def pack_edges(out_ref, planes, cols):
    first = jnp.where(lax.axis_index("gy") == 0, cols - DEPTH, 0)
    lane = lanes_of((ROWS, LANES))
    for group in range(-(-len(planes) // GROUP)):
        packed = jnp.zeros((ROWS, LANES), jnp.float32)
        for slot, plane in enumerate(planes[group * GROUP : (group + 1) * GROUP]):
            moved = pltpu.roll(plane, lax.rem(DEPTH * slot - first + LANES, LANES), 1)
            packed = jnp.where((lane >= DEPTH * slot) & (lane < DEPTH * (slot + 1)), moved, packed)
        out_ref[group * ROWS : (group + 1) * ROWS, :] = packed


def with_edge(own, edge_ref, index, cols):
    group, slot = divmod(index, GROUP)
    moved = pltpu.roll(tile(edge_ref, group), (cols - DEPTH * slot) % LANES, 1)
    return jnp.where(lanes_of(own.shape) < cols, own, moved)


def over_rows(values):
    return jnp.sum(values, axis=0, keepdims=True)


def whole(values):
    return jnp.sum(over_rows(values), axis=1, keepdims=True)


def coefficient_planes(coef, sources, levels, cols):
    coef[...] = jnp.zeros(coef.shape, jnp.float32)
    for level in range(levels):
        for kind, source in enumerate(sources):
            at = (kind * levels + level) * ROWS
            coef[at : at + ROWS, :cols] = source[level].astype(jnp.float32)


def project(out_z, at, totals, scale):
    for m, total in enumerate(totals):
        out_z[at + m : at + m + 1, : total.shape[1]] = scale * over_rows(total)


def start(planes, levels, cols, count):
    ens_scale = math.sqrt(ensemble_share / (count - 1))
    base = planes * ROWS
    edge_rows = -(-(planes + 3 * levels) // GROUP) * ROWS

    def kernel(*refs):
        sources, (out_z, out_e, coef), copies, weighted, sems = refs[:7], refs[7:10], refs[10:17], refs[17], refs[18]
        moves = [pltpu.make_async_copy(a, b, sems.at[i]) for i, (a, b) in enumerate(zip(sources, copies, strict=True))]
        for move in moves:
            move.start()
        innov, prec, scale, mask, kx, ky, members = copies
        out_z[...] = jnp.zeros(out_z.shape, jnp.float32)
        for move in moves[:6]:
            move.wait()
        coefficient_planes(coef, (kx, ky, mask), levels, cols)
        for plane in range(planes):
            weighted[plane] = mask[plane % levels].astype(jnp.float32) * (prec[plane] * innov[plane])
            out_z[plane * ROWS : (plane + 1) * ROWS, :cols] = scale[plane] * weighted[plane]
        edges = [tile(out_z, plane) for plane in range(planes)]
        pack_edges(out_e, edges + [tile(coef, index) for index in range(3 * levels)], cols)
        moves[6].wait()
        totals = [jnp.zeros((ROWS, cols), jnp.float32) for _ in range(count)]
        for plane in range(planes):
            for m in range(count):
                totals[m] += members[m, plane] * weighted[plane]
        project(out_z, base, totals, ens_scale)
        out_e[edge_rows:, :] = out_z[base:, :]

    outs = [f32(base + ROWS, LANES), f32(edge_rows + ROWS, LANES), f32(3 * levels * ROWS, LANES)]
    field, flat = (planes, ROWS, cols), (levels, ROWS, cols)
    kept = [(field, jnp.float32)] * 3 + [(flat, jnp.int32)] + [(flat, jnp.float32)] * 2 + [((count,) + field, jnp.float32)]
    scratch = [pltpu.VMEM(*one) for one in kept] + [pltpu.VMEM(field, jnp.float32), pltpu.SemaphoreType.DMA((7,))]
    return kernel, outs, scratch


def observe(planes, levels, cols, count, with_weights):
    ens_scale = math.sqrt(ensemble_share / (count - 1))
    base = planes * ROWS
    edge_rows = -(-planes // GROUP) * ROWS
    sums_at = base + ROWS * with_weights

    def kernel(*refs):
        own, other, weights, sums, vert, prec, scale, mask, members = refs[:9]
        if with_weights:
            out_z, out_e, seen = refs[9:]
        else:
            seen, out_z, out_e, now = refs[9:]
        out_z[...] = jnp.zeros(out_z.shape, jnp.float32)
        totals = [jnp.zeros((ROWS, cols), jnp.float32) for _ in range(count)]
        energy = jnp.zeros((ROWS, cols), jnp.float32)
        cross = jnp.zeros((ROWS, cols), jnp.float32)
        here = lax.axis_index("gz") * levels
        there = (1 - lax.axis_index("gz")) * levels
        for plane in range(planes):
            field, level = divmod(plane, levels)
            wet = mask[level].astype(jnp.float32)
            static = jnp.zeros((ROWS, cols), jnp.float32)
            for k in range(levels):
                row = (field * 2 * levels + here + level) * 2 * levels
                static += vert[pl.ds(row + here + k, 1), :cols] * tile(own, field * levels + k)[:, :cols]
                static += vert[pl.ds(row + there + k, 1), :cols] * tile(other, field * levels + k)[:, :cols]
            ensemble = jnp.zeros((ROWS, cols), jnp.float32)
            for m in range(count):
                ensemble += weights[m : m + 1, :cols] * members[m, plane]
            seen_now = wet * (SQRT_STATIC * (scale[plane] * static) + ens_scale * ensemble)
            weighted = wet * (prec[plane] * seen_now)
            if with_weights:
                seen[plane] = seen_now
                energy += seen_now * weighted
                for m in range(count):
                    totals[m] += members[m, plane] * weighted
            else:
                now[plane] = seen_now
                before = seen[plane]
                energy += before * (prec[plane] * before)
                cross += before * weighted
            out_z[plane * ROWS : (plane + 1) * ROWS, :cols] = scale[plane] * weighted
        if with_weights:
            project(out_z, base, totals, ens_scale)
        out_z[sums_at : sums_at + SUMS, :] = sums[...]
        if with_weights:
            out_z[sums_at : sums_at + 1, :cols] = over_rows(energy)
        else:
            energy, cross = whole(energy), whole(cross)
            share = jnp.where(energy > 0.0, -cross / jnp.where(energy > 0.0, energy, 1.0), 0.0)
            rest = jnp.zeros((ROWS, cols), jnp.float32)
            left = jnp.zeros((ROWS, cols), jnp.float32)
            for plane in range(planes):
                before = seen[plane]
                gap = now[plane] + share * before
                rest += gap * (prec[plane] * gap)
                left += before * (prec[plane] * gap)
            place = (lax.axis_index("gx") * 2 + lax.axis_index("gy")) * 2 + lax.axis_index("gz")
            own_lane = lanes_of((1, LANES)) == place
            for index, value in enumerate((whole(rest), whole(left), share, energy)):
                out_z[sums_at + index : sums_at + index + 1, :] = jnp.where(own_lane, value, 0.0)
        pack_edges(out_e, [tile(out_z, plane) for plane in range(planes)], cols)
        out_e[edge_rows:, :] = out_z[base:, :]

    tail = (ROWS * with_weights) + SUMS
    outs = [f32(base + tail, LANES), f32(edge_rows + tail, LANES)]
    if with_weights:
        return kernel, outs + [f32(planes, ROWS, cols)], ()
    return kernel, outs, [pltpu.VMEM((planes, ROWS, cols), jnp.float32)]


def mix_back(first, far, planes, levels, cols, tail):
    base = planes * ROWS
    coefs = 3 * levels if first else 0
    fields = planes // levels

    def kernel(*refs):
        if first:
            own, other, edge, edge_other, vert, coef, out_all, out_near = refs
        else:
            own, other, edge, edge_other, vert, out_all, out_near = refs
        here = lax.axis_index("gz") * levels
        there = (1 - lax.axis_index("gz")) * levels
        upper = lax.broadcasted_iota(jnp.int32, (8, LANES), 0) < 4

        def put(index, values):
            out_all[index * ROWS : (index + 1) * ROWS, :] = values
            if far:
                out_near[index * 8 : (index + 1) * 8, :] = jnp.where(upper, values[:8], values[8:])

        for field in range(fields):
            mine = [with_edge(tile(own, field * levels + l), edge, field * levels + l, cols) for l in range(levels)]
            theirs = [
                with_edge(tile(other, field * levels + l), edge_other, field * levels + l, cols) for l in range(levels)
            ]
            for k in range(levels):
                mixed = jnp.zeros((ROWS, LANES), jnp.float32)
                for l in range(levels):
                    block = field * 2 * levels
                    mixed += vert[pl.ds((block + here + l) * 2 * levels + here + k, 1), :] * mine[l]
                    mixed += vert[pl.ds((block + there + l) * 2 * levels + here + k, 1), :] * theirs[l]
                put(field * levels + k, mixed)
        for index in range(coefs):
            put(planes + index, with_edge(tile(coef, index), edge, planes + index, cols))
        packed = -(-(planes + coefs) // GROUP) * ROWS
        total = (own[base:, :] + other[base:, :]) + (edge[packed:, :] + edge_other[packed:, :])
        out_all[(planes + coefs) * ROWS :, :] = total
        out_near[far * (planes + coefs) * 8 :, :] = total

    count = planes + coefs
    return kernel, [f32(count * ROWS + tail, LANES), f32(far * count * 8 + tail, LANES)]


def fetch_window(target, nat, index, own, first, near, third, slot):
    even = lax.rem(lax.axis_index("gx"), 2) == 0
    one, three = tile(first, slot), tile(third, slot)
    nat[index, 0:16, :] = tile(own, slot)
    nat[index, 16:32, :] = jnp.where(even, one, three)
    nat[index, 32:40, :] = jnp.zeros((8, LANES), jnp.float32) if near is None else tile(near, slot, 8)
    nat[index, 40:56, :] = jnp.where(even, three, one)
    for t in range(TILES):
        target[index, t * 8 : (t + 1) * 8, :] = nat[index, pl.ds(t, 8, stride=TILES), :]


def own_rows(values, nat, index):
    for t in range(TILES):
        nat[index, pl.ds(t, 8, stride=TILES), :] = values[t * 8 : (t + 1) * 8]
    return nat[index, 0:ROWS, :]


def eight(ref, *index):
    return [ref[(*index, pl.ds(t * 8, 8), slice(None))] for t in range(TILES)]


def after(tiles):
    return tiles[1:] + [pltpu.roll(tiles[0], 7, 0)]


def run_steps(buf, coef, steps, planes, levels):
    for number in range(KMAX):
        for level in range(levels):
            east, north = eight(coef, 0, level), eight(coef, 1, level)
            for field in range(planes // levels):
                plane = field * levels + level
                active = jnp.where(steps[field : field + 1, :] > float(number), 1.0, 0.0).astype(jnp.float32)
                u = eight(buf, plane)
                flux_east = [c * (v - w) for c, v, w in zip(east, after(u), u, strict=True)]
                flux_west = [pltpu.roll(flux_east[-1], 1, 0)] + flux_east[:-1]
                for t in range(TILES):
                    flux_north = north[t] * (pltpu.roll(u[t], LANES - 1, 1) - u[t])
                    change = (flux_east[t] - flux_west[t]) + (flux_north - pltpu.roll(flux_north, 1, 1))
                    buf[plane, t * 8 : (t + 1) * 8, :] = u[t] + active * change


def make_coefs(coef, kinds, levels, cols):
    last = jnp.where(lax.axis_index("gy") == 0, LANES - 1, cols - 1)
    inside = lanes_of((8, LANES)) != last
    for level in range(levels):
        kx, ky, wet = (eight(kinds, kind * levels + level) for kind in range(3))
        for t, beyond in enumerate(after(wet)):
            rows = slice(t * 8, (t + 1) * 8)
            coef[0, level, rows, :] = kx[t] * wet[t] * beyond
            coef[1, level, rows, :] = jnp.where(inside, ky[t] * wet[t] * pltpu.roll(wet[t], LANES - 1, 1), 0.0)


def own_cells(cols):
    row = lax.broadcasted_iota(jnp.int32, (WIN, LANES), 0)
    row = lax.rem(row, 8) * TILES + lax.div(row, 8)
    return jnp.where((row < ROWS) & (lanes_of((WIN, LANES)) < cols), 1.0, 0.0).astype(jnp.float32)


def spread(values):
    return jnp.broadcast_to(jnp.sum(values, axis=1, keepdims=True), values.shape)


def window_scratch(planes):
    return [pltpu.VMEM((planes, WIN, LANES), jnp.float32)] * 2


def first_diffuse(planes, levels, cols):
    coefs = 3 * levels

    def kernel(own, first, near, third, steps, coef, resid, weights, sums, out_g, buf, nat):
        for index in range(coefs):
            fetch_window(buf, nat, index, own, first, near, third, planes + index)
        make_coefs(coef, buf, levels, cols)
        for plane in range(planes):
            fetch_window(buf, nat, plane, own, first, near, third, plane)
        at, near_at = (planes + coefs) * ROWS, (planes + coefs) * 8
        weights[...] = spread((own[at:, :] + first[at:, :]) + (near[near_at:, :] + third[at:, :]))
        run_steps(buf, coef, steps, planes, levels)
        squares = jnp.zeros((WIN, LANES), jnp.float32)
        for plane in range(planes):
            value = SQRT_STATIC * buf[plane]
            resid[plane] = value
            buf[plane] = value
            squares += value * value
        sums[...] = jnp.zeros(sums.shape, jnp.float32)
        sums[4:5, :] = over_rows(own_cells(cols) * squares)
        run_steps(buf, coef, steps, planes, levels)
        for plane in range(planes):
            out_g[plane * ROWS : (plane + 1) * ROWS, :] = own_rows(buf[plane], nat, plane)

    outs = [
        f32(2, levels, WIN, LANES),
        f32(planes, WIN, LANES),
        f32(ROWS, LANES),
        f32(SUMS, LANES),
        f32(planes * ROWS, LANES),
    ]
    return kernel, outs, window_scratch(planes)


def second_diffuse(planes, levels, cols):
    def kernel(own, first, near, third, steps, coef, resid, weights, image, new, new_w, sums, facts, out_g, buf, nat):
        for plane in range(planes):
            fetch_window(buf, nat, plane, own, first, near, third, plane)
        at, near_at = planes * ROWS, planes * 8
        total = spread((own[at:, :] + first[at:, :]) + (near[near_at:, :] + third[at:, :]))
        energy = total[ROWS : ROWS + 1]
        rr = total[ROWS + 4 : ROWS + 5] + over_rows(weights[...] * weights[...])
        step = rr / (rr + energy)
        new_w[...] = weights[...] - step * (weights[...] + total[:ROWS])
        facts[...] = jnp.zeros(facts.shape, jnp.float32)
        facts[0:1, :] = rr
        facts[1:2, :] = step
        run_steps(buf, coef, steps, planes, levels)
        squares = jnp.zeros((WIN, LANES), jnp.float32)
        cross = jnp.zeros((WIN, LANES), jnp.float32)
        for plane in range(planes):
            direction = resid[plane]
            image_now = direction + SQRT_STATIC * buf[plane]
            value = direction - step * image_now
            image[plane] = image_now
            new[plane] = value
            buf[plane] = value
            squares += value * value
            cross += value * direction
        sums[...] = jnp.zeros(sums.shape, jnp.float32)
        sums[4:5, :] = over_rows(own_cells(cols) * squares)
        sums[5:6, :] = over_rows(own_cells(cols) * cross)
        run_steps(buf, coef, steps, planes, levels)
        for plane in range(planes):
            out_g[plane * ROWS : (plane + 1) * ROWS, :] = own_rows(buf[plane], nat, plane)

    block = f32(planes, WIN, LANES)
    outs = [block, block, f32(ROWS, LANES), f32(SUMS, LANES), f32(SUMS, LANES), f32(planes * ROWS, LANES)]
    return kernel, outs, window_scratch(planes)


def last_diffuse(planes, levels, cols):
    def kernel(
        own, first, near, third, steps, coef, resid, weights, image, new, new_w, facts, control, control_w, final, buf, nat
    ):
        for plane in range(planes):
            fetch_window(buf, nat, plane, own, first, None, third, plane)
        at = planes * ROWS
        lanes = (own[at:, :] + first[at:, :]) + (near[...] + third[at:, :])
        total = spread(lanes)
        rr, step = facts[0:1, :], facts[1:2, :]
        new_rr = total[4:5] + over_rows(new_w[...] * new_w[...])
        cross_rr = total[5:6] + over_rows(new_w[...] * weights[...])
        ratio = new_rr / rr
        gap = ratio - lanes[2:3]
        energy = spread(lanes[0:1] + gap * (2.0 * lanes[1:2] + gap * lanes[3:4]))
        squares = new_rr + ratio * (2.0 * cross_rr + ratio * rr)
        new_step = new_rr / (squares + energy)
        combined = step * weights[...] + new_step * (new_w[...] + ratio * weights[...])
        diagonal = lax.broadcasted_iota(jnp.int32, combined.shape, 0) == lanes_of(combined.shape)
        control_w[...] = over_rows(jnp.where(diagonal, combined, 0.0))[:, :ROWS]
        run_steps(buf, coef, steps, planes, levels)
        for plane in range(planes):
            direction, value = resid[plane], new[plane]
            new_direction = value + ratio * direction
            new_image = (value + SQRT_STATIC * buf[plane]) + ratio * image[plane]
            control[plane] = own_rows(step * direction + new_step * new_direction, nat, plane)[:, :cols]
            final[plane] = own_rows(value - new_step * new_image, nat, plane)[:, :cols]

    outs = [f32(planes, ROWS, cols), f32(1, ROWS), f32(planes, ROWS, cols)]
    return kernel, outs, window_scratch(planes)


def moved_to(values, x, y, z):
    sizes = [lax.axis_size(axis) for axis in AXES]
    here = [(a, b, c) for a in range(sizes[0]) for b in range(sizes[1]) for c in range(sizes[2])]
    number = {place: index for index, place in enumerate(here)}
    return lax.ppermute(values, AXES, [(number[a, b, c], number[a ^ x, b ^ y, c ^ z]) for a, b, c in here])


def across(kernel_of, out_z, out_e, vert, extra):
    other = moved_to(out_z, 0, 0, 1)
    edge = moved_to(out_e, 0, 1, 0)
    edge_other = moved_to(out_e, 0, 1, 1)
    kernel, outs = kernel_of
    own, near = call(kernel, outs, [VMEM] * (5 + len(extra)), (out_z, other, edge, edge_other, vert, *extra))
    return own, moved_to(own, 1, 0, 0), moved_to(near, 2, 0, 0), moved_to(own, 3, 0, 0)


def shards_small(
    innovation, obs_precision, error_scale, kappa_x, kappa_y, sea_mask, members, vertical, diffusion_steps
):
    fields, levels, rows, cols = innovation.shape
    count = members.shape[0]
    planes = fields * levels
    block = (planes, rows, cols)
    innov, prec, scale = (a.reshape(block) for a in (innovation, obs_precision, error_scale))
    ens = members.reshape((count,) + block)
    vert = jnp.broadcast_to(vertical.reshape(-1, 1), (vertical.size, LANES))
    steps = jnp.broadcast_to(diffusion_steps.astype(jnp.float32)[:, None], (fields, LANES))

    kernel, outs, scratch = start(planes, levels, cols, count)
    args = (innov, prec, scale, sea_mask, kappa_x, kappa_y, ens)
    out_z, out_e, coef_own = call(kernel, outs, [HBM] * 7, args, scratch, 56)
    parts = across(mix_back(True, True, planes, levels, cols, ROWS), out_z, out_e, vert, (coef_own,))
    kernel, outs, scratch = first_diffuse(planes, levels, cols)
    coef, resid, weights, sums, out_g = call(kernel, outs, [VMEM] * 5, (*parts, steps), scratch)

    kernel, outs, scratch = observe(planes, levels, cols, count, True)
    args = (out_g, moved_to(out_g, 0, 0, 1), weights, sums, vert, prec, scale, sea_mask, ens)
    out_z, out_e, seen = call(kernel, outs, [VMEM] * 9, args, scratch)
    parts = across(mix_back(False, True, planes, levels, cols, ROWS + SUMS), out_z, out_e, vert, ())
    kernel, outs, scratch = second_diffuse(planes, levels, cols)
    args = (*parts, steps, coef, resid, weights)
    image, new, new_w, sums, facts, out_g = call(kernel, outs, [VMEM] * 8, args, scratch)

    kernel, outs, scratch = observe(planes, levels, cols, count, False)
    args = (out_g, moved_to(out_g, 0, 0, 1), new_w, sums, vert, prec, scale, sea_mask, ens, seen)
    out_z, out_e = call(kernel, outs, [VMEM] * 10, args, scratch)
    parts = across(mix_back(False, False, planes, levels, cols, SUMS), out_z, out_e, vert, ())
    kernel, outs, scratch = last_diffuse(planes, levels, cols)
    args = (*parts, steps, coef, resid, weights, image, new, new_w, facts)
    control, control_w, final = call(kernel, outs, [VMEM] * 12, args, scratch)
    return control.reshape(innovation.shape), control_w.reshape(count), final.reshape(innovation.shape)


def shards(innovation, obs_precision, error_scale, kappa_x, kappa_y, sea_mask, members, vertical, diffusion_steps):
    arrays = (innovation, obs_precision, error_scale, kappa_x, kappa_y, sea_mask, members, vertical, diffusion_steps)
    sizes = tuple(lax.axis_size(axis) for axis in AXES)
    rows, cols = innovation.shape[2:]
    fits = rows == ROWS and members.shape[0] == ROWS and DEPTH <= cols <= LANES - DEPTH and ITERS == 2
    if sizes == (4, 2, 2) and fits:
        return shards_small(*arrays)
    return shards_any(*arrays)


def solution(mesh):
    placed = (
        P("grp", "gz", "gx", "gy"),
        P("grp", "gz", "gx", "gy"),
        P(None, "gz", "gx", "gy"),
        P("gz", "gx", "gy"),
        P("gz", "gx", "gy"),
        P("gz", "gx", "gy"),
        P("grp", None, "gz", "gx", "gy"),
        P(),
        P(),
    )
    return jax.shard_map(
        shards,
        mesh=mesh,
        in_specs=placed,
        out_specs=(P("grp", "gz", "gx", "gy"), P("grp"), P("grp", "gz", "gx", "gy")),
        check_vma=False,
    )
```

```python
import functools
import math


import jax
import jax.numpy as jnp
from jax import lax
from jax.experimental import pallas as pl
from jax.experimental.pallas import tpu as pltpu
from jax.sharding import PartitionSpec as P

KMAX = 10
ITERS = 2


static_share = 0.6
ensemble_share = 0.4


def extended(cells, sides, width):
    for axis, dim in sides:
        count = lax.axis_size(axis)
        head = lax.slice_in_dim(cells, 0, width, axis=dim)
        tail = lax.slice_in_dim(cells, cells.shape[dim] - width, cells.shape[dim], axis=dim)
        cells = jnp.concatenate(
            [
                lax.ppermute(tail, axis, [(i, (i + 1) % count) for i in range(count)]),
                cells,
                lax.ppermute(head, axis, [((i + 1) % count, i) for i in range(count)]),
            ],
            axis=dim,
        )
    return cells


def level_mix(source, mixing):
    local_levels = source.shape[1]
    gathered = lax.all_gather(source, "gz", axis=1, tiled=True)
    own_rows = lax.dynamic_slice_in_dim(
        mixing, lax.axis_index("gz") * local_levels, local_levels, 1
    )
    return jnp.einsum("flk,fkxy->flxy", own_rows, gathered, precision=lax.Precision.HIGHEST)


def diffuse(source, padded, step_counts, halo_depth):
    current = source
    for segment in range(KMAX // halo_depth):
        current = extended(current, (("gx", 2), ("gy", 3)), halo_depth)
        for substep in range(halo_depth):
            number = segment * halo_depth + substep
            offset = KMAX - halo_depth + substep
            rows_now = current.shape[2]
            cols_now = current.shape[3]
            window = padded[:, :, offset : offset + rows_now, offset : offset + cols_now]
            east_kappa = window[0]
            north_kappa = window[1]
            wet_window = window[2]
            east_coef = east_kappa[:, :-1, :] * wet_window[:, :-1, :] * wet_window[:, 1:, :]
            flux_east = east_coef * (current[:, :, 1:, :] - current[:, :, :-1, :])
            div_east = (flux_east[:, :, 1:, :] - flux_east[:, :, :-1, :])[:, :, :, 1:-1]
            north_coef = north_kappa[:, :, :-1] * wet_window[:, :, :-1] * wet_window[:, :, 1:]
            flux_north = north_coef * (current[:, :, :, 1:] - current[:, :, :, :-1])
            div_north = (flux_north[:, :, :, 1:] - flux_north[:, :, :, :-1])[:, :, 1:-1, :]
            active = (step_counts > number).astype(jnp.float32)[:, None, None, None]
            current = current[:, :, 1:-1, 1:-1] + active * (div_east + div_north)
    return current


def both_sums(terms, partial_value):
    return lax.psum((terms, partial_value), ("gx", "gy", "gz"))


def squares(resid_field):
    return lax.psum(jnp.sum(resid_field * resid_field), ("gx", "gy", "gz"))


def shards_any(
    innovation,
    obs_precision,
    error_scale,
    kappa_x,
    kappa_y,
    sea_mask,
    members,
    vertical,
    diffusion_steps,
):
    wet_cells = sea_mask.astype(jnp.float32)
    coefficients = jnp.stack([kappa_x, kappa_y, wet_cells])
    padded = extended(coefficients, (("gx", 2), ("gy", 3)), KMAX)
    cols_dev = wet_cells.shape[2]
    y_position = (
        lax.axis_index("gy") * cols_dev + jnp.arange(cols_dev + 2 * KMAX, dtype=jnp.int32) - KMAX
    )
    inside = ((y_position >= 0) & (y_position < cols_dev * lax.axis_size("gy"))).astype(jnp.float32)
    padded = jnp.stack([padded[0], padded[1], padded[2] * inside[None, None, :]])
    halo_depth = 2
    transposed = jnp.swapaxes(vertical, 1, 2)
    sqrt_static = math.sqrt(static_share)
    ens_scale = math.sqrt(ensemble_share / (members.shape[0] - 1))

    def static_back(masked):
        return sqrt_static * diffuse(
            level_mix(error_scale * masked, transposed), padded, diffusion_steps, halo_depth
        )

    def ensemble_terms(masked):
        return jnp.einsum("mflxy,flxy->m", members, masked, precision=lax.Precision.HIGHEST)

    masked = wet_cells * (obs_precision * innovation)
    resid_field = static_back(masked)
    ens_sum, field_norm = both_sums(ensemble_terms(masked), jnp.sum(resid_field * resid_field))
    resid_weights = ens_scale * ens_sum
    norm_now = field_norm + jnp.sum(resid_weights * resid_weights)
    dir_field, dir_weights = (resid_field, resid_weights)
    control_field = jnp.zeros_like(resid_field)
    control_weights = jnp.zeros(resid_weights.shape, jnp.float32)
    for iteration in range(ITERS):
        static = error_scale * level_mix(
            diffuse(dir_field, padded, diffusion_steps, halo_depth), vertical
        )
        ensemble = jnp.einsum(
            "m,mflxy->flxy", dir_weights, members, precision=lax.Precision.HIGHEST
        )
        observed = wet_cells * (sqrt_static * static + ens_scale * ensemble)
        weighted = obs_precision * observed
        masked = wet_cells * weighted
        image_field = dir_field + static_back(masked)
        ens_sum, curve_part = both_sums(ensemble_terms(masked), jnp.sum(dir_field * image_field))
        image_weights = dir_weights + ens_scale * ens_sum
        curvature = curve_part + jnp.sum(dir_weights * image_weights)
        step_length = norm_now / curvature
        control_field = control_field + step_length * dir_field
        control_weights = control_weights + step_length * dir_weights
        resid_field = resid_field - step_length * image_field
        resid_weights = resid_weights - step_length * image_weights
        if iteration + 1 < ITERS:
            norm_next = squares(resid_field) + jnp.sum(resid_weights * resid_weights)
            ratio_next = norm_next / norm_now
            dir_field = resid_field + ratio_next * dir_field
            dir_weights = resid_weights + ratio_next * dir_weights
            norm_now = norm_next
    return (control_field, control_weights, resid_field)

ROWS = 16
WIN = 56
TILES = WIN // 8
NEAR_TILES = 5
LANES = 128
DEPTH = 2 * KMAX
GROUP = LANES // DEPTH
SUMS = 8
FETCHES = 4
AXES = ("gx", "gy", "gz")
VMEM = pl.BlockSpec(memory_space=pltpu.VMEM)
HBM = pl.BlockSpec(memory_space=pltpu.HBM)
SQRT_STATIC = math.sqrt(static_share)


def f32(*shape):
    return jax.ShapeDtypeStruct(shape, jnp.float32)


def call(kernel, outs, specs, args, scratch=(), grant=32):
    return pl.pallas_call(
        kernel,
        out_shape=outs,
        in_specs=specs,
        out_specs=[VMEM] * len(outs),
        scratch_shapes=list(scratch),
        compiler_params=pltpu.CompilerParams(vmem_limit_bytes=grant * 1024 * 1024),
    )(*args)


def lanes_of(shape):
    return lax.broadcasted_iota(jnp.int32, shape, len(shape) - 1)


def tile(ref, index, size=ROWS):
    return ref[index * size : (index + 1) * size, :]


def pack_edges(out_ref, planes, cols):
    first = jnp.where(lax.axis_index("gy") == 0, cols - DEPTH, 0)
    lane = lanes_of((ROWS, LANES))
    for group in range(-(-len(planes) // GROUP)):
        packed = jnp.zeros((ROWS, LANES), jnp.float32)
        for slot, plane in enumerate(planes[group * GROUP : (group + 1) * GROUP]):
            moved = pltpu.roll(plane, lax.rem(DEPTH * slot - first + LANES, LANES), 1)
            packed = jnp.where((lane >= DEPTH * slot) & (lane < DEPTH * (slot + 1)), moved, packed)
        out_ref[group * ROWS : (group + 1) * ROWS, :] = packed


def with_edge(own, edge_ref, index, cols):
    group, slot = divmod(index, GROUP)
    moved = pltpu.roll(tile(edge_ref, group), (cols - DEPTH * slot) % LANES, 1)
    return jnp.where(lanes_of(own.shape) < cols, own, moved)


def over_rows(values):
    return jnp.sum(values, axis=0, keepdims=True)


def whole(values):
    return jnp.sum(over_rows(values), axis=1, keepdims=True)


def coefficient_planes(coef, sources, levels, cols):
    coef[...] = jnp.zeros(coef.shape, jnp.float32)
    for level in range(levels):
        for kind, source in enumerate(sources):
            at = (kind * levels + level) * ROWS
            coef[at : at + ROWS, :cols] = source[level].astype(jnp.float32)


def project(out_z, at, totals, scale):
    for m, total in enumerate(totals):
        out_z[at + m : at + m + 1, : total.shape[1]] = scale * over_rows(total)


def start(planes, levels, cols, count):
    ens_scale = math.sqrt(ensemble_share / (count - 1))
    base = planes * ROWS
    edge_rows = -(-(planes + 3 * levels) // GROUP) * ROWS

    def kernel(*refs):
        sources, (out_z, out_e, coef), copies, weighted, sems = refs[:7], refs[7:10], refs[10:17], refs[17], refs[18]
        pairs = list(zip(sources[:6], copies[:6], strict=True))
        for part in range(FETCHES):
            rows = pl.ds(part * (count // FETCHES), count // FETCHES)
            pairs.append((sources[6].at[rows], copies[6].at[rows]))
        moves = [pltpu.make_async_copy(a, b, sems.at[i]) for i, (a, b) in enumerate(pairs)]
        for move in moves:
            move.start()
        innov, prec, scale, mask, kx, ky, members = copies
        out_z[...] = jnp.zeros(out_z.shape, jnp.float32)
        for move in moves[:6]:
            move.wait()
        coefficient_planes(coef, (kx, ky, mask), levels, cols)
        for plane in range(planes):
            weighted[plane] = mask[plane % levels].astype(jnp.float32) * (prec[plane] * innov[plane])
            out_z[plane * ROWS : (plane + 1) * ROWS, :cols] = scale[plane] * weighted[plane]
        edges = [tile(out_z, plane) for plane in range(planes)]
        pack_edges(out_e, edges + [tile(coef, index) for index in range(3 * levels)], cols)
        for move in moves[6:]:
            move.wait()
        totals = [jnp.zeros((ROWS, cols), jnp.float32) for _ in range(count)]
        for plane in range(planes):
            for m in range(count):
                totals[m] += members[m, plane] * weighted[plane]
        project(out_z, base, totals, ens_scale)
        out_e[edge_rows:, :] = out_z[base:, :]

    outs = [f32(base + ROWS, LANES), f32(edge_rows + ROWS, LANES), f32(3 * levels * ROWS, LANES)]
    field, flat = (planes, ROWS, cols), (levels, ROWS, cols)
    kept = [(field, jnp.float32)] * 3 + [(flat, jnp.int32)] + [(flat, jnp.float32)] * 2 + [((count,) + field, jnp.float32)]
    scratch = [pltpu.VMEM(*one) for one in kept] + [pltpu.VMEM(field, jnp.float32), pltpu.SemaphoreType.DMA((6 + FETCHES,))]
    return kernel, outs, scratch


def observe(planes, levels, cols, count, with_weights):
    ens_scale = math.sqrt(ensemble_share / (count - 1))
    base = planes * ROWS
    edge_rows = -(-planes // GROUP) * ROWS
    sums_at = base + ROWS * with_weights

    def kernel(*refs):
        own, other, weights, sums, vert, prec, scale, mask, members = refs[:9]
        if with_weights:
            out_z, out_e, seen = refs[9:]
        else:
            seen, out_z, out_e, now = refs[9:]
        out_z[...] = jnp.zeros(out_z.shape, jnp.float32)
        totals = [jnp.zeros((ROWS, cols), jnp.float32) for _ in range(count)]
        energy = jnp.zeros((ROWS, cols), jnp.float32)
        cross = jnp.zeros((ROWS, cols), jnp.float32)
        here = lax.axis_index("gz") * levels
        there = (1 - lax.axis_index("gz")) * levels
        for plane in range(planes):
            field, level = divmod(plane, levels)
            wet = mask[level].astype(jnp.float32)
            static = jnp.zeros((ROWS, cols), jnp.float32)
            for k in range(levels):
                row = (field * 2 * levels + here + level) * 2 * levels
                static += vert[pl.ds(row + here + k, 1), :cols] * tile(own, field * levels + k)[:, :cols]
                static += vert[pl.ds(row + there + k, 1), :cols] * tile(other, field * levels + k)[:, :cols]
            ensemble = jnp.zeros((ROWS, cols), jnp.float32)
            for m in range(count):
                ensemble += weights[m : m + 1, :cols] * members[m, plane]
            seen_now = wet * (SQRT_STATIC * (scale[plane] * static) + ens_scale * ensemble)
            weighted = wet * (prec[plane] * seen_now)
            if with_weights:
                seen[plane] = seen_now
                energy += seen_now * weighted
                for m in range(count):
                    totals[m] += members[m, plane] * weighted
            else:
                now[plane] = seen_now
                before = seen[plane]
                energy += before * (prec[plane] * before)
                cross += before * weighted
            out_z[plane * ROWS : (plane + 1) * ROWS, :cols] = scale[plane] * weighted
        if with_weights:
            project(out_z, base, totals, ens_scale)
        out_z[sums_at : sums_at + SUMS, :] = sums[...]
        if with_weights:
            out_z[sums_at : sums_at + 1, :cols] = over_rows(energy)
        else:
            energy, cross = whole(energy), whole(cross)
            share = jnp.where(energy > 0.0, -cross / jnp.where(energy > 0.0, energy, 1.0), 0.0)
            rest = jnp.zeros((ROWS, cols), jnp.float32)
            left = jnp.zeros((ROWS, cols), jnp.float32)
            for plane in range(planes):
                before = seen[plane]
                gap = now[plane] + share * before
                rest += gap * (prec[plane] * gap)
                left += before * (prec[plane] * gap)
            place = (lax.axis_index("gx") * 2 + lax.axis_index("gy")) * 2 + lax.axis_index("gz")
            own_lane = lanes_of((1, LANES)) == place
            for index, value in enumerate((whole(rest), whole(left), share, energy)):
                out_z[sums_at + index : sums_at + index + 1, :] = jnp.where(own_lane, value, 0.0)
        pack_edges(out_e, [tile(out_z, plane) for plane in range(planes)], cols)
        out_e[edge_rows:, :] = out_z[base:, :]

    tail = (ROWS * with_weights) + SUMS
    outs = [f32(base + tail, LANES), f32(edge_rows + tail, LANES)]
    if with_weights:
        return kernel, outs + [f32(planes, ROWS, cols)], ()
    return kernel, outs, [pltpu.VMEM((planes, ROWS, cols), jnp.float32)]


def mix_back(first, far, planes, levels, cols, tail):
    base = planes * ROWS
    coefs = 2 * levels if first else 0
    fields = planes // levels
    count = planes + coefs
    sent = -(-planes * KMAX // 8) * 8

    def kernel(*refs):
        if first:
            own, other, edge, edge_other, vert, raw, out_all, out_near = refs
        elif far:
            own, other, edge, edge_other, vert, out_all, out_near = refs
        else:
            own, other, edge, edge_other, vert, out_own, out_one, out_three, out_sums = refs
        here = lax.axis_index("gz") * levels
        there = (1 - lax.axis_index("gz")) * levels
        even = lax.rem(lax.axis_index("gx"), 2) == 0
        upper = lax.broadcasted_iota(jnp.int32, (8, LANES), 0) < 4

        def put(index, values):
            if far:
                out_all[index * ROWS : (index + 1) * ROWS, :] = values
                out_near[index * 8 : (index + 1) * 8, :] = jnp.where(upper, values[:8], values[8:])
            else:
                out_own[index * ROWS : (index + 1) * ROWS, :] = values
                head, end = values[:KMAX], values[ROWS - KMAX :]
                out_one[index * KMAX : (index + 1) * KMAX, :] = jnp.where(even, end, head)
                out_three[index * KMAX : (index + 1) * KMAX, :] = jnp.where(even, head, end)

        for field in range(fields):
            mine = [with_edge(tile(own, field * levels + l), edge, field * levels + l, cols) for l in range(levels)]
            theirs = [
                with_edge(tile(other, field * levels + l), edge_other, field * levels + l, cols) for l in range(levels)
            ]
            for k in range(levels):
                mixed = jnp.zeros((ROWS, LANES), jnp.float32)
                for l in range(levels):
                    block = field * 2 * levels
                    mixed += vert[pl.ds((block + here + l) * 2 * levels + here + k, 1), :] * mine[l]
                    mixed += vert[pl.ds((block + there + l) * 2 * levels + here + k, 1), :] * theirs[l]
                put(field * levels + k, mixed)
        packed = -(-(planes + (3 * levels if first else 0)) // GROUP) * ROWS
        total = (own[base:, :] + other[base:, :]) + (edge[packed:, :] + edge_other[packed:, :])
        if not far:
            out_sums[...] = total
            out_one[sent:, :] = total
            out_three[sent:, :] = total
            return
        at, near_at = count * ROWS, count * 8
        out_all[at : at + tail, :] = total
        out_near[near_at : near_at + tail, :] = total
        if first:
            last = jnp.where(lax.axis_index("gy") == 0, LANES - 1, cols - 1)
            lane = lanes_of((ROWS, LANES))
            bottom = lax.broadcasted_iota(jnp.int32, (ROWS, LANES), 0) == ROWS - 1
            wets = jnp.zeros((8, LANES), jnp.float32)
            for level in range(levels):
                kx, ky, wet = (
                    with_edge(tile(raw, kind * levels + level), edge, planes + kind * levels + level, cols) for kind in range(3)
                )
                put(planes + level, kx * wet * jnp.where(bottom, 1.0, pltpu.roll(wet, ROWS - 1, 0)))
                put(planes + levels + level, jnp.where(lane == last, 0.0, ky * wet * pltpu.roll(wet, LANES - 1, 1)))
                wets = jnp.where(lax.broadcasted_iota(jnp.int32, (8, LANES), 0) == level, wet[:1], wets)
            out_all[at + tail :, :] = wets
            out_near[near_at + tail :, :] = wets

    if not far:
        return kernel, [f32(base, LANES)] + [f32(sent + tail, LANES)] * 2 + [f32(tail, LANES)]
    tail_all = tail + (8 if first else 0)
    return kernel, [f32(count * ROWS + tail_all, LANES), f32(count * 8 + tail_all, LANES)]


def pass_on(*refs):
    half = len(refs) // 2
    for source, target in zip(refs[:half], refs[half:], strict=True):
        target[...] = source[...]


def is_even():
    return lax.rem(lax.axis_index("gx"), 2) == 0


def far_window(nat, index, own, first, near, third, slot):
    even = is_even()
    one, three = tile(first, slot), tile(third, slot)
    nat[index, 0:16, :] = tile(own, slot)
    nat[index, 16:32, :] = jnp.where(even, one, three)
    nat[index, 32:40, :] = tile(near, slot, 8)
    nat[index, 40:56, :] = jnp.where(even, three, one)


def shorten(nat, index):
    return jnp.concatenate([nat[index, 0:28, :], nat[index, 44:56, :]], axis=0)


def dealt(nat, index, tiles):
    return [nat[index, pl.ds(t, 8, stride=tiles), :] for t in range(tiles)]


def deal(buf, nat, index, tiles):
    for t, values in enumerate(dealt(nat, index, tiles)):
        buf[index, t * 8 : (t + 1) * 8, :] = values


def undeal(nat, buf, index, tiles):
    for t in range(tiles):
        nat[index, pl.ds(t, 8, stride=tiles), :] = buf[index, t * 8 : (t + 1) * 8, :]


def eight(ref, tiles, *index):
    return [ref[(*index, pl.ds(t * 8, 8), slice(None))] for t in range(tiles)]


def after(tiles):
    return tiles[1:] + [pltpu.roll(tiles[0], 7, 0)]


def run_steps(buf, coef, steps, planes, levels, tiles):
    for number in range(KMAX):
        for level in range(levels):
            east, north = eight(coef, tiles, 0, level), eight(coef, tiles, 1, level)
            for field in range(planes // levels):
                plane = field * levels + level
                active = jnp.where(steps[field : field + 1, :] > float(number), 1.0, 0.0).astype(jnp.float32)
                u = eight(buf, tiles, plane)
                flux_east = [c * (v - w) for c, v, w in zip(east, after(u), u, strict=True)]
                flux_west = [pltpu.roll(flux_east[-1], 1, 0)] + flux_east[:-1]
                for t in range(tiles):
                    flux_north = north[t] * (pltpu.roll(u[t], LANES - 1, 1) - u[t])
                    change = (flux_east[t] - flux_west[t]) + (flux_north - pltpu.roll(flux_north, 1, 1))
                    buf[plane, t * 8 : (t + 1) * 8, :] = u[t] + active * change


def own_sum(values, cols):
    return over_rows(jnp.where(lanes_of(values.shape) < cols, values, 0.0))


def spread(values):
    return jnp.broadcast_to(jnp.sum(values, axis=1, keepdims=True), values.shape)


def window_scratch(planes):
    return [pltpu.VMEM((planes, WIN, LANES), jnp.float32)] * 2


def diffuse_own(out_g, field, buf, nat, coef, steps, planes, levels):
    for plane in range(planes):
        for t, values in enumerate(dealt(field, plane, NEAR_TILES)):
            buf[plane, t * 8 : (t + 1) * 8, :] = values
    run_steps(buf, coef, steps, planes, levels, NEAR_TILES)
    for plane in range(planes):
        undeal(nat, buf, plane, NEAR_TILES)
        out_g[plane * ROWS : (plane + 1) * ROWS, :] = nat[plane, :ROWS, :]


def first_diffuse(planes, levels, cols):
    coefs = 2 * levels

    def kernel(own, first, near, third, steps, coef, coef_near, resid, weights, sums, out_g, buf, nat):
        even = is_even()
        at, near_at = (planes + coefs) * ROWS, (planes + coefs) * 8
        for index in range(coefs):
            far_window(nat, index, own, first, near, third, planes + index)
            if index < levels:
                row, near_row = at + ROWS + index, near_at + ROWS + index
                one, three = first[row : row + 1, :], third[row : row + 1, :]
                nat[index, 15:16, :] = nat[index, 15:16, :] * jnp.where(even, one, three)
                nat[index, 31:32, :] = nat[index, 31:32, :] * near[near_row : near_row + 1, :]
                nat[index, 39:40, :] = nat[index, 39:40, :] * jnp.where(even, three, one)
                nat[index, 55:56, :] = nat[index, 55:56, :] * own[row : row + 1, :]
            kind, level = divmod(index, levels)
            for t, values in enumerate(dealt(nat, index, TILES)):
                coef[kind, level, t * 8 : (t + 1) * 8, :] = values
            buf[index, : 8 * NEAR_TILES, :] = shorten(nat, index)
            for t, values in enumerate(dealt(buf, index, NEAR_TILES)):
                coef_near[kind, level, t * 8 : (t + 1) * 8, :] = values
        for plane in range(planes):
            far_window(nat, plane, own, first, near, third, plane)
            deal(buf, nat, plane, TILES)
        sent = slice(at, at + ROWS)
        weights[...] = spread((own[sent, :] + first[sent, :]) + (near[near_at : near_at + ROWS, :] + third[sent, :]))
        run_steps(buf, coef, steps, planes, levels, TILES)
        squares = jnp.zeros((ROWS, LANES), jnp.float32)
        for plane in range(planes):
            undeal(nat, buf, plane, TILES)
            value = SQRT_STATIC * shorten(nat, plane)
            resid[plane] = value
            squares += value[:ROWS] * value[:ROWS]
        sums[...] = jnp.zeros(sums.shape, jnp.float32)
        sums[4:5, :] = own_sum(squares, cols)
        diffuse_own(out_g, resid, buf, nat, coef_near, steps, planes, levels)

    outs = [
        f32(2, levels, WIN, LANES),
        f32(2, levels, 8 * NEAR_TILES, LANES),
        f32(planes, 8 * NEAR_TILES, LANES),
        f32(ROWS, LANES),
        f32(SUMS, LANES),
        f32(planes * ROWS, LANES),
    ]
    return kernel, outs, window_scratch(planes)


def second_diffuse(planes, levels, cols):
    def kernel(
        own, first, near, third, steps, coef, coef_near, resid, weights, image, new, new_w, sums, facts, out_g, buf, nat, field
    ):
        for plane in range(planes):
            far_window(nat, plane, own, first, near, third, plane)
            deal(buf, nat, plane, TILES)
        at, near_at = planes * ROWS, planes * 8
        total = spread((own[at:, :] + first[at:, :]) + (near[near_at:, :] + third[at:, :]))
        energy = total[ROWS : ROWS + 1]
        rr = total[ROWS + 4 : ROWS + 5] + over_rows(weights[...] * weights[...])
        step = rr / (rr + energy)
        new_w[...] = weights[...] - step * (weights[...] + total[:ROWS])
        facts[...] = jnp.zeros(facts.shape, jnp.float32)
        facts[0:1, :] = rr
        facts[1:2, :] = step
        run_steps(buf, coef, steps, planes, levels, TILES)
        squares = jnp.zeros((ROWS, LANES), jnp.float32)
        cross = jnp.zeros((ROWS, LANES), jnp.float32)
        for plane in range(planes):
            undeal(nat, buf, plane, TILES)
            direction = resid[plane]
            image_now = direction + SQRT_STATIC * shorten(nat, plane)
            value = direction - step * image_now
            field[plane] = value
            image[plane] = image_now[:ROWS]
            new[plane] = value[:ROWS]
            squares += value[:ROWS] * value[:ROWS]
            cross += value[:ROWS] * direction[:ROWS]
        sums[...] = jnp.zeros(sums.shape, jnp.float32)
        sums[4:5, :] = own_sum(squares, cols)
        sums[5:6, :] = own_sum(cross, cols)
        diffuse_own(out_g, field, buf, nat, coef_near, steps, planes, levels)

    block = f32(planes, ROWS, LANES)
    outs = [block, block, f32(ROWS, LANES), f32(SUMS, LANES), f32(SUMS, LANES), f32(planes * ROWS, LANES)]
    return kernel, outs, window_scratch(planes) + [pltpu.VMEM((planes, 8 * NEAR_TILES, LANES), jnp.float32)]


def last_diffuse(planes, levels, cols):
    def kernel(
        own, one, three, sums, sums_two, steps, coef, resid, weights, image, new, new_w, facts,
        control, control_w, final, buf, nat,
    ):
        even = is_even()
        gap_rows = jnp.zeros((4, LANES), jnp.float32)
        for plane in range(planes):
            first, third = tile(one, plane, KMAX), tile(three, plane, KMAX)
            nat[plane, 0:16, :] = tile(own, plane)
            nat[plane, 16:26, :] = jnp.where(even, first, third)
            nat[plane, 26:30, :] = gap_rows
            nat[plane, 30:40, :] = jnp.where(even, third, first)
            deal(buf, nat, plane, NEAR_TILES)
        sent = one.shape[0] - SUMS
        lanes = (sums[...] + one[sent:, :]) + (sums_two[...] + three[sent:, :])
        total = spread(lanes)
        rr, step = facts[0:1, :], facts[1:2, :]
        new_rr = total[4:5] + over_rows(new_w[...] * new_w[...])
        cross_rr = total[5:6] + over_rows(new_w[...] * weights[...])
        ratio = new_rr / rr
        gap = ratio - lanes[2:3]
        energy = spread(lanes[0:1] + gap * (2.0 * lanes[1:2] + gap * lanes[3:4]))
        squares = new_rr + ratio * (2.0 * cross_rr + ratio * rr)
        new_step = new_rr / (squares + energy)
        combined = step * weights[...] + new_step * (new_w[...] + ratio * weights[...])
        diagonal = lax.broadcasted_iota(jnp.int32, combined.shape, 0) == lanes_of(combined.shape)
        control_w[...] = over_rows(jnp.where(diagonal, combined, 0.0))[:, :ROWS]
        run_steps(buf, coef, steps, planes, levels, NEAR_TILES)
        for plane in range(planes):
            undeal(nat, buf, plane, NEAR_TILES)
            direction, value = resid[plane, :ROWS, :], new[plane]
            new_direction = value + ratio * direction
            new_image = (value + SQRT_STATIC * nat[plane, :ROWS, :]) + ratio * image[plane]
            control[plane] = (step * direction + new_step * new_direction)[:, :cols]
            final[plane] = (value - new_step * new_image)[:, :cols]

    outs = [f32(planes, ROWS, cols), f32(1, ROWS), f32(planes, ROWS, cols)]
    return kernel, outs, window_scratch(planes)


def moved_to(values, x, y, z):
    sizes = [lax.axis_size(axis) for axis in AXES]
    here = [(a, b, c) for a in range(sizes[0]) for b in range(sizes[1]) for c in range(sizes[2])]
    number = {place: index for index, place in enumerate(here)}
    return lax.ppermute(values, AXES, [(number[a, b, c], number[a ^ x, b ^ y, c ^ z]) for a, b, c in here])


def mix_round(kernel_of, out_z, out_e, vert, raw=None):
    other = moved_to(out_z, 0, 0, 1)
    edge = moved_to(out_e, 0, 1, 0)
    edge_other = moved_to(out_e, 0, 1, 1)
    kernel, outs = kernel_of
    args = (out_z, other, edge, edge_other, vert)
    if raw is not None:
        own, raw = call(pass_on, [f32(*out_z.shape), f32(*raw.shape)], [VMEM] * 2, (out_z, raw))
        args = (own, *args[1:], raw)
    return call(kernel, outs, [VMEM] * len(args), args)


def far_round(own, near):
    return own, moved_to(own, 1, 0, 0), moved_to(near, 2, 0, 0), moved_to(own, 3, 0, 0)


def shards_small(
    innovation, obs_precision, error_scale, kappa_x, kappa_y, sea_mask, members, vertical, diffusion_steps
):
    fields, levels, rows, cols = innovation.shape
    count = members.shape[0]
    planes = fields * levels
    block = (planes, rows, cols)
    innov, prec, scale = (a.reshape(block) for a in (innovation, obs_precision, error_scale))
    ens = members.reshape((count,) + block)
    vert = jnp.broadcast_to(vertical.reshape(-1, 1), (vertical.size, LANES))
    steps = jnp.broadcast_to(diffusion_steps.astype(jnp.float32)[:, None], (fields, LANES))

    kernel, outs, scratch = start(planes, levels, cols, count)
    args = (innov, prec, scale, sea_mask, kappa_x, kappa_y, ens)
    out_z, out_e, raw = call(kernel, outs, [HBM] * 7, args, scratch, 56)
    parts = far_round(*mix_round(mix_back(True, True, planes, levels, cols, ROWS), out_z, out_e, vert, raw))
    kernel, outs, scratch = first_diffuse(planes, levels, cols)
    coef, coef_near, resid, weights, sums, out_g = call(kernel, outs, [VMEM] * 5, (*parts, steps), scratch)

    kernel, outs, scratch = observe(planes, levels, cols, count, True)
    args = (out_g, moved_to(out_g, 0, 0, 1), weights, sums, vert, prec, scale, sea_mask, ens)
    out_z, out_e, seen = call(kernel, outs, [VMEM] * 9, args, scratch)
    parts = far_round(*mix_round(mix_back(False, True, planes, levels, cols, ROWS + SUMS), out_z, out_e, vert))
    kernel, outs, scratch = second_diffuse(planes, levels, cols)
    args = (*parts, steps, coef, coef_near, resid, weights)
    image, new, new_w, sums, facts, out_g = call(kernel, outs, [VMEM] * 9, args, scratch)

    kernel, outs, scratch = observe(planes, levels, cols, count, False)
    args = (out_g, moved_to(out_g, 0, 0, 1), new_w, sums, vert, prec, scale, sea_mask, ens, seen)
    out_z, out_e = call(kernel, outs, [VMEM] * 10, args, scratch)
    own, one, three, sums = mix_round(mix_back(False, False, planes, levels, cols, SUMS), out_z, out_e, vert)
    parts = (own, moved_to(one, 1, 0, 0), moved_to(three, 3, 0, 0), sums, moved_to(sums, 2, 0, 0))
    kernel, outs, scratch = last_diffuse(planes, levels, cols)
    args = (*parts, steps, coef_near, resid, weights, image, new, new_w, facts)
    control, control_w, final = call(kernel, outs, [VMEM] * 13, args, scratch)
    return control.reshape(innovation.shape), control_w.reshape(count), final.reshape(innovation.shape)


def shards(innovation, obs_precision, error_scale, kappa_x, kappa_y, sea_mask, members, vertical, diffusion_steps):
    arrays = (innovation, obs_precision, error_scale, kappa_x, kappa_y, sea_mask, members, vertical, diffusion_steps)
    sizes = tuple(lax.axis_size(axis) for axis in AXES)
    rows, cols = innovation.shape[2:]
    fits = rows == ROWS and members.shape[0] == ROWS and DEPTH <= cols <= LANES - DEPTH and ITERS == 2
    if sizes == (4, 2, 2) and fits:
        return shards_small(*arrays)
    return shards_any(*arrays)


def solution(mesh):
    placed = (
        P("grp", "gz", "gx", "gy"),
        P("grp", "gz", "gx", "gy"),
        P(None, "gz", "gx", "gy"),
        P("gz", "gx", "gy"),
        P("gz", "gx", "gy"),
        P("gz", "gx", "gy"),
        P("grp", None, "gz", "gx", "gy"),
        P(),
        P(),
    )
    return jax.shard_map(
        shards,
        mesh=mesh,
        in_specs=placed,
        out_specs=(P("grp", "gz", "gx", "gy"), P("grp"), P("grp", "gz", "gx", "gy")),
        check_vma=False,
    )
```

```python
import functools
import math


import jax
import jax.numpy as jnp
from jax import lax
from jax.experimental import pallas as pl
from jax.experimental.pallas import tpu as pltpu
from jax.sharding import PartitionSpec as P

KMAX = 10
ITERS = 2


static_share = 0.6
ensemble_share = 0.4


def extended(cells, sides, width):
    for axis, dim in sides:
        count = lax.axis_size(axis)
        head = lax.slice_in_dim(cells, 0, width, axis=dim)
        tail = lax.slice_in_dim(cells, cells.shape[dim] - width, cells.shape[dim], axis=dim)
        cells = jnp.concatenate(
            [
                lax.ppermute(tail, axis, [(i, (i + 1) % count) for i in range(count)]),
                cells,
                lax.ppermute(head, axis, [((i + 1) % count, i) for i in range(count)]),
            ],
            axis=dim,
        )
    return cells


def level_mix(source, mixing):
    local_levels = source.shape[1]
    gathered = lax.all_gather(source, "gz", axis=1, tiled=True)
    own_rows = lax.dynamic_slice_in_dim(
        mixing, lax.axis_index("gz") * local_levels, local_levels, 1
    )
    return jnp.einsum("flk,fkxy->flxy", own_rows, gathered, precision=lax.Precision.HIGHEST)


def diffuse(source, padded, step_counts, halo_depth):
    current = source
    for segment in range(KMAX // halo_depth):
        current = extended(current, (("gx", 2), ("gy", 3)), halo_depth)
        for substep in range(halo_depth):
            number = segment * halo_depth + substep
            offset = KMAX - halo_depth + substep
            rows_now = current.shape[2]
            cols_now = current.shape[3]
            window = padded[:, :, offset : offset + rows_now, offset : offset + cols_now]
            east_kappa = window[0]
            north_kappa = window[1]
            wet_window = window[2]
            east_coef = east_kappa[:, :-1, :] * wet_window[:, :-1, :] * wet_window[:, 1:, :]
            flux_east = east_coef * (current[:, :, 1:, :] - current[:, :, :-1, :])
            div_east = (flux_east[:, :, 1:, :] - flux_east[:, :, :-1, :])[:, :, :, 1:-1]
            north_coef = north_kappa[:, :, :-1] * wet_window[:, :, :-1] * wet_window[:, :, 1:]
            flux_north = north_coef * (current[:, :, :, 1:] - current[:, :, :, :-1])
            div_north = (flux_north[:, :, :, 1:] - flux_north[:, :, :, :-1])[:, :, 1:-1, :]
            active = (step_counts > number).astype(jnp.float32)[:, None, None, None]
            current = current[:, :, 1:-1, 1:-1] + active * (div_east + div_north)
    return current


def both_sums(terms, partial_value):
    return lax.psum((terms, partial_value), ("gx", "gy", "gz"))


def squares(resid_field):
    return lax.psum(jnp.sum(resid_field * resid_field), ("gx", "gy", "gz"))


def shards_any(
    innovation,
    obs_precision,
    error_scale,
    kappa_x,
    kappa_y,
    sea_mask,
    members,
    vertical,
    diffusion_steps,
):
    wet_cells = sea_mask.astype(jnp.float32)
    coefficients = jnp.stack([kappa_x, kappa_y, wet_cells])
    padded = extended(coefficients, (("gx", 2), ("gy", 3)), KMAX)
    cols_dev = wet_cells.shape[2]
    y_position = (
        lax.axis_index("gy") * cols_dev + jnp.arange(cols_dev + 2 * KMAX, dtype=jnp.int32) - KMAX
    )
    inside = ((y_position >= 0) & (y_position < cols_dev * lax.axis_size("gy"))).astype(jnp.float32)
    padded = jnp.stack([padded[0], padded[1], padded[2] * inside[None, None, :]])
    halo_depth = 2
    transposed = jnp.swapaxes(vertical, 1, 2)
    sqrt_static = math.sqrt(static_share)
    ens_scale = math.sqrt(ensemble_share / (members.shape[0] - 1))

    def static_back(masked):
        return sqrt_static * diffuse(
            level_mix(error_scale * masked, transposed), padded, diffusion_steps, halo_depth
        )

    def ensemble_terms(masked):
        return jnp.einsum("mflxy,flxy->m", members, masked, precision=lax.Precision.HIGHEST)

    masked = wet_cells * (obs_precision * innovation)
    resid_field = static_back(masked)
    ens_sum, field_norm = both_sums(ensemble_terms(masked), jnp.sum(resid_field * resid_field))
    resid_weights = ens_scale * ens_sum
    norm_now = field_norm + jnp.sum(resid_weights * resid_weights)
    dir_field, dir_weights = (resid_field, resid_weights)
    control_field = jnp.zeros_like(resid_field)
    control_weights = jnp.zeros(resid_weights.shape, jnp.float32)
    for iteration in range(ITERS):
        static = error_scale * level_mix(
            diffuse(dir_field, padded, diffusion_steps, halo_depth), vertical
        )
        ensemble = jnp.einsum(
            "m,mflxy->flxy", dir_weights, members, precision=lax.Precision.HIGHEST
        )
        observed = wet_cells * (sqrt_static * static + ens_scale * ensemble)
        weighted = obs_precision * observed
        masked = wet_cells * weighted
        image_field = dir_field + static_back(masked)
        ens_sum, curve_part = both_sums(ensemble_terms(masked), jnp.sum(dir_field * image_field))
        image_weights = dir_weights + ens_scale * ens_sum
        curvature = curve_part + jnp.sum(dir_weights * image_weights)
        step_length = norm_now / curvature
        control_field = control_field + step_length * dir_field
        control_weights = control_weights + step_length * dir_weights
        resid_field = resid_field - step_length * image_field
        resid_weights = resid_weights - step_length * image_weights
        if iteration + 1 < ITERS:
            norm_next = squares(resid_field) + jnp.sum(resid_weights * resid_weights)
            ratio_next = norm_next / norm_now
            dir_field = resid_field + ratio_next * dir_field
            dir_weights = resid_weights + ratio_next * dir_weights
            norm_now = norm_next
    return (control_field, control_weights, resid_field)

ROWS = 16
WIN = 56
TILES = WIN // 8
NEAR_TILES = 5
LANES = 128
DEPTH = 2 * KMAX
GROUP = LANES // DEPTH
SUMS = 8
FETCHES = 4
AXES = ("gx", "gy", "gz")
VMEM = pl.BlockSpec(memory_space=pltpu.VMEM)
HBM = pl.BlockSpec(memory_space=pltpu.HBM)
SQRT_STATIC = math.sqrt(static_share)


def f32(*shape):
    return jax.ShapeDtypeStruct(shape, jnp.float32)


def call(kernel, outs, specs, args, scratch=(), grant=32):
    return pl.pallas_call(
        kernel,
        out_shape=outs,
        in_specs=specs,
        out_specs=[VMEM] * len(outs),
        scratch_shapes=list(scratch),
        compiler_params=pltpu.CompilerParams(vmem_limit_bytes=grant * 1024 * 1024),
    )(*args)


def lanes_of(shape):
    return lax.broadcasted_iota(jnp.int32, shape, len(shape) - 1)


def tile(ref, index, size=ROWS):
    return ref[index * size : (index + 1) * size, :]


def pack_edges(out_ref, planes, cols):
    first = jnp.where(lax.axis_index("gy") == 0, cols - DEPTH, 0)
    lane = lanes_of((ROWS, LANES))
    for group in range(-(-len(planes) // GROUP)):
        packed = jnp.zeros((ROWS, LANES), jnp.float32)
        for slot, plane in enumerate(planes[group * GROUP : (group + 1) * GROUP]):
            moved = pltpu.roll(plane, lax.rem(DEPTH * slot - first + LANES, LANES), 1)
            packed = jnp.where((lane >= DEPTH * slot) & (lane < DEPTH * (slot + 1)), moved, packed)
        out_ref[group * ROWS : (group + 1) * ROWS, :] = packed


def with_edge(own, edge_ref, index, cols):
    group, slot = divmod(index, GROUP)
    moved = pltpu.roll(tile(edge_ref, group), (cols - DEPTH * slot) % LANES, 1)
    return jnp.where(lanes_of(own.shape) < cols, own, moved)


def over_rows(values):
    return jnp.sum(values, axis=0, keepdims=True)


def whole(values):
    return jnp.sum(over_rows(values), axis=1, keepdims=True)


def coefficient_planes(coef, sources, levels, cols):
    coef[...] = jnp.zeros(coef.shape, jnp.float32)
    for level in range(levels):
        for kind, source in enumerate(sources):
            at = (kind * levels + level) * ROWS
            coef[at : at + ROWS, :cols] = source[level].astype(jnp.float32)


def project(out_z, at, totals, scale):
    for m, total in enumerate(totals):
        out_z[at + m : at + m + 1, : total.shape[1]] = scale * over_rows(total)


def start(planes, levels, cols, count):
    ens_scale = math.sqrt(ensemble_share / (count - 1))
    base = planes * ROWS
    edge_rows = -(-(planes + 3 * levels) // GROUP) * ROWS

    def kernel(*refs):
        sources, (out_z, out_e, coef), copies, weighted, sems = refs[:7], refs[7:10], refs[10:17], refs[17], refs[18]
        pairs = list(zip(sources[:6], copies[:6], strict=True))
        for part in range(FETCHES):
            rows = pl.ds(part * (count // FETCHES), count // FETCHES)
            pairs.append((sources[6].at[rows], copies[6].at[rows]))
        moves = [pltpu.make_async_copy(a, b, sems.at[i]) for i, (a, b) in enumerate(pairs)]
        for move in moves:
            move.start()
        innov, prec, scale, mask, kx, ky, members = copies
        out_z[...] = jnp.zeros(out_z.shape, jnp.float32)
        for move in moves[:6]:
            move.wait()
        coefficient_planes(coef, (kx, ky, mask), levels, cols)
        for plane in range(planes):
            weighted[plane] = mask[plane % levels].astype(jnp.float32) * (prec[plane] * innov[plane])
            out_z[plane * ROWS : (plane + 1) * ROWS, :cols] = scale[plane] * weighted[plane]
        edges = [tile(out_z, plane) for plane in range(planes)]
        pack_edges(out_e, edges + [tile(coef, index) for index in range(3 * levels)], cols)
        for move in moves[6:]:
            move.wait()
        totals = [jnp.zeros((ROWS, cols), jnp.float32) for _ in range(count)]
        for plane in range(planes):
            for m in range(count):
                totals[m] += members[m, plane] * weighted[plane]
        project(out_z, base, totals, ens_scale)
        out_e[edge_rows:, :] = out_z[base:, :]

    outs = [f32(base + ROWS, LANES), f32(edge_rows + ROWS, LANES), f32(3 * levels * ROWS, LANES)]
    field, flat = (planes, ROWS, cols), (levels, ROWS, cols)
    kept = [(field, jnp.float32)] * 3 + [(flat, jnp.int32)] + [(flat, jnp.float32)] * 2 + [((count,) + field, jnp.float32)]
    scratch = [pltpu.VMEM(*one) for one in kept] + [pltpu.VMEM(field, jnp.float32), pltpu.SemaphoreType.DMA((6 + FETCHES,))]
    return kernel, outs, scratch


def observe(planes, levels, cols, count, with_weights):
    ens_scale = math.sqrt(ensemble_share / (count - 1))
    base = planes * ROWS
    edge_rows = -(-planes // GROUP) * ROWS
    sums_at = base + ROWS * with_weights

    def kernel(*refs):
        own, other, weights, sums, vert, prec, scale, mask, members = refs[:9]
        if with_weights:
            out_z, out_e, seen = refs[9:]
        else:
            seen, out_z, out_e, now = refs[9:]
        out_z[...] = jnp.zeros(out_z.shape, jnp.float32)
        totals = [jnp.zeros((ROWS, cols), jnp.float32) for _ in range(count)]
        energy = jnp.zeros((ROWS, cols), jnp.float32)
        cross = jnp.zeros((ROWS, cols), jnp.float32)
        here = lax.axis_index("gz") * levels
        there = (1 - lax.axis_index("gz")) * levels
        for plane in range(planes):
            field, level = divmod(plane, levels)
            wet = mask[level].astype(jnp.float32)
            static = jnp.zeros((ROWS, cols), jnp.float32)
            for k in range(levels):
                row = (field * 2 * levels + here + level) * 2 * levels
                static += vert[pl.ds(row + here + k, 1), :cols] * tile(own, field * levels + k)[:, :cols]
                static += vert[pl.ds(row + there + k, 1), :cols] * tile(other, field * levels + k)[:, :cols]
            ensemble = jnp.zeros((ROWS, cols), jnp.float32)
            for m in range(count):
                ensemble += weights[m : m + 1, :cols] * members[m, plane]
            seen_now = wet * (SQRT_STATIC * (scale[plane] * static) + ens_scale * ensemble)
            weighted = wet * (prec[plane] * seen_now)
            if with_weights:
                seen[plane] = seen_now
                energy += seen_now * weighted
                for m in range(count):
                    totals[m] += members[m, plane] * weighted
            else:
                now[plane] = seen_now
                before = seen[plane]
                energy += before * (prec[plane] * before)
                cross += before * weighted
            out_z[plane * ROWS : (plane + 1) * ROWS, :cols] = scale[plane] * weighted
        if with_weights:
            project(out_z, base, totals, ens_scale)
        out_z[sums_at : sums_at + SUMS, :] = sums[...]
        if with_weights:
            out_z[sums_at : sums_at + 1, :cols] = over_rows(energy)
        else:
            energy, cross = whole(energy), whole(cross)
            share = jnp.where(energy > 0.0, -cross / jnp.where(energy > 0.0, energy, 1.0), 0.0)
            rest = jnp.zeros((ROWS, cols), jnp.float32)
            left = jnp.zeros((ROWS, cols), jnp.float32)
            for plane in range(planes):
                before = seen[plane]
                gap = now[plane] + share * before
                rest += gap * (prec[plane] * gap)
                left += before * (prec[plane] * gap)
            place = (lax.axis_index("gx") * 2 + lax.axis_index("gy")) * 2 + lax.axis_index("gz")
            own_lane = lanes_of((1, LANES)) == place
            for index, value in enumerate((whole(rest), whole(left), share, energy)):
                out_z[sums_at + index : sums_at + index + 1, :] = jnp.where(own_lane, value, 0.0)
        pack_edges(out_e, [tile(out_z, plane) for plane in range(planes)], cols)
        out_e[edge_rows:, :] = out_z[base:, :]

    tail = (ROWS * with_weights) + SUMS
    outs = [f32(base + tail, LANES), f32(edge_rows + tail, LANES)]
    if with_weights:
        return kernel, outs + [f32(planes, ROWS, cols)], ()
    return kernel, outs, [pltpu.VMEM((planes, ROWS, cols), jnp.float32)]


def mix_back(first, far, planes, levels, cols, tail):
    base = planes * ROWS
    coefs = 2 * levels if first else 0
    fields = planes // levels
    count = planes + coefs
    sent = -(-planes * KMAX // 8) * 8

    def kernel(*refs):
        if first:
            own, other, edge, edge_other, vert, raw, out_all, out_near = refs
        elif far:
            own, other, edge, edge_other, vert, out_all, out_near = refs
        else:
            own, other, edge, edge_other, vert, out_own, out_one, out_three, out_sums = refs
        here = lax.axis_index("gz") * levels
        there = (1 - lax.axis_index("gz")) * levels
        even = lax.rem(lax.axis_index("gx"), 2) == 0
        upper = lax.broadcasted_iota(jnp.int32, (8, LANES), 0) < 4

        def put(index, values):
            if far:
                out_all[index * ROWS : (index + 1) * ROWS, :] = values
                out_near[index * 8 : (index + 1) * 8, :] = jnp.where(upper, values[:8], values[8:])
            else:
                out_own[index * ROWS : (index + 1) * ROWS, :] = values
                head, end = values[:KMAX], values[ROWS - KMAX :]
                out_one[index * KMAX : (index + 1) * KMAX, :] = jnp.where(even, end, head)
                out_three[index * KMAX : (index + 1) * KMAX, :] = jnp.where(even, head, end)

        for field in range(fields):
            mine = [with_edge(tile(own, field * levels + l), edge, field * levels + l, cols) for l in range(levels)]
            theirs = [
                with_edge(tile(other, field * levels + l), edge_other, field * levels + l, cols) for l in range(levels)
            ]
            for k in range(levels):
                mixed = jnp.zeros((ROWS, LANES), jnp.float32)
                for l in range(levels):
                    block = field * 2 * levels
                    mixed += vert[pl.ds((block + here + l) * 2 * levels + here + k, 1), :] * mine[l]
                    mixed += vert[pl.ds((block + there + l) * 2 * levels + here + k, 1), :] * theirs[l]
                put(field * levels + k, mixed)
        packed = -(-(planes + (3 * levels if first else 0)) // GROUP) * ROWS
        total = (own[base:, :] + other[base:, :]) + (edge[packed:, :] + edge_other[packed:, :])
        if not far:
            out_sums[...] = total
            out_one[sent:, :] = total
            out_three[sent:, :] = total
            return
        at, near_at = count * ROWS, count * 8
        out_all[at : at + tail, :] = total
        out_near[near_at : near_at + tail, :] = total
        if first:
            last = jnp.where(lax.axis_index("gy") == 0, LANES - 1, cols - 1)
            lane = lanes_of((ROWS, LANES))
            bottom = lax.broadcasted_iota(jnp.int32, (ROWS, LANES), 0) == ROWS - 1
            wets = jnp.zeros((8, LANES), jnp.float32)
            for level in range(levels):
                kx, ky, wet = (
                    with_edge(tile(raw, kind * levels + level), edge, planes + kind * levels + level, cols) for kind in range(3)
                )
                put(planes + level, kx * wet * jnp.where(bottom, 1.0, pltpu.roll(wet, ROWS - 1, 0)))
                put(planes + levels + level, jnp.where(lane == last, 0.0, ky * wet * pltpu.roll(wet, LANES - 1, 1)))
                wets = jnp.where(lax.broadcasted_iota(jnp.int32, (8, LANES), 0) == level, wet[:1], wets)
            out_all[at + tail :, :] = wets
            out_near[near_at + tail :, :] = wets

    if not far:
        return kernel, [f32(base, LANES)] + [f32(sent + tail, LANES)] * 2 + [f32(tail, LANES)]
    tail_all = tail + (8 if first else 0)
    return kernel, [f32(count * ROWS + tail_all, LANES), f32(count * 8 + tail_all, LANES)]


def pass_on(*refs):
    half = len(refs) // 2
    for source, target in zip(refs[:half], refs[half:], strict=True):
        target[...] = source[...]


def is_even():
    return lax.rem(lax.axis_index("gx"), 2) == 0


def far_window(nat, index, own, first, near, third, slot):
    even = is_even()
    one, three = tile(first, slot), tile(third, slot)
    nat[index, 0:16, :] = tile(own, slot)
    nat[index, 16:32, :] = jnp.where(even, one, three)
    nat[index, 32:40, :] = tile(near, slot, 8)
    nat[index, 40:56, :] = jnp.where(even, three, one)


def shorten(nat, index):
    return jnp.concatenate([nat[index, 0:28, :], nat[index, 44:56, :]], axis=0)


def dealt(nat, index, tiles):
    return [nat[index, pl.ds(t, 8, stride=tiles), :] for t in range(tiles)]


def deal(buf, nat, index, tiles):
    for t, values in enumerate(dealt(nat, index, tiles)):
        buf[index, t * 8 : (t + 1) * 8, :] = values


def undeal(nat, buf, index, tiles):
    for t in range(tiles):
        nat[index, pl.ds(t, 8, stride=tiles), :] = buf[index, t * 8 : (t + 1) * 8, :]


def eight(ref, tiles, *index):
    return [ref[(*index, pl.ds(t * 8, 8), slice(None))] for t in range(tiles)]


def after(tiles):
    return tiles[1:] + [pltpu.roll(tiles[0], 7, 0)]


def run_steps(buf, spare, coef, steps, planes, levels, tiles):
    for number in range(KMAX):
        source, target = (buf, spare)[number % 2], (spare, buf)[number % 2]
        for level in range(levels):
            east, north, south = (eight(coef, tiles, kind, level) for kind in range(3))
            for field in range(planes // levels):
                plane = field * levels + level
                active = jnp.where(steps[field : field + 1, :] > float(number), 1.0, 0.0).astype(jnp.float32)
                u = eight(source, tiles, plane)
                flux_east = [c * (v - w) for c, v, w in zip(east, after(u), u, strict=True)]
                flux_west = [pltpu.roll(flux_east[-1], 1, 0)] + flux_east[:-1]
                for t in range(tiles):
                    to_north = north[t] * (pltpu.roll(u[t], LANES - 1, 1) - u[t])
                    to_south = south[t] * (pltpu.roll(u[t], 1, 1) - u[t])
                    change = (flux_east[t] - flux_west[t]) + (to_north + to_south)
                    target[plane, t * 8 : (t + 1) * 8, :] = u[t] + active * change


def own_sum(values, cols):
    return over_rows(jnp.where(lanes_of(values.shape) < cols, values, 0.0))


def spread(values):
    return jnp.broadcast_to(jnp.sum(values, axis=1, keepdims=True), values.shape)


def window_scratch(planes):
    return [pltpu.VMEM((planes, WIN, LANES), jnp.float32)] * 2


def diffuse_own(out_g, field, buf, nat, coef, steps, planes, levels):
    for plane in range(planes):
        for t, values in enumerate(dealt(field, plane, NEAR_TILES)):
            buf[plane, t * 8 : (t + 1) * 8, :] = values
    run_steps(buf, nat, coef, steps, planes, levels, NEAR_TILES)
    for plane in range(planes):
        undeal(nat, buf, plane, NEAR_TILES)
        out_g[plane * ROWS : (plane + 1) * ROWS, :] = nat[plane, :ROWS, :]


def first_diffuse(planes, levels, cols):
    coefs = 2 * levels

    def kernel(own, first, near, third, steps, coef, coef_near, resid, weights, sums, out_g, buf, nat):
        even = is_even()
        at, near_at = (planes + coefs) * ROWS, (planes + coefs) * 8
        for index in range(coefs):
            far_window(nat, index, own, first, near, third, planes + index)
            if index < levels:
                row, near_row = at + ROWS + index, near_at + ROWS + index
                one, three = first[row : row + 1, :], third[row : row + 1, :]
                nat[index, 15:16, :] = nat[index, 15:16, :] * jnp.where(even, one, three)
                nat[index, 31:32, :] = nat[index, 31:32, :] * near[near_row : near_row + 1, :]
                nat[index, 39:40, :] = nat[index, 39:40, :] * jnp.where(even, three, one)
                nat[index, 55:56, :] = nat[index, 55:56, :] * own[row : row + 1, :]
            buf[index, : 8 * NEAR_TILES, :] = shorten(nat, index)
            kind, level = divmod(index, levels)
            for target, window, tiles in ((coef, nat, TILES), (coef_near, buf, NEAR_TILES)):
                for t, values in enumerate(dealt(window, index, tiles)):
                    target[kind, level, t * 8 : (t + 1) * 8, :] = values
                    if kind == 1:
                        target[2, level, t * 8 : (t + 1) * 8, :] = pltpu.roll(values, 1, 1)
        for plane in range(planes):
            far_window(nat, plane, own, first, near, third, plane)
            deal(buf, nat, plane, TILES)
        sent = slice(at, at + ROWS)
        weights[...] = spread((own[sent, :] + first[sent, :]) + (near[near_at : near_at + ROWS, :] + third[sent, :]))
        run_steps(buf, nat, coef, steps, planes, levels, TILES)
        squares = jnp.zeros((ROWS, LANES), jnp.float32)
        for plane in range(planes):
            undeal(nat, buf, plane, TILES)
            value = SQRT_STATIC * shorten(nat, plane)
            resid[plane] = value
            squares += value[:ROWS] * value[:ROWS]
        sums[...] = jnp.zeros(sums.shape, jnp.float32)
        sums[4:5, :] = own_sum(squares, cols)
        diffuse_own(out_g, resid, buf, nat, coef_near, steps, planes, levels)

    outs = [
        f32(3, levels, WIN, LANES),
        f32(3, levels, 8 * NEAR_TILES, LANES),
        f32(planes, 8 * NEAR_TILES, LANES),
        f32(ROWS, LANES),
        f32(SUMS, LANES),
        f32(planes * ROWS, LANES),
    ]
    return kernel, outs, window_scratch(planes)


def second_diffuse(planes, levels, cols):
    def kernel(
        own, first, near, third, steps, coef, coef_near, resid, weights, image, new, new_w, sums, facts, out_g, buf, nat, field
    ):
        for plane in range(planes):
            far_window(nat, plane, own, first, near, third, plane)
            deal(buf, nat, plane, TILES)
        at, near_at = planes * ROWS, planes * 8
        total = spread((own[at:, :] + first[at:, :]) + (near[near_at:, :] + third[at:, :]))
        energy = total[ROWS : ROWS + 1]
        rr = total[ROWS + 4 : ROWS + 5] + over_rows(weights[...] * weights[...])
        step = rr / (rr + energy)
        new_w[...] = weights[...] - step * (weights[...] + total[:ROWS])
        facts[...] = jnp.zeros(facts.shape, jnp.float32)
        facts[0:1, :] = rr
        facts[1:2, :] = step
        run_steps(buf, nat, coef, steps, planes, levels, TILES)
        squares = jnp.zeros((ROWS, LANES), jnp.float32)
        cross = jnp.zeros((ROWS, LANES), jnp.float32)
        for plane in range(planes):
            undeal(nat, buf, plane, TILES)
            direction = resid[plane]
            image_now = direction + SQRT_STATIC * shorten(nat, plane)
            value = direction - step * image_now
            field[plane] = value
            image[plane] = image_now[:ROWS]
            new[plane] = value[:ROWS]
            squares += value[:ROWS] * value[:ROWS]
            cross += value[:ROWS] * direction[:ROWS]
        sums[...] = jnp.zeros(sums.shape, jnp.float32)
        sums[4:5, :] = own_sum(squares, cols)
        sums[5:6, :] = own_sum(cross, cols)
        diffuse_own(out_g, field, buf, nat, coef_near, steps, planes, levels)

    block = f32(planes, ROWS, LANES)
    outs = [block, block, f32(ROWS, LANES), f32(SUMS, LANES), f32(SUMS, LANES), f32(planes * ROWS, LANES)]
    return kernel, outs, window_scratch(planes) + [pltpu.VMEM((planes, 8 * NEAR_TILES, LANES), jnp.float32)]


def last_diffuse(planes, levels, cols):
    def kernel(
        own, one, three, sums, sums_two, steps, coef, resid, weights, image, new, new_w, facts,
        control, control_w, final, buf, nat,
    ):
        even = is_even()
        gap_rows = jnp.zeros((4, LANES), jnp.float32)
        for plane in range(planes):
            first, third = tile(one, plane, KMAX), tile(three, plane, KMAX)
            nat[plane, 0:16, :] = tile(own, plane)
            nat[plane, 16:26, :] = jnp.where(even, first, third)
            nat[plane, 26:30, :] = gap_rows
            nat[plane, 30:40, :] = jnp.where(even, third, first)
            deal(buf, nat, plane, NEAR_TILES)
        sent = one.shape[0] - SUMS
        lanes = (sums[...] + one[sent:, :]) + (sums_two[...] + three[sent:, :])
        total = spread(lanes)
        rr, step = facts[0:1, :], facts[1:2, :]
        new_rr = total[4:5] + over_rows(new_w[...] * new_w[...])
        cross_rr = total[5:6] + over_rows(new_w[...] * weights[...])
        ratio = new_rr / rr
        gap = ratio - lanes[2:3]
        energy = spread(lanes[0:1] + gap * (2.0 * lanes[1:2] + gap * lanes[3:4]))
        squares = new_rr + ratio * (2.0 * cross_rr + ratio * rr)
        new_step = new_rr / (squares + energy)
        combined = step * weights[...] + new_step * (new_w[...] + ratio * weights[...])
        diagonal = lax.broadcasted_iota(jnp.int32, combined.shape, 0) == lanes_of(combined.shape)
        control_w[...] = over_rows(jnp.where(diagonal, combined, 0.0))[:, :ROWS]
        run_steps(buf, nat, coef, steps, planes, levels, NEAR_TILES)
        for plane in range(planes):
            undeal(nat, buf, plane, NEAR_TILES)
            direction, value = resid[plane, :ROWS, :], new[plane]
            new_direction = value + ratio * direction
            new_image = (value + SQRT_STATIC * nat[plane, :ROWS, :]) + ratio * image[plane]
            control[plane] = (step * direction + new_step * new_direction)[:, :cols]
            final[plane] = (value - new_step * new_image)[:, :cols]

    outs = [f32(planes, ROWS, cols), f32(1, ROWS), f32(planes, ROWS, cols)]
    return kernel, outs, window_scratch(planes)


def moved_to(values, x, y, z):
    sizes = [lax.axis_size(axis) for axis in AXES]
    here = [(a, b, c) for a in range(sizes[0]) for b in range(sizes[1]) for c in range(sizes[2])]
    number = {place: index for index, place in enumerate(here)}
    return lax.ppermute(values, AXES, [(number[a, b, c], number[a ^ x, b ^ y, c ^ z]) for a, b, c in here])


def mix_round(kernel_of, out_z, out_e, vert, raw=None):
    other = moved_to(out_z, 0, 0, 1)
    edge = moved_to(out_e, 0, 1, 0)
    edge_other = moved_to(out_e, 0, 1, 1)
    kernel, outs = kernel_of
    args = (out_z, other, edge, edge_other, vert)
    if raw is not None:
        own, raw = call(pass_on, [f32(*out_z.shape), f32(*raw.shape)], [VMEM] * 2, (out_z, raw))
        args = (own, *args[1:], raw)
    return call(kernel, outs, [VMEM] * len(args), args)


def far_round(own, near):
    return own, moved_to(own, 1, 0, 0), moved_to(near, 2, 0, 0), moved_to(own, 3, 0, 0)


def shards_small(
    innovation, obs_precision, error_scale, kappa_x, kappa_y, sea_mask, members, vertical, diffusion_steps
):
    fields, levels, rows, cols = innovation.shape
    count = members.shape[0]
    planes = fields * levels
    block = (planes, rows, cols)
    innov, prec, scale = (a.reshape(block) for a in (innovation, obs_precision, error_scale))
    ens = members.reshape((count,) + block)
    vert = jnp.broadcast_to(vertical.reshape(-1, 1), (vertical.size, LANES))
    steps = jnp.broadcast_to(diffusion_steps.astype(jnp.float32)[:, None], (fields, LANES))

    kernel, outs, scratch = start(planes, levels, cols, count)
    args = (innov, prec, scale, sea_mask, kappa_x, kappa_y, ens)
    out_z, out_e, raw = call(kernel, outs, [HBM] * 7, args, scratch, 56)
    parts = far_round(*mix_round(mix_back(True, True, planes, levels, cols, ROWS), out_z, out_e, vert, raw))
    kernel, outs, scratch = first_diffuse(planes, levels, cols)
    coef, coef_near, resid, weights, sums, out_g = call(kernel, outs, [VMEM] * 5, (*parts, steps), scratch)

    kernel, outs, scratch = observe(planes, levels, cols, count, True)
    args = (out_g, moved_to(out_g, 0, 0, 1), weights, sums, vert, prec, scale, sea_mask, ens)
    out_z, out_e, seen = call(kernel, outs, [VMEM] * 9, args, scratch)
    parts = far_round(*mix_round(mix_back(False, True, planes, levels, cols, ROWS + SUMS), out_z, out_e, vert))
    kernel, outs, scratch = second_diffuse(planes, levels, cols)
    args = (*parts, steps, coef, coef_near, resid, weights)
    image, new, new_w, sums, facts, out_g = call(kernel, outs, [VMEM] * 9, args, scratch)

    kernel, outs, scratch = observe(planes, levels, cols, count, False)
    args = (out_g, moved_to(out_g, 0, 0, 1), new_w, sums, vert, prec, scale, sea_mask, ens, seen)
    out_z, out_e = call(kernel, outs, [VMEM] * 10, args, scratch)
    own, one, three, sums = mix_round(mix_back(False, False, planes, levels, cols, SUMS), out_z, out_e, vert)
    parts = (own, moved_to(one, 1, 0, 0), moved_to(three, 3, 0, 0), sums, moved_to(sums, 2, 0, 0))
    kernel, outs, scratch = last_diffuse(planes, levels, cols)
    args = (*parts, steps, coef_near, resid, weights, image, new, new_w, facts)
    control, control_w, final = call(kernel, outs, [VMEM] * 13, args, scratch)
    return control.reshape(innovation.shape), control_w.reshape(count), final.reshape(innovation.shape)


def shards(innovation, obs_precision, error_scale, kappa_x, kappa_y, sea_mask, members, vertical, diffusion_steps):
    arrays = (innovation, obs_precision, error_scale, kappa_x, kappa_y, sea_mask, members, vertical, diffusion_steps)
    sizes = tuple(lax.axis_size(axis) for axis in AXES)
    rows, cols = innovation.shape[2:]
    fits = rows == ROWS and members.shape[0] == ROWS and DEPTH <= cols <= LANES - DEPTH and ITERS == 2
    if sizes == (4, 2, 2) and fits:
        return shards_small(*arrays)
    return shards_any(*arrays)


def solution(mesh):
    placed = (
        P("grp", "gz", "gx", "gy"),
        P("grp", "gz", "gx", "gy"),
        P(None, "gz", "gx", "gy"),
        P("gz", "gx", "gy"),
        P("gz", "gx", "gy"),
        P("gz", "gx", "gy"),
        P("grp", None, "gz", "gx", "gy"),
        P(),
        P(),
    )
    return jax.shard_map(
        shards,
        mesh=mesh,
        in_specs=placed,
        out_specs=(P("grp", "gz", "gx", "gy"), P("grp"), P("grp", "gz", "gx", "gy")),
        check_vma=False,
    )
```

```python
import functools
import math


import jax
import jax.numpy as jnp
from jax import lax
from jax.experimental import pallas as pl
from jax.experimental.pallas import tpu as pltpu
from jax.sharding import PartitionSpec as P

KMAX = 10
ITERS = 2


static_share = 0.6
ensemble_share = 0.4


def extended(cells, sides, width):
    for axis, dim in sides:
        count = lax.axis_size(axis)
        head = lax.slice_in_dim(cells, 0, width, axis=dim)
        tail = lax.slice_in_dim(cells, cells.shape[dim] - width, cells.shape[dim], axis=dim)
        cells = jnp.concatenate(
            [
                lax.ppermute(tail, axis, [(i, (i + 1) % count) for i in range(count)]),
                cells,
                lax.ppermute(head, axis, [((i + 1) % count, i) for i in range(count)]),
            ],
            axis=dim,
        )
    return cells


def level_mix(source, mixing):
    local_levels = source.shape[1]
    gathered = lax.all_gather(source, "gz", axis=1, tiled=True)
    own_rows = lax.dynamic_slice_in_dim(
        mixing, lax.axis_index("gz") * local_levels, local_levels, 1
    )
    return jnp.einsum("flk,fkxy->flxy", own_rows, gathered, precision=lax.Precision.HIGHEST)


def diffuse(source, padded, step_counts, halo_depth):
    current = source
    for segment in range(KMAX // halo_depth):
        current = extended(current, (("gx", 2), ("gy", 3)), halo_depth)
        for substep in range(halo_depth):
            number = segment * halo_depth + substep
            offset = KMAX - halo_depth + substep
            rows_now = current.shape[2]
            cols_now = current.shape[3]
            window = padded[:, :, offset : offset + rows_now, offset : offset + cols_now]
            east_kappa = window[0]
            north_kappa = window[1]
            wet_window = window[2]
            east_coef = east_kappa[:, :-1, :] * wet_window[:, :-1, :] * wet_window[:, 1:, :]
            flux_east = east_coef * (current[:, :, 1:, :] - current[:, :, :-1, :])
            div_east = (flux_east[:, :, 1:, :] - flux_east[:, :, :-1, :])[:, :, :, 1:-1]
            north_coef = north_kappa[:, :, :-1] * wet_window[:, :, :-1] * wet_window[:, :, 1:]
            flux_north = north_coef * (current[:, :, :, 1:] - current[:, :, :, :-1])
            div_north = (flux_north[:, :, :, 1:] - flux_north[:, :, :, :-1])[:, :, 1:-1, :]
            active = (step_counts > number).astype(jnp.float32)[:, None, None, None]
            current = current[:, :, 1:-1, 1:-1] + active * (div_east + div_north)
    return current


def both_sums(terms, partial_value):
    return lax.psum((terms, partial_value), ("gx", "gy", "gz"))


def squares(resid_field):
    return lax.psum(jnp.sum(resid_field * resid_field), ("gx", "gy", "gz"))


def shards_any(
    innovation,
    obs_precision,
    error_scale,
    kappa_x,
    kappa_y,
    sea_mask,
    members,
    vertical,
    diffusion_steps,
):
    wet_cells = sea_mask.astype(jnp.float32)
    coefficients = jnp.stack([kappa_x, kappa_y, wet_cells])
    padded = extended(coefficients, (("gx", 2), ("gy", 3)), KMAX)
    cols_dev = wet_cells.shape[2]
    y_position = (
        lax.axis_index("gy") * cols_dev + jnp.arange(cols_dev + 2 * KMAX, dtype=jnp.int32) - KMAX
    )
    inside = ((y_position >= 0) & (y_position < cols_dev * lax.axis_size("gy"))).astype(jnp.float32)
    padded = jnp.stack([padded[0], padded[1], padded[2] * inside[None, None, :]])
    halo_depth = 2
    transposed = jnp.swapaxes(vertical, 1, 2)
    sqrt_static = math.sqrt(static_share)
    ens_scale = math.sqrt(ensemble_share / (members.shape[0] - 1))

    def static_back(masked):
        return sqrt_static * diffuse(
            level_mix(error_scale * masked, transposed), padded, diffusion_steps, halo_depth
        )

    def ensemble_terms(masked):
        return jnp.einsum("mflxy,flxy->m", members, masked, precision=lax.Precision.HIGHEST)

    masked = wet_cells * (obs_precision * innovation)
    resid_field = static_back(masked)
    ens_sum, field_norm = both_sums(ensemble_terms(masked), jnp.sum(resid_field * resid_field))
    resid_weights = ens_scale * ens_sum
    norm_now = field_norm + jnp.sum(resid_weights * resid_weights)
    dir_field, dir_weights = (resid_field, resid_weights)
    control_field = jnp.zeros_like(resid_field)
    control_weights = jnp.zeros(resid_weights.shape, jnp.float32)
    for iteration in range(ITERS):
        static = error_scale * level_mix(
            diffuse(dir_field, padded, diffusion_steps, halo_depth), vertical
        )
        ensemble = jnp.einsum(
            "m,mflxy->flxy", dir_weights, members, precision=lax.Precision.HIGHEST
        )
        observed = wet_cells * (sqrt_static * static + ens_scale * ensemble)
        weighted = obs_precision * observed
        masked = wet_cells * weighted
        image_field = dir_field + static_back(masked)
        ens_sum, curve_part = both_sums(ensemble_terms(masked), jnp.sum(dir_field * image_field))
        image_weights = dir_weights + ens_scale * ens_sum
        curvature = curve_part + jnp.sum(dir_weights * image_weights)
        step_length = norm_now / curvature
        control_field = control_field + step_length * dir_field
        control_weights = control_weights + step_length * dir_weights
        resid_field = resid_field - step_length * image_field
        resid_weights = resid_weights - step_length * image_weights
        if iteration + 1 < ITERS:
            norm_next = squares(resid_field) + jnp.sum(resid_weights * resid_weights)
            ratio_next = norm_next / norm_now
            dir_field = resid_field + ratio_next * dir_field
            dir_weights = resid_weights + ratio_next * dir_weights
            norm_now = norm_next
    return (control_field, control_weights, resid_field)

ROWS = 16
WIN = 56
TILES = WIN // 8
NEAR_TILES = 5
LANES = 128
DEPTH = 2 * KMAX
GROUP = LANES // DEPTH
SUMS = 8
FETCHES = 4
AXES = ("gx", "gy", "gz")
VMEM = pl.BlockSpec(memory_space=pltpu.VMEM)
HBM = pl.BlockSpec(memory_space=pltpu.HBM)
SQRT_STATIC = math.sqrt(static_share)


def f32(*shape):
    return jax.ShapeDtypeStruct(shape, jnp.float32)


def call(kernel, outs, specs, args, scratch=(), grant=32):
    return pl.pallas_call(
        kernel,
        out_shape=outs,
        in_specs=specs,
        out_specs=[VMEM] * len(outs),
        scratch_shapes=list(scratch),
        compiler_params=pltpu.CompilerParams(vmem_limit_bytes=grant * 1024 * 1024),
    )(*args)


def lanes_of(shape):
    return lax.broadcasted_iota(jnp.int32, shape, len(shape) - 1)


def tile(ref, index, size=ROWS):
    return ref[index * size : (index + 1) * size, :]


def pack_edges(out_ref, planes, cols):
    first = jnp.where(lax.axis_index("gy") == 0, cols - DEPTH, 0)
    lane = lanes_of((ROWS, LANES))
    for group in range(-(-len(planes) // GROUP)):
        packed = jnp.zeros((ROWS, LANES), jnp.float32)
        for slot, plane in enumerate(planes[group * GROUP : (group + 1) * GROUP]):
            moved = pltpu.roll(plane, lax.rem(DEPTH * slot - first + LANES, LANES), 1)
            packed = jnp.where((lane >= DEPTH * slot) & (lane < DEPTH * (slot + 1)), moved, packed)
        out_ref[group * ROWS : (group + 1) * ROWS, :] = packed


def with_edge(own, edge_ref, index, cols):
    group, slot = divmod(index, GROUP)
    moved = pltpu.roll(tile(edge_ref, group), (cols - DEPTH * slot) % LANES, 1)
    return jnp.where(lanes_of(own.shape) < cols, own, moved)


def over_rows(values):
    return jnp.sum(values, axis=0, keepdims=True)


def whole(values):
    return jnp.sum(over_rows(values), axis=1, keepdims=True)


def coefficient_planes(coef, sources, levels, cols):
    coef[...] = jnp.zeros(coef.shape, jnp.float32)
    for level in range(levels):
        for kind, source in enumerate(sources):
            at = (kind * levels + level) * ROWS
            coef[at : at + ROWS, :cols] = source[level].astype(jnp.float32)


def project(out_z, at, totals, scale):
    for m, total in enumerate(totals):
        out_z[at + m : at + m + 1, : total.shape[1]] = scale * over_rows(total)


def start(planes, levels, cols, count):
    ens_scale = math.sqrt(ensemble_share / (count - 1))
    base = planes * ROWS
    edge_rows = -(-(planes + 3 * levels) // GROUP) * ROWS

    def kernel(*refs):
        sources, (out_z, out_e, coef), copies, weighted, sems = refs[:7], refs[7:10], refs[10:17], refs[17], refs[18]
        pairs = list(zip(sources[:6], copies[:6], strict=True))
        for part in range(FETCHES):
            rows = pl.ds(part * (count // FETCHES), count // FETCHES)
            pairs.append((sources[6].at[rows], copies[6].at[rows]))
        moves = [pltpu.make_async_copy(a, b, sems.at[i]) for i, (a, b) in enumerate(pairs)]
        for move in moves:
            move.start()
        innov, prec, scale, mask, kx, ky, members = copies
        out_z[...] = jnp.zeros(out_z.shape, jnp.float32)
        for move in moves[:6]:
            move.wait()
        coefficient_planes(coef, (kx, ky, mask), levels, cols)
        for plane in range(planes):
            weighted[plane] = mask[plane % levels].astype(jnp.float32) * (prec[plane] * innov[plane])
            out_z[plane * ROWS : (plane + 1) * ROWS, :cols] = scale[plane] * weighted[plane]
        edges = [tile(out_z, plane) for plane in range(planes)]
        pack_edges(out_e, edges + [tile(coef, index) for index in range(3 * levels)], cols)
        each = count // FETCHES
        for part in range(FETCHES):
            moves[6 + part].wait()
            totals = [jnp.zeros((ROWS, cols), jnp.float32) for _ in range(each)]
            for plane in range(planes):
                for m in range(each):
                    totals[m] += members[part * each + m, plane] * weighted[plane]
            project(out_z, base + part * each, totals, ens_scale)
        out_e[edge_rows:, :] = out_z[base:, :]

    outs = [f32(base + ROWS, LANES), f32(edge_rows + ROWS, LANES), f32(3 * levels * ROWS, LANES)]
    field, flat = (planes, ROWS, cols), (levels, ROWS, cols)
    kept = [(field, jnp.float32)] * 3 + [(flat, jnp.int32)] + [(flat, jnp.float32)] * 2 + [((count,) + field, jnp.float32)]
    scratch = [pltpu.VMEM(*one) for one in kept] + [pltpu.VMEM(field, jnp.float32), pltpu.SemaphoreType.DMA((6 + FETCHES,))]
    return kernel, outs, scratch


def observe(planes, levels, cols, count, with_weights):
    ens_scale = math.sqrt(ensemble_share / (count - 1))
    base = planes * ROWS
    edge_rows = -(-planes // GROUP) * ROWS
    sums_at = base + ROWS * with_weights

    def kernel(*refs):
        own, other, weights, sums, vert, prec, scale, mask, members = refs[:9]
        if with_weights:
            out_z, out_e, seen = refs[9:]
        else:
            seen, out_z, out_e, now = refs[9:]
        out_z[...] = jnp.zeros(out_z.shape, jnp.float32)
        totals = [jnp.zeros((ROWS, cols), jnp.float32) for _ in range(count)]
        energy = jnp.zeros((ROWS, cols), jnp.float32)
        cross = jnp.zeros((ROWS, cols), jnp.float32)
        here = lax.axis_index("gz") * levels
        there = (1 - lax.axis_index("gz")) * levels
        for plane in range(planes):
            field, level = divmod(plane, levels)
            wet = mask[level].astype(jnp.float32)
            static = jnp.zeros((ROWS, cols), jnp.float32)
            for k in range(levels):
                row = (field * 2 * levels + here + level) * 2 * levels
                static += vert[pl.ds(row + here + k, 1), :cols] * tile(own, field * levels + k)[:, :cols]
                static += vert[pl.ds(row + there + k, 1), :cols] * tile(other, field * levels + k)[:, :cols]
            ensemble = jnp.zeros((ROWS, cols), jnp.float32)
            for m in range(count):
                ensemble += weights[m : m + 1, :cols] * members[m, plane]
            seen_now = wet * (SQRT_STATIC * (scale[plane] * static) + ens_scale * ensemble)
            weighted = wet * (prec[plane] * seen_now)
            if with_weights:
                seen[plane] = seen_now
                energy += seen_now * weighted
                for m in range(count):
                    totals[m] += members[m, plane] * weighted
            else:
                now[plane] = seen_now
                before = seen[plane]
                energy += before * (prec[plane] * before)
                cross += before * weighted
            out_z[plane * ROWS : (plane + 1) * ROWS, :cols] = scale[plane] * weighted
        if with_weights:
            project(out_z, base, totals, ens_scale)
        out_z[sums_at : sums_at + SUMS, :] = sums[...]
        if with_weights:
            out_z[sums_at : sums_at + 1, :cols] = over_rows(energy)
        else:
            energy, cross = whole(energy), whole(cross)
            share = jnp.where(energy > 0.0, -cross / jnp.where(energy > 0.0, energy, 1.0), 0.0)
            rest = jnp.zeros((ROWS, cols), jnp.float32)
            left = jnp.zeros((ROWS, cols), jnp.float32)
            for plane in range(planes):
                before = seen[plane]
                gap = now[plane] + share * before
                rest += gap * (prec[plane] * gap)
                left += before * (prec[plane] * gap)
            place = (lax.axis_index("gx") * 2 + lax.axis_index("gy")) * 2 + lax.axis_index("gz")
            own_lane = lanes_of((1, LANES)) == place
            for index, value in enumerate((whole(rest), whole(left), share, energy)):
                out_z[sums_at + index : sums_at + index + 1, :] = jnp.where(own_lane, value, 0.0)
        pack_edges(out_e, [tile(out_z, plane) for plane in range(planes)], cols)
        out_e[edge_rows:, :] = out_z[base:, :]

    tail = (ROWS * with_weights) + SUMS
    outs = [f32(base + tail, LANES), f32(edge_rows + tail, LANES)]
    if with_weights:
        return kernel, outs + [f32(planes, ROWS, cols)], ()
    return kernel, outs, [pltpu.VMEM((planes, ROWS, cols), jnp.float32)]


def mix_back(first, far, planes, levels, cols, tail):
    base = planes * ROWS
    coefs = 2 * levels if first else 0
    fields = planes // levels
    count = planes + coefs
    sent = -(-planes * KMAX // 8) * 8

    def kernel(*refs):
        if first:
            own, other, edge, edge_other, vert, raw, out_all, out_near = refs
        elif far:
            own, other, edge, edge_other, vert, out_all, out_near = refs
        else:
            own, other, edge, edge_other, vert, out_own, out_one, out_three, out_sums = refs
        here = lax.axis_index("gz") * levels
        there = (1 - lax.axis_index("gz")) * levels
        even = lax.rem(lax.axis_index("gx"), 2) == 0
        upper = lax.broadcasted_iota(jnp.int32, (8, LANES), 0) < 4

        def put(index, values):
            if far:
                out_all[index * ROWS : (index + 1) * ROWS, :] = values
                out_near[index * 8 : (index + 1) * 8, :] = jnp.where(upper, values[:8], values[8:])
            else:
                out_own[index * ROWS : (index + 1) * ROWS, :] = values
                head, end = values[:KMAX], values[ROWS - KMAX :]
                out_one[index * KMAX : (index + 1) * KMAX, :] = jnp.where(even, end, head)
                out_three[index * KMAX : (index + 1) * KMAX, :] = jnp.where(even, head, end)

        for field in range(fields):
            mine = [with_edge(tile(own, field * levels + l), edge, field * levels + l, cols) for l in range(levels)]
            theirs = [
                with_edge(tile(other, field * levels + l), edge_other, field * levels + l, cols) for l in range(levels)
            ]
            for k in range(levels):
                mixed = jnp.zeros((ROWS, LANES), jnp.float32)
                for l in range(levels):
                    block = field * 2 * levels
                    mixed += vert[pl.ds((block + here + l) * 2 * levels + here + k, 1), :] * mine[l]
                    mixed += vert[pl.ds((block + there + l) * 2 * levels + here + k, 1), :] * theirs[l]
                put(field * levels + k, mixed)
        packed = -(-(planes + (3 * levels if first else 0)) // GROUP) * ROWS
        total = (own[base:, :] + other[base:, :]) + (edge[packed:, :] + edge_other[packed:, :])
        if not far:
            out_sums[...] = total
            out_one[sent:, :] = total
            out_three[sent:, :] = total
            return
        at, near_at = count * ROWS, count * 8
        out_all[at : at + tail, :] = total
        out_near[near_at : near_at + tail, :] = total
        if first:
            last = jnp.where(lax.axis_index("gy") == 0, LANES - 1, cols - 1)
            lane = lanes_of((ROWS, LANES))
            bottom = lax.broadcasted_iota(jnp.int32, (ROWS, LANES), 0) == ROWS - 1
            wets = jnp.zeros((8, LANES), jnp.float32)
            for level in range(levels):
                kx, ky, wet = (
                    with_edge(tile(raw, kind * levels + level), edge, planes + kind * levels + level, cols) for kind in range(3)
                )
                put(planes + level, kx * wet * jnp.where(bottom, 1.0, pltpu.roll(wet, ROWS - 1, 0)))
                put(planes + levels + level, jnp.where(lane == last, 0.0, ky * wet * pltpu.roll(wet, LANES - 1, 1)))
                wets = jnp.where(lax.broadcasted_iota(jnp.int32, (8, LANES), 0) == level, wet[:1], wets)
            out_all[at + tail :, :] = wets
            out_near[near_at + tail :, :] = wets

    if not far:
        return kernel, [f32(base, LANES)] + [f32(sent + tail, LANES)] * 2 + [f32(tail, LANES)]
    tail_all = tail + (8 if first else 0)
    return kernel, [f32(count * ROWS + tail_all, LANES), f32(count * 8 + tail_all, LANES)]


def pass_on(*refs):
    half = len(refs) // 2
    for source, target in zip(refs[:half], refs[half:], strict=True):
        target[...] = source[...]


def is_even():
    return lax.rem(lax.axis_index("gx"), 2) == 0


def far_window(nat, index, own, first, near, third, slot):
    even = is_even()
    one, three = tile(first, slot), tile(third, slot)
    nat[index, 0:16, :] = tile(own, slot)
    nat[index, 16:32, :] = jnp.where(even, one, three)
    nat[index, 32:40, :] = tile(near, slot, 8)
    nat[index, 40:56, :] = jnp.where(even, three, one)


def shorten(nat, index):
    return jnp.concatenate([nat[index, 0:28, :], nat[index, 44:56, :]], axis=0)


def dealt(nat, index, tiles):
    return [nat[index, pl.ds(t, 8, stride=tiles), :] for t in range(tiles)]


def deal(buf, nat, index, tiles):
    for t, values in enumerate(dealt(nat, index, tiles)):
        buf[index, t * 8 : (t + 1) * 8, :] = values


def undeal(nat, buf, index, tiles):
    for t in range(tiles):
        nat[index, pl.ds(t, 8, stride=tiles), :] = buf[index, t * 8 : (t + 1) * 8, :]


def eight(ref, tiles, *index):
    return [ref[(*index, pl.ds(t * 8, 8), slice(None))] for t in range(tiles)]


def after(tiles):
    return tiles[1:] + [pltpu.roll(tiles[0], 7, 0)]


def run_steps(buf, spare, coef, steps, planes, levels, tiles):
    for number in range(KMAX):
        source, target = (buf, spare)[number % 2], (spare, buf)[number % 2]
        for level in range(levels):
            east, north, south = (eight(coef, tiles, kind, level) for kind in range(3))
            for field in range(planes // levels):
                plane = field * levels + level
                active = jnp.where(steps[field : field + 1, :] > float(number), 1.0, 0.0).astype(jnp.float32)
                u = eight(source, tiles, plane)
                flux_east = [c * (v - w) for c, v, w in zip(east, after(u), u, strict=True)]
                flux_west = [pltpu.roll(flux_east[-1], 1, 0)] + flux_east[:-1]
                for t in range(tiles):
                    to_north = north[t] * (pltpu.roll(u[t], LANES - 1, 1) - u[t])
                    to_south = south[t] * (pltpu.roll(u[t], 1, 1) - u[t])
                    change = (flux_east[t] - flux_west[t]) + (to_north + to_south)
                    target[plane, t * 8 : (t + 1) * 8, :] = u[t] + active * change


def own_sum(values, cols):
    return over_rows(jnp.where(lanes_of(values.shape) < cols, values, 0.0))


def spread(values):
    return jnp.broadcast_to(jnp.sum(values, axis=1, keepdims=True), values.shape)


def window_scratch(planes):
    return [pltpu.VMEM((planes, WIN, LANES), jnp.float32)] * 2


def diffuse_own(out_g, field, buf, nat, coef, steps, planes, levels):
    for plane in range(planes):
        for t, values in enumerate(dealt(field, plane, NEAR_TILES)):
            buf[plane, t * 8 : (t + 1) * 8, :] = values
    run_steps(buf, nat, coef, steps, planes, levels, NEAR_TILES)
    for plane in range(planes):
        undeal(nat, buf, plane, NEAR_TILES)
        out_g[plane * ROWS : (plane + 1) * ROWS, :] = nat[plane, :ROWS, :]


def first_diffuse(planes, levels, cols):
    coefs = 2 * levels

    def kernel(own, first, near, third, steps, coef, coef_near, resid, weights, sums, out_g, buf, nat):
        even = is_even()
        at, near_at = (planes + coefs) * ROWS, (planes + coefs) * 8
        for index in range(coefs):
            far_window(nat, index, own, first, near, third, planes + index)
            if index < levels:
                row, near_row = at + ROWS + index, near_at + ROWS + index
                one, three = first[row : row + 1, :], third[row : row + 1, :]
                nat[index, 15:16, :] = nat[index, 15:16, :] * jnp.where(even, one, three)
                nat[index, 31:32, :] = nat[index, 31:32, :] * near[near_row : near_row + 1, :]
                nat[index, 39:40, :] = nat[index, 39:40, :] * jnp.where(even, three, one)
                nat[index, 55:56, :] = nat[index, 55:56, :] * own[row : row + 1, :]
            buf[index, : 8 * NEAR_TILES, :] = shorten(nat, index)
            kind, level = divmod(index, levels)
            for target, window, tiles in ((coef, nat, TILES), (coef_near, buf, NEAR_TILES)):
                for t, values in enumerate(dealt(window, index, tiles)):
                    target[kind, level, t * 8 : (t + 1) * 8, :] = values
                    if kind == 1:
                        target[2, level, t * 8 : (t + 1) * 8, :] = pltpu.roll(values, 1, 1)
        for plane in range(planes):
            far_window(nat, plane, own, first, near, third, plane)
            deal(buf, nat, plane, TILES)
        sent = slice(at, at + ROWS)
        weights[...] = spread((own[sent, :] + first[sent, :]) + (near[near_at : near_at + ROWS, :] + third[sent, :]))
        run_steps(buf, nat, coef, steps, planes, levels, TILES)
        squares = jnp.zeros((ROWS, LANES), jnp.float32)
        for plane in range(planes):
            undeal(nat, buf, plane, TILES)
            value = SQRT_STATIC * shorten(nat, plane)
            resid[plane] = value
            squares += value[:ROWS] * value[:ROWS]
        sums[...] = jnp.zeros(sums.shape, jnp.float32)
        sums[4:5, :] = own_sum(squares, cols)
        diffuse_own(out_g, resid, buf, nat, coef_near, steps, planes, levels)

    outs = [
        f32(3, levels, WIN, LANES),
        f32(3, levels, 8 * NEAR_TILES, LANES),
        f32(planes, 8 * NEAR_TILES, LANES),
        f32(ROWS, LANES),
        f32(SUMS, LANES),
        f32(planes * ROWS, LANES),
    ]
    return kernel, outs, window_scratch(planes)


def second_diffuse(planes, levels, cols):
    def kernel(
        own, first, near, third, steps, coef, coef_near, resid, weights, image, new, new_w, sums, facts, out_g, buf, nat, field
    ):
        for plane in range(planes):
            far_window(nat, plane, own, first, near, third, plane)
            deal(buf, nat, plane, TILES)
        at, near_at = planes * ROWS, planes * 8
        total = spread((own[at:, :] + first[at:, :]) + (near[near_at:, :] + third[at:, :]))
        energy = total[ROWS : ROWS + 1]
        rr = total[ROWS + 4 : ROWS + 5] + over_rows(weights[...] * weights[...])
        step = rr / (rr + energy)
        new_w[...] = weights[...] - step * (weights[...] + total[:ROWS])
        facts[...] = jnp.zeros(facts.shape, jnp.float32)
        facts[0:1, :] = rr
        facts[1:2, :] = step
        run_steps(buf, nat, coef, steps, planes, levels, TILES)
        squares = jnp.zeros((ROWS, LANES), jnp.float32)
        cross = jnp.zeros((ROWS, LANES), jnp.float32)
        for plane in range(planes):
            undeal(nat, buf, plane, TILES)
            direction = resid[plane]
            image_now = direction + SQRT_STATIC * shorten(nat, plane)
            value = direction - step * image_now
            field[plane] = value
            image[plane] = image_now[:ROWS]
            new[plane] = value[:ROWS]
            squares += value[:ROWS] * value[:ROWS]
            cross += value[:ROWS] * direction[:ROWS]
        sums[...] = jnp.zeros(sums.shape, jnp.float32)
        sums[4:5, :] = own_sum(squares, cols)
        sums[5:6, :] = own_sum(cross, cols)
        diffuse_own(out_g, field, buf, nat, coef_near, steps, planes, levels)

    block = f32(planes, ROWS, LANES)
    outs = [block, block, f32(ROWS, LANES), f32(SUMS, LANES), f32(SUMS, LANES), f32(planes * ROWS, LANES)]
    return kernel, outs, window_scratch(planes) + [pltpu.VMEM((planes, 8 * NEAR_TILES, LANES), jnp.float32)]


def last_diffuse(planes, levels, cols):
    def kernel(own, one, three, sums, steps, coef, out_g, out_sums, buf, nat):
        even = is_even()
        gap_rows = jnp.zeros((4, LANES), jnp.float32)
        for plane in range(planes):
            first, third = tile(one, plane, KMAX), tile(three, plane, KMAX)
            nat[plane, 0:16, :] = tile(own, plane)
            nat[plane, 16:26, :] = jnp.where(even, first, third)
            nat[plane, 26:30, :] = gap_rows
            nat[plane, 30:40, :] = jnp.where(even, third, first)
            deal(buf, nat, plane, NEAR_TILES)
        sent = one.shape[0] - SUMS
        out_sums[0] = sums[...] + one[sent:, :]
        out_sums[1] = three[sent:, :]
        run_steps(buf, nat, coef, steps, planes, levels, NEAR_TILES)
        for plane in range(planes):
            undeal(nat, buf, plane, NEAR_TILES)
            out_g[plane] = nat[plane, :ROWS, :]

    return kernel, [f32(planes, ROWS, LANES), f32(2, SUMS, LANES)], window_scratch(planes)


def finish(planes, cols):
    def kernel(diffused, sums, sums_two, resid, weights, image, new, new_w, facts, control, control_w, final):
        lanes = sums[0] + (sums_two[...] + sums[1])
        total = spread(lanes)
        rr, step = facts[0:1, :], facts[1:2, :]
        new_rr = total[4:5] + over_rows(new_w[...] * new_w[...])
        cross_rr = total[5:6] + over_rows(new_w[...] * weights[...])
        ratio = new_rr / rr
        gap = ratio - lanes[2:3]
        energy = spread(lanes[0:1] + gap * (2.0 * lanes[1:2] + gap * lanes[3:4]))
        squares = new_rr + ratio * (2.0 * cross_rr + ratio * rr)
        new_step = new_rr / (squares + energy)
        combined = step * weights[...] + new_step * (new_w[...] + ratio * weights[...])
        diagonal = lax.broadcasted_iota(jnp.int32, combined.shape, 0) == lanes_of(combined.shape)
        control_w[...] = over_rows(jnp.where(diagonal, combined, 0.0))[:, :ROWS]
        for plane in range(planes):
            direction, value = resid[plane, :ROWS, :], new[plane]
            new_direction = value + ratio * direction
            new_image = (value + SQRT_STATIC * diffused[plane]) + ratio * image[plane]
            control[plane] = (step * direction + new_step * new_direction)[:, :cols]
            final[plane] = (value - new_step * new_image)[:, :cols]

    return kernel, [f32(planes, ROWS, cols), f32(1, ROWS), f32(planes, ROWS, cols)]


def moved_to(values, x, y, z):
    sizes = [lax.axis_size(axis) for axis in AXES]
    here = [(a, b, c) for a in range(sizes[0]) for b in range(sizes[1]) for c in range(sizes[2])]
    number = {place: index for index, place in enumerate(here)}
    return lax.ppermute(values, AXES, [(number[a, b, c], number[a ^ x, b ^ y, c ^ z]) for a, b, c in here])


def mix_round(kernel_of, out_z, out_e, vert, raw=None):
    other = moved_to(out_z, 0, 0, 1)
    edge = moved_to(out_e, 0, 1, 0)
    edge_other = moved_to(out_e, 0, 1, 1)
    kernel, outs = kernel_of
    args = (out_z, other, edge, edge_other, vert)
    if raw is not None:
        own, raw = call(pass_on, [f32(*out_z.shape), f32(*raw.shape)], [VMEM] * 2, (out_z, raw))
        args = (own, *args[1:], raw)
    return call(kernel, outs, [VMEM] * len(args), args)


def far_round(own, near):
    return own, moved_to(own, 1, 0, 0), moved_to(near, 2, 0, 0), moved_to(own, 3, 0, 0)


def shards_small(
    innovation, obs_precision, error_scale, kappa_x, kappa_y, sea_mask, members, vertical, diffusion_steps
):
    fields, levels, rows, cols = innovation.shape
    count = members.shape[0]
    planes = fields * levels
    block = (planes, rows, cols)
    innov, prec, scale = (a.reshape(block) for a in (innovation, obs_precision, error_scale))
    ens = members.reshape((count,) + block)
    vert = jnp.broadcast_to(vertical.reshape(-1, 1), (vertical.size, LANES))
    steps = jnp.broadcast_to(diffusion_steps.astype(jnp.float32)[:, None], (fields, LANES))

    kernel, outs, scratch = start(planes, levels, cols, count)
    args = (innov, prec, scale, sea_mask, kappa_x, kappa_y, ens)
    out_z, out_e, raw = call(kernel, outs, [HBM] * 7, args, scratch, 56)
    parts = far_round(*mix_round(mix_back(True, True, planes, levels, cols, ROWS), out_z, out_e, vert, raw))
    kernel, outs, scratch = first_diffuse(planes, levels, cols)
    coef, coef_near, resid, weights, sums, out_g = call(kernel, outs, [VMEM] * 5, (*parts, steps), scratch)

    kernel, outs, scratch = observe(planes, levels, cols, count, True)
    args = (out_g, moved_to(out_g, 0, 0, 1), weights, sums, vert, prec, scale, sea_mask, ens)
    out_z, out_e, seen = call(kernel, outs, [VMEM] * 9, args, scratch)
    parts = far_round(*mix_round(mix_back(False, True, planes, levels, cols, ROWS + SUMS), out_z, out_e, vert))
    kernel, outs, scratch = second_diffuse(planes, levels, cols)
    args = (*parts, steps, coef, coef_near, resid, weights)
    image, new, new_w, sums, facts, out_g = call(kernel, outs, [VMEM] * 9, args, scratch)

    kernel, outs, scratch = observe(planes, levels, cols, count, False)
    args = (out_g, moved_to(out_g, 0, 0, 1), new_w, sums, vert, prec, scale, sea_mask, ens, seen)
    out_z, out_e = call(kernel, outs, [VMEM] * 10, args, scratch)
    own, one, three, sums = mix_round(mix_back(False, False, planes, levels, cols, SUMS), out_z, out_e, vert)
    sums_two = moved_to(sums, 2, 0, 0)
    kernel, outs, scratch = last_diffuse(planes, levels, cols)
    args = (own, moved_to(one, 1, 0, 0), moved_to(three, 3, 0, 0), sums, steps, coef_near)
    diffused, sums = call(kernel, outs, [VMEM] * 6, args, scratch)
    kernel, outs = finish(planes, cols)
    args = (diffused, sums, sums_two, resid, weights, image, new, new_w, facts)
    control, control_w, final = call(kernel, outs, [VMEM] * 9, args)
    return control.reshape(innovation.shape), control_w.reshape(count), final.reshape(innovation.shape)


def shards(innovation, obs_precision, error_scale, kappa_x, kappa_y, sea_mask, members, vertical, diffusion_steps):
    arrays = (innovation, obs_precision, error_scale, kappa_x, kappa_y, sea_mask, members, vertical, diffusion_steps)
    sizes = tuple(lax.axis_size(axis) for axis in AXES)
    rows, cols = innovation.shape[2:]
    fits = rows == ROWS and members.shape[0] == ROWS and DEPTH <= cols <= LANES - DEPTH and ITERS == 2
    if sizes == (4, 2, 2) and fits:
        return shards_small(*arrays)
    return shards_any(*arrays)


def solution(mesh):
    placed = (
        P("grp", "gz", "gx", "gy"),
        P("grp", "gz", "gx", "gy"),
        P(None, "gz", "gx", "gy"),
        P("gz", "gx", "gy"),
        P("gz", "gx", "gy"),
        P("gz", "gx", "gy"),
        P("grp", None, "gz", "gx", "gy"),
        P(),
        P(),
    )
    return jax.shard_map(
        shards,
        mesh=mesh,
        in_specs=placed,
        out_specs=(P("grp", "gz", "gx", "gy"), P("grp"), P("grp", "gz", "gx", "gy")),
        check_vma=False,
    )
```

```python
import functools
import math


import jax
import jax.numpy as jnp
from jax import lax
from jax.experimental import pallas as pl
from jax.experimental.pallas import tpu as pltpu
from jax.sharding import PartitionSpec as P

KMAX = 10
ITERS = 2


static_share = 0.6
ensemble_share = 0.4


def extended(cells, sides, width):
    for axis, dim in sides:
        count = lax.axis_size(axis)
        head = lax.slice_in_dim(cells, 0, width, axis=dim)
        tail = lax.slice_in_dim(cells, cells.shape[dim] - width, cells.shape[dim], axis=dim)
        cells = jnp.concatenate(
            [
                lax.ppermute(tail, axis, [(i, (i + 1) % count) for i in range(count)]),
                cells,
                lax.ppermute(head, axis, [((i + 1) % count, i) for i in range(count)]),
            ],
            axis=dim,
        )
    return cells


def level_mix(source, mixing):
    local_levels = source.shape[1]
    gathered = lax.all_gather(source, "gz", axis=1, tiled=True)
    own_rows = lax.dynamic_slice_in_dim(
        mixing, lax.axis_index("gz") * local_levels, local_levels, 1
    )
    return jnp.einsum("flk,fkxy->flxy", own_rows, gathered, precision=lax.Precision.HIGHEST)


def diffuse(source, padded, step_counts, halo_depth):
    current = source
    for segment in range(KMAX // halo_depth):
        current = extended(current, (("gx", 2), ("gy", 3)), halo_depth)
        for substep in range(halo_depth):
            number = segment * halo_depth + substep
            offset = KMAX - halo_depth + substep
            rows_now = current.shape[2]
            cols_now = current.shape[3]
            window = padded[:, :, offset : offset + rows_now, offset : offset + cols_now]
            east_kappa = window[0]
            north_kappa = window[1]
            wet_window = window[2]
            east_coef = east_kappa[:, :-1, :] * wet_window[:, :-1, :] * wet_window[:, 1:, :]
            flux_east = east_coef * (current[:, :, 1:, :] - current[:, :, :-1, :])
            div_east = (flux_east[:, :, 1:, :] - flux_east[:, :, :-1, :])[:, :, :, 1:-1]
            north_coef = north_kappa[:, :, :-1] * wet_window[:, :, :-1] * wet_window[:, :, 1:]
            flux_north = north_coef * (current[:, :, :, 1:] - current[:, :, :, :-1])
            div_north = (flux_north[:, :, :, 1:] - flux_north[:, :, :, :-1])[:, :, 1:-1, :]
            active = (step_counts > number).astype(jnp.float32)[:, None, None, None]
            current = current[:, :, 1:-1, 1:-1] + active * (div_east + div_north)
    return current


def both_sums(terms, partial_value):
    return lax.psum((terms, partial_value), ("gx", "gy", "gz"))


def squares(resid_field):
    return lax.psum(jnp.sum(resid_field * resid_field), ("gx", "gy", "gz"))


def shards_any(
    innovation,
    obs_precision,
    error_scale,
    kappa_x,
    kappa_y,
    sea_mask,
    members,
    vertical,
    diffusion_steps,
):
    wet_cells = sea_mask.astype(jnp.float32)
    coefficients = jnp.stack([kappa_x, kappa_y, wet_cells])
    padded = extended(coefficients, (("gx", 2), ("gy", 3)), KMAX)
    cols_dev = wet_cells.shape[2]
    y_position = (
        lax.axis_index("gy") * cols_dev + jnp.arange(cols_dev + 2 * KMAX, dtype=jnp.int32) - KMAX
    )
    inside = ((y_position >= 0) & (y_position < cols_dev * lax.axis_size("gy"))).astype(jnp.float32)
    padded = jnp.stack([padded[0], padded[1], padded[2] * inside[None, None, :]])
    halo_depth = 2
    transposed = jnp.swapaxes(vertical, 1, 2)
    sqrt_static = math.sqrt(static_share)
    ens_scale = math.sqrt(ensemble_share / (members.shape[0] - 1))

    def static_back(masked):
        return sqrt_static * diffuse(
            level_mix(error_scale * masked, transposed), padded, diffusion_steps, halo_depth
        )

    def ensemble_terms(masked):
        return jnp.einsum("mflxy,flxy->m", members, masked, precision=lax.Precision.HIGHEST)

    masked = wet_cells * (obs_precision * innovation)
    resid_field = static_back(masked)
    ens_sum, field_norm = both_sums(ensemble_terms(masked), jnp.sum(resid_field * resid_field))
    resid_weights = ens_scale * ens_sum
    norm_now = field_norm + jnp.sum(resid_weights * resid_weights)
    dir_field, dir_weights = (resid_field, resid_weights)
    control_field = jnp.zeros_like(resid_field)
    control_weights = jnp.zeros(resid_weights.shape, jnp.float32)
    for iteration in range(ITERS):
        static = error_scale * level_mix(
            diffuse(dir_field, padded, diffusion_steps, halo_depth), vertical
        )
        ensemble = jnp.einsum(
            "m,mflxy->flxy", dir_weights, members, precision=lax.Precision.HIGHEST
        )
        observed = wet_cells * (sqrt_static * static + ens_scale * ensemble)
        weighted = obs_precision * observed
        masked = wet_cells * weighted
        image_field = dir_field + static_back(masked)
        ens_sum, curve_part = both_sums(ensemble_terms(masked), jnp.sum(dir_field * image_field))
        image_weights = dir_weights + ens_scale * ens_sum
        curvature = curve_part + jnp.sum(dir_weights * image_weights)
        step_length = norm_now / curvature
        control_field = control_field + step_length * dir_field
        control_weights = control_weights + step_length * dir_weights
        resid_field = resid_field - step_length * image_field
        resid_weights = resid_weights - step_length * image_weights
        if iteration + 1 < ITERS:
            norm_next = squares(resid_field) + jnp.sum(resid_weights * resid_weights)
            ratio_next = norm_next / norm_now
            dir_field = resid_field + ratio_next * dir_field
            dir_weights = resid_weights + ratio_next * dir_weights
            norm_now = norm_next
    return (control_field, control_weights, resid_field)

ROWS = 16
WIN = 56
TILES = WIN // 8
NEAR_TILES = 5
LANES = 128
DEPTH = 2 * KMAX
GROUP = LANES // DEPTH
SUMS = 8
FETCHES = 4
AXES = ("gx", "gy", "gz")
VMEM = pl.BlockSpec(memory_space=pltpu.VMEM)
HBM = pl.BlockSpec(memory_space=pltpu.HBM)
SQRT_STATIC = math.sqrt(static_share)


def f32(*shape):
    return jax.ShapeDtypeStruct(shape, jnp.float32)


def call(kernel, outs, specs, args, scratch=(), grant=32):
    return pl.pallas_call(
        kernel,
        out_shape=outs,
        in_specs=specs,
        out_specs=[VMEM] * len(outs),
        scratch_shapes=list(scratch),
        compiler_params=pltpu.CompilerParams(vmem_limit_bytes=grant * 1024 * 1024),
    )(*args)


def lanes_of(shape):
    return lax.broadcasted_iota(jnp.int32, shape, len(shape) - 1)


def tile(ref, index, size=ROWS):
    return ref[index * size : (index + 1) * size, :]


def pack_edges(out_ref, planes, cols):
    first = jnp.where(lax.axis_index("gy") == 0, cols - DEPTH, 0)
    lane = lanes_of((ROWS, LANES))
    for group in range(-(-len(planes) // GROUP)):
        packed = jnp.zeros((ROWS, LANES), jnp.float32)
        for slot, plane in enumerate(planes[group * GROUP : (group + 1) * GROUP]):
            moved = pltpu.roll(plane, lax.rem(DEPTH * slot - first + LANES, LANES), 1)
            packed = jnp.where((lane >= DEPTH * slot) & (lane < DEPTH * (slot + 1)), moved, packed)
        out_ref[group * ROWS : (group + 1) * ROWS, :] = packed


def with_edge(own, edge_ref, index, cols):
    group, slot = divmod(index, GROUP)
    moved = pltpu.roll(tile(edge_ref, group), (cols - DEPTH * slot) % LANES, 1)
    return jnp.where(lanes_of(own.shape) < cols, own, moved)


def over_rows(values):
    return jnp.sum(values, axis=0, keepdims=True)


def whole(values):
    return jnp.sum(over_rows(values), axis=1, keepdims=True)


def on_diagonal(values):
    rows = lax.broadcasted_iota(jnp.int32, values.shape, 0)
    return over_rows(jnp.where(rows == lanes_of(values.shape), values, 0.0))


def off_diagonal(row, count):
    shape = (count, LANES)
    rows = lax.broadcasted_iota(jnp.int32, shape, 0)
    return spread(jnp.where(rows == lanes_of(shape), jnp.broadcast_to(row, shape), 0.0))


def spread(values):
    return jnp.broadcast_to(jnp.sum(values, axis=1, keepdims=True), values.shape)


def coefficient_planes(coef, sources, levels, cols):
    coef[...] = jnp.zeros(coef.shape, jnp.float32)
    for level in range(levels):
        for kind, source in enumerate(sources):
            at = (kind * levels + level) * ROWS
            coef[at : at + ROWS, :cols] = source[level].astype(jnp.float32)


def project(stack, at, totals, scale):
    for m, total in enumerate(totals):
        stack[at + m : at + m + 1, : total.shape[1]] = scale * over_rows(total)


def start(planes, levels, cols, count):
    ens_scale = math.sqrt(ensemble_share / (count - 1))
    base = planes * ROWS
    edge_rows = -(-(planes + 3 * levels) // GROUP) * ROWS

    def kernel(*refs):
        sources, (out_z, out_e, coef), copies, (weighted, stack, sems) = refs[:7], refs[7:10], refs[10:17], refs[17:]
        pairs = list(zip(sources[:6], copies[:6], strict=True))
        for part in range(FETCHES):
            rows = pl.ds(part * (count // FETCHES), count // FETCHES)
            pairs.append((sources[6].at[rows], copies[6].at[rows]))
        moves = [pltpu.make_async_copy(a, b, sems.at[i]) for i, (a, b) in enumerate(pairs)]
        for move in moves:
            move.start()
        innov, prec, scale, mask, kx, ky, members = copies
        out_z[...] = jnp.zeros(out_z.shape, jnp.float32)
        stack[...] = jnp.zeros(stack.shape, jnp.float32)
        for move in moves[:6]:
            move.wait()
        coefficient_planes(coef, (kx, ky, mask), levels, cols)
        for plane in range(planes):
            weighted[plane] = mask[plane % levels].astype(jnp.float32) * (prec[plane] * innov[plane])
            out_z[plane * ROWS : (plane + 1) * ROWS, :cols] = scale[plane] * weighted[plane]
        edges = [tile(out_z, plane) for plane in range(planes)]
        pack_edges(out_e, edges + [tile(coef, index) for index in range(3 * levels)], cols)
        each = count // FETCHES
        for part in range(FETCHES):
            moves[6 + part].wait()
            totals = [jnp.zeros((ROWS, cols), jnp.float32) for _ in range(each)]
            for plane in range(planes):
                for m in range(each):
                    totals[m] += members[part * each + m, plane] * weighted[plane]
            project(stack, part * each, totals, ens_scale)
        out_z[base : base + 1, :] = on_diagonal(spread(stack[...]))
        out_e[edge_rows:, :] = out_z[base:, :]

    outs = [f32(base + SUMS, LANES), f32(edge_rows + SUMS, LANES), f32(3 * levels * ROWS, LANES)]
    field, flat = (planes, ROWS, cols), (levels, ROWS, cols)
    kept = [(field, jnp.float32)] * 3 + [(flat, jnp.int32)] + [(flat, jnp.float32)] * 2 + [((count,) + field, jnp.float32)]
    scratch = [pltpu.VMEM(*one) for one in kept] + [pltpu.VMEM(field, jnp.float32), pltpu.VMEM((ROWS, LANES), jnp.float32)]
    scratch.append(pltpu.SemaphoreType.DMA((6 + FETCHES,)))
    return kernel, outs, scratch


def observe(planes, levels, cols, count, with_weights):
    ens_scale = math.sqrt(ensemble_share / (count - 1))
    base = planes * ROWS
    edge_rows = -(-planes // GROUP) * ROWS

    def kernel(*refs):
        own, other, weights, sums, vert, prec, scale, mask, members = refs[:9]
        if with_weights:
            out_z, out_e, seen, stack = refs[9:]
        else:
            seen, out_z, out_e, now = refs[9:]
        out_z[...] = jnp.zeros(out_z.shape, jnp.float32)
        totals = [jnp.zeros((ROWS, cols), jnp.float32) for _ in range(count)]
        energy = jnp.zeros((ROWS, cols), jnp.float32)
        cross = jnp.zeros((ROWS, cols), jnp.float32)
        here = lax.axis_index("gz") * levels
        there = (1 - lax.axis_index("gz")) * levels
        for plane in range(planes):
            field, level = divmod(plane, levels)
            wet = mask[level].astype(jnp.float32)
            static = jnp.zeros((ROWS, cols), jnp.float32)
            for k in range(levels):
                row = (field * 2 * levels + here + level) * 2 * levels
                static += vert[pl.ds(row + here + k, 1), :cols] * tile(own, field * levels + k)[:, :cols]
                static += vert[pl.ds(row + there + k, 1), :cols] * tile(other, field * levels + k)[:, :cols]
            ensemble = jnp.zeros((ROWS, cols), jnp.float32)
            for m in range(count):
                ensemble += weights[m : m + 1, :cols] * members[m, plane]
            seen_now = wet * (SQRT_STATIC * (scale[plane] * static) + ens_scale * ensemble)
            weighted = wet * (prec[plane] * seen_now)
            if with_weights:
                seen[plane] = seen_now
                energy += seen_now * weighted
                for m in range(count):
                    totals[m] += members[m, plane] * weighted
            else:
                now[plane] = seen_now
                before = seen[plane]
                energy += before * (prec[plane] * before)
                cross += before * weighted
            out_z[plane * ROWS : (plane + 1) * ROWS, :cols] = scale[plane] * weighted
        if with_weights:
            stack[:ROWS, :] = jnp.zeros((ROWS, LANES), jnp.float32)
            project(stack, 0, totals, ens_scale)
            stack[ROWS:, :] = sums[...]
            stack[ROWS : ROWS + 1, :cols] = over_rows(energy)
            out_z[base : base + 1, :] = on_diagonal(spread(stack[...]))
        else:
            out_z[base:, :] = sums[...]
            energy, cross = whole(energy), whole(cross)
            share = jnp.where(energy > 0.0, -cross / jnp.where(energy > 0.0, energy, 1.0), 0.0)
            rest = jnp.zeros((ROWS, cols), jnp.float32)
            left = jnp.zeros((ROWS, cols), jnp.float32)
            for plane in range(planes):
                before = seen[plane]
                gap = now[plane] + share * before
                rest += gap * (prec[plane] * gap)
                left += before * (prec[plane] * gap)
            place = (lax.axis_index("gx") * 2 + lax.axis_index("gy")) * 2 + lax.axis_index("gz")
            own_lane = lanes_of((1, LANES)) == place
            for index, value in enumerate((whole(rest), whole(left), share, energy)):
                out_z[base + index : base + index + 1, :] = jnp.where(own_lane, value, 0.0)
        pack_edges(out_e, [tile(out_z, plane) for plane in range(planes)], cols)
        out_e[edge_rows:, :] = out_z[base:, :]

    outs = [f32(base + SUMS, LANES), f32(edge_rows + SUMS, LANES)]
    if with_weights:
        return kernel, outs + [f32(planes, ROWS, cols)], [pltpu.VMEM((ROWS + SUMS, LANES), jnp.float32)]
    return kernel, outs, [pltpu.VMEM((planes, ROWS, cols), jnp.float32)]


def mix_back(first, far, planes, levels, cols):
    base = planes * ROWS
    coefs = 2 * levels if first else 0
    fields = planes // levels
    count = planes + coefs
    sent = -(-planes * KMAX // 8) * 8

    def kernel(*refs):
        if first:
            own, other, edge, edge_other, vert, raw, out_all, out_near = refs
        elif far:
            own, other, edge, edge_other, vert, out_all, out_near = refs
        else:
            own, other, edge, edge_other, vert, out_own, out_one, out_three, out_sums = refs
        here = lax.axis_index("gz") * levels
        there = (1 - lax.axis_index("gz")) * levels
        even = lax.rem(lax.axis_index("gx"), 2) == 0
        upper = lax.broadcasted_iota(jnp.int32, (8, LANES), 0) < 4

        def put(index, values):
            if far:
                out_all[index * ROWS : (index + 1) * ROWS, :] = values
                out_near[index * 8 : (index + 1) * 8, :] = jnp.where(upper, values[:8], values[8:])
            else:
                out_own[index * ROWS : (index + 1) * ROWS, :] = values
                head, end = values[:KMAX], values[ROWS - KMAX :]
                out_one[index * KMAX : (index + 1) * KMAX, :] = jnp.where(even, end, head)
                out_three[index * KMAX : (index + 1) * KMAX, :] = jnp.where(even, head, end)

        for field in range(fields):
            mine = [with_edge(tile(own, field * levels + l), edge, field * levels + l, cols) for l in range(levels)]
            theirs = [
                with_edge(tile(other, field * levels + l), edge_other, field * levels + l, cols) for l in range(levels)
            ]
            for k in range(levels):
                mixed = jnp.zeros((ROWS, LANES), jnp.float32)
                for l in range(levels):
                    block = field * 2 * levels
                    mixed += vert[pl.ds((block + here + l) * 2 * levels + here + k, 1), :] * mine[l]
                    mixed += vert[pl.ds((block + there + l) * 2 * levels + here + k, 1), :] * theirs[l]
                put(field * levels + k, mixed)
        packed = -(-(planes + (3 * levels if first else 0)) // GROUP) * ROWS
        total = (own[base:, :] + other[base:, :]) + (edge[packed:, :] + edge_other[packed:, :])
        if not far:
            out_sums[...] = total
            out_one[sent:, :] = total
            out_three[sent:, :] = total
            return
        at, near_at = count * ROWS, count * 8
        if first:
            last = jnp.where(lax.axis_index("gy") == 0, LANES - 1, cols - 1)
            lane = lanes_of((ROWS, LANES))
            bottom = lax.broadcasted_iota(jnp.int32, (ROWS, LANES), 0) == ROWS - 1
            for level in range(levels):
                kx, ky, wet = (
                    with_edge(tile(raw, kind * levels + level), edge, planes + kind * levels + level, cols) for kind in range(3)
                )
                put(planes + level, kx * wet * jnp.where(bottom, 1.0, pltpu.roll(wet, ROWS - 1, 0)))
                put(planes + levels + level, jnp.where(lane == last, 0.0, ky * wet * pltpu.roll(wet, LANES - 1, 1)))
                total = jnp.where(lax.broadcasted_iota(jnp.int32, total.shape, 0) == 1 + level, wet[:1], total)
        out_all[at:, :] = total
        out_near[near_at:, :] = total

    if not far:
        return kernel, [f32(base, LANES)] + [f32(sent + SUMS, LANES)] * 2 + [f32(SUMS, LANES)]
    return kernel, [f32(count * ROWS + SUMS, LANES), f32(count * 8 + SUMS, LANES)]


def is_even():
    return lax.rem(lax.axis_index("gx"), 2) == 0


def far_window(nat, index, own, first, near, third, slot):
    even = is_even()
    one, three = tile(first, slot), tile(third, slot)
    nat[index, 0:16, :] = tile(own, slot)
    nat[index, 16:32, :] = jnp.where(even, one, three)
    nat[index, 32:40, :] = tile(near, slot, 8)
    nat[index, 40:56, :] = jnp.where(even, three, one)


def shorten(nat, index):
    return jnp.concatenate([nat[index, 0:28, :], nat[index, 44:56, :]], axis=0)


def dealt(nat, index, tiles):
    return [nat[index, pl.ds(t, 8, stride=tiles), :] for t in range(tiles)]


def deal(buf, nat, index, tiles):
    for t, values in enumerate(dealt(nat, index, tiles)):
        buf[index, t * 8 : (t + 1) * 8, :] = values


def undeal(nat, buf, index, tiles):
    for t in range(tiles):
        nat[index, pl.ds(t, 8, stride=tiles), :] = buf[index, t * 8 : (t + 1) * 8, :]


def eight(ref, tiles, *index):
    return [ref[(*index, pl.ds(t * 8, 8), slice(None))] for t in range(tiles)]


def after(tiles):
    return tiles[1:] + [pltpu.roll(tiles[0], 7, 0)]


def run_steps(buf, spare, coef, steps, planes, levels, tiles):
    for number in range(KMAX):
        source, target = (buf, spare)[number % 2], (spare, buf)[number % 2]
        for level in range(levels):
            east, north, south = (eight(coef, tiles, kind, level) for kind in range(3))
            for field in range(planes // levels):
                plane = field * levels + level
                active = jnp.where(steps[field : field + 1, :] > float(number), 1.0, 0.0).astype(jnp.float32)
                u = eight(source, tiles, plane)
                flux_east = [c * (v - w) for c, v, w in zip(east, after(u), u, strict=True)]
                flux_west = [pltpu.roll(flux_east[-1], 1, 0)] + flux_east[:-1]
                for t in range(tiles):
                    to_north = north[t] * (pltpu.roll(u[t], LANES - 1, 1) - u[t])
                    to_south = south[t] * (pltpu.roll(u[t], 1, 1) - u[t])
                    change = (flux_east[t] - flux_west[t]) + (to_north + to_south)
                    target[plane, t * 8 : (t + 1) * 8, :] = u[t] + active * change


def own_sum(values, cols):
    return over_rows(jnp.where(lanes_of(values.shape) < cols, values, 0.0))


def window_scratch(planes):
    return [pltpu.VMEM((planes, WIN, LANES), jnp.float32)] * 2


def diffuse_own(out_g, field, buf, nat, coef, steps, planes, levels):
    for plane in range(planes):
        for t, values in enumerate(dealt(field, plane, NEAR_TILES)):
            buf[plane, t * 8 : (t + 1) * 8, :] = values
    run_steps(buf, nat, coef, steps, planes, levels, NEAR_TILES)
    for plane in range(planes):
        undeal(nat, buf, plane, NEAR_TILES)
        out_g[plane * ROWS : (plane + 1) * ROWS, :] = nat[plane, :ROWS, :]


def first_diffuse(planes, levels, cols):
    coefs = 2 * levels

    def kernel(own, first, near, third, steps, coef, coef_near, resid, weights, sums, out_g, buf, nat):
        even = is_even()
        at, near_at = (planes + coefs) * ROWS, (planes + coefs) * 8
        for index in range(coefs):
            far_window(nat, index, own, first, near, third, planes + index)
            if index < levels:
                row, near_row = at + 1 + index, near_at + 1 + index
                one, three = first[row : row + 1, :], third[row : row + 1, :]
                nat[index, 15:16, :] = nat[index, 15:16, :] * jnp.where(even, one, three)
                nat[index, 31:32, :] = nat[index, 31:32, :] * near[near_row : near_row + 1, :]
                nat[index, 39:40, :] = nat[index, 39:40, :] * jnp.where(even, three, one)
                nat[index, 55:56, :] = nat[index, 55:56, :] * own[row : row + 1, :]
            buf[index, : 8 * NEAR_TILES, :] = shorten(nat, index)
            kind, level = divmod(index, levels)
            for target, window, tiles in ((coef, nat, TILES), (coef_near, buf, NEAR_TILES)):
                for t, values in enumerate(dealt(window, index, tiles)):
                    target[kind, level, t * 8 : (t + 1) * 8, :] = values
                    if kind == 1:
                        target[2, level, t * 8 : (t + 1) * 8, :] = pltpu.roll(values, 1, 1)
        for plane in range(planes):
            far_window(nat, plane, own, first, near, third, plane)
            deal(buf, nat, plane, TILES)
        sent = slice(at, at + 1)
        total = (own[sent, :] + first[sent, :]) + (near[near_at : near_at + 1, :] + third[sent, :])
        weights[...] = off_diagonal(total, ROWS)
        run_steps(buf, nat, coef, steps, planes, levels, TILES)
        squares = jnp.zeros((ROWS, LANES), jnp.float32)
        for plane in range(planes):
            undeal(nat, buf, plane, TILES)
            value = SQRT_STATIC * shorten(nat, plane)
            resid[plane] = value
            squares += value[:ROWS] * value[:ROWS]
        sums[...] = jnp.zeros(sums.shape, jnp.float32)
        sums[4:5, :] = own_sum(squares, cols)
        diffuse_own(out_g, resid, buf, nat, coef_near, steps, planes, levels)

    outs = [
        f32(3, levels, WIN, LANES),
        f32(3, levels, 8 * NEAR_TILES, LANES),
        f32(planes, 8 * NEAR_TILES, LANES),
        f32(ROWS, LANES),
        f32(SUMS, LANES),
        f32(planes * ROWS, LANES),
    ]
    return kernel, outs, window_scratch(planes)


def second_diffuse(planes, levels, cols):
    def kernel(
        own, first, near, third, steps, coef, coef_near, resid, weights, image, new, new_w, sums, facts, out_g, buf, nat, field
    ):
        for plane in range(planes):
            far_window(nat, plane, own, first, near, third, plane)
            deal(buf, nat, plane, TILES)
        at, near_at = planes * ROWS, planes * 8
        sent = slice(at, at + 1)
        total = (own[sent, :] + first[sent, :]) + (near[near_at : near_at + 1, :] + third[sent, :])
        total = off_diagonal(total, ROWS + SUMS)
        energy = total[ROWS : ROWS + 1]
        rr = total[ROWS + 4 : ROWS + 5] + over_rows(weights[...] * weights[...])
        step = rr / (rr + energy)
        new_w[...] = weights[...] - step * (weights[...] + total[:ROWS])
        facts[...] = jnp.zeros(facts.shape, jnp.float32)
        facts[0:1, :] = rr
        facts[1:2, :] = step
        run_steps(buf, nat, coef, steps, planes, levels, TILES)
        squares = jnp.zeros((ROWS, LANES), jnp.float32)
        cross = jnp.zeros((ROWS, LANES), jnp.float32)
        for plane in range(planes):
            undeal(nat, buf, plane, TILES)
            direction = resid[plane]
            image_now = direction + SQRT_STATIC * shorten(nat, plane)
            value = direction - step * image_now
            field[plane] = value
            image[plane] = image_now[:ROWS]
            new[plane] = value[:ROWS]
            squares += value[:ROWS] * value[:ROWS]
            cross += value[:ROWS] * direction[:ROWS]
        sums[...] = jnp.zeros(sums.shape, jnp.float32)
        sums[4:5, :] = own_sum(squares, cols)
        sums[5:6, :] = own_sum(cross, cols)
        diffuse_own(out_g, field, buf, nat, coef_near, steps, planes, levels)

    block = f32(planes, ROWS, LANES)
    outs = [block, block, f32(ROWS, LANES), f32(SUMS, LANES), f32(SUMS, LANES), f32(planes * ROWS, LANES)]
    return kernel, outs, window_scratch(planes) + [pltpu.VMEM((planes, 8 * NEAR_TILES, LANES), jnp.float32)]


def last_diffuse(planes, levels, cols):
    def kernel(own, one, three, sums, steps, coef, out_g, out_sums, buf, nat):
        even = is_even()
        gap_rows = jnp.zeros((4, LANES), jnp.float32)
        for plane in range(planes):
            first, third = tile(one, plane, KMAX), tile(three, plane, KMAX)
            nat[plane, 0:16, :] = tile(own, plane)
            nat[plane, 16:26, :] = jnp.where(even, first, third)
            nat[plane, 26:30, :] = gap_rows
            nat[plane, 30:40, :] = jnp.where(even, third, first)
            deal(buf, nat, plane, NEAR_TILES)
        sent = one.shape[0] - SUMS
        out_sums[0] = sums[...] + one[sent:, :]
        out_sums[1] = three[sent:, :]
        run_steps(buf, nat, coef, steps, planes, levels, NEAR_TILES)
        for plane in range(planes):
            undeal(nat, buf, plane, NEAR_TILES)
            out_g[plane] = nat[plane, :ROWS, :]

    return kernel, [f32(planes, ROWS, LANES), f32(2, SUMS, LANES)], window_scratch(planes)


def finish(planes, cols):
    def kernel(diffused, sums, sums_two, resid, weights, image, new, new_w, facts, control, control_w, final):
        lanes = sums[0] + (sums_two[...] + sums[1])
        total = spread(lanes)
        rr, step = facts[0:1, :], facts[1:2, :]
        new_rr = total[4:5] + over_rows(new_w[...] * new_w[...])
        cross_rr = total[5:6] + over_rows(new_w[...] * weights[...])
        ratio = new_rr / rr
        gap = ratio - lanes[2:3]
        energy = spread(lanes[0:1] + gap * (2.0 * lanes[1:2] + gap * lanes[3:4]))
        squares = new_rr + ratio * (2.0 * cross_rr + ratio * rr)
        new_step = new_rr / (squares + energy)
        combined = step * weights[...] + new_step * (new_w[...] + ratio * weights[...])
        diagonal = lax.broadcasted_iota(jnp.int32, combined.shape, 0) == lanes_of(combined.shape)
        control_w[...] = over_rows(jnp.where(diagonal, combined, 0.0))[:, :ROWS]
        for plane in range(planes):
            direction, value = resid[plane, :ROWS, :], new[plane]
            new_direction = value + ratio * direction
            new_image = (value + SQRT_STATIC * diffused[plane]) + ratio * image[plane]
            control[plane] = (step * direction + new_step * new_direction)[:, :cols]
            final[plane] = (value - new_step * new_image)[:, :cols]

    return kernel, [f32(planes, ROWS, cols), f32(1, ROWS), f32(planes, ROWS, cols)]


def moved_to(values, x, y, z):
    sizes = [lax.axis_size(axis) for axis in AXES]
    here = [(a, b, c) for a in range(sizes[0]) for b in range(sizes[1]) for c in range(sizes[2])]
    number = {place: index for index, place in enumerate(here)}
    return lax.ppermute(values, AXES, [(number[a, b, c], number[a ^ x, b ^ y, c ^ z]) for a, b, c in here])


def mix_round(kernel_of, out_z, out_e, vert, raw=None):
    other = moved_to(out_z, 0, 0, 1)
    edge = moved_to(out_e, 0, 1, 0)
    edge_other = moved_to(out_e, 0, 1, 1)
    kernel, outs = kernel_of
    args = (out_z, other, edge, edge_other, vert)
    if raw is not None:
        args += (raw,)
    return call(kernel, outs, [VMEM] * len(args), args)


def far_round(own, near):
    return own, moved_to(own, 1, 0, 0), moved_to(near, 2, 0, 0), moved_to(own, 3, 0, 0)


def shards_small(
    innovation, obs_precision, error_scale, kappa_x, kappa_y, sea_mask, members, vertical, diffusion_steps
):
    fields, levels, rows, cols = innovation.shape
    count = members.shape[0]
    planes = fields * levels
    block = (planes, rows, cols)
    innov, prec, scale = (a.reshape(block) for a in (innovation, obs_precision, error_scale))
    ens = members.reshape((count,) + block)
    vert = jnp.broadcast_to(vertical.reshape(-1, 1), (vertical.size, LANES))
    steps = jnp.broadcast_to(diffusion_steps.astype(jnp.float32)[:, None], (fields, LANES))

    kernel, outs, scratch = start(planes, levels, cols, count)
    args = (innov, prec, scale, sea_mask, kappa_x, kappa_y, ens)
    args = [pltpu.with_memory_space_constraint(a, pltpu.HBM) for a in args]
    out_z, out_e, raw = call(kernel, outs, [HBM] * 7, args, scratch)
    parts = far_round(*mix_round(mix_back(True, True, planes, levels, cols), out_z, out_e, vert, raw))
    kernel, outs, scratch = first_diffuse(planes, levels, cols)
    coef, coef_near, resid, weights, sums, out_g = call(kernel, outs, [VMEM] * 5, (*parts, steps), scratch)

    kernel, outs, scratch = observe(planes, levels, cols, count, True)
    args = (out_g, moved_to(out_g, 0, 0, 1), weights, sums, vert, prec, scale, sea_mask, ens)
    out_z, out_e, seen = call(kernel, outs, [VMEM] * 9, args, scratch)
    parts = far_round(*mix_round(mix_back(False, True, planes, levels, cols), out_z, out_e, vert))
    kernel, outs, scratch = second_diffuse(planes, levels, cols)
    args = (*parts, steps, coef, coef_near, resid, weights)
    image, new, new_w, sums, facts, out_g = call(kernel, outs, [VMEM] * 9, args, scratch)

    kernel, outs, scratch = observe(planes, levels, cols, count, False)
    args = (out_g, moved_to(out_g, 0, 0, 1), new_w, sums, vert, prec, scale, sea_mask, ens, seen)
    out_z, out_e = call(kernel, outs, [VMEM] * 10, args, scratch)
    own, one, three, sums = mix_round(mix_back(False, False, planes, levels, cols), out_z, out_e, vert)
    sums_two = moved_to(sums, 2, 0, 0)
    kernel, outs, scratch = last_diffuse(planes, levels, cols)
    args = (own, moved_to(one, 1, 0, 0), moved_to(three, 3, 0, 0), sums, steps, coef_near)
    diffused, sums = call(kernel, outs, [VMEM] * 6, args, scratch)
    kernel, outs = finish(planes, cols)
    args = (diffused, sums, sums_two, resid, weights, image, new, new_w, facts)
    control, control_w, final = call(kernel, outs, [VMEM] * 9, args)
    return control.reshape(innovation.shape), control_w.reshape(count), final.reshape(innovation.shape)


def shards(innovation, obs_precision, error_scale, kappa_x, kappa_y, sea_mask, members, vertical, diffusion_steps):
    arrays = (innovation, obs_precision, error_scale, kappa_x, kappa_y, sea_mask, members, vertical, diffusion_steps)
    sizes = tuple(lax.axis_size(axis) for axis in AXES)
    rows, cols = innovation.shape[2:]
    fits = rows == ROWS and members.shape[0] == ROWS and DEPTH <= cols <= LANES - DEPTH and ITERS == 2
    if sizes == (4, 2, 2) and fits:
        return shards_small(*arrays)
    return shards_any(*arrays)


def solution(mesh):
    placed = (
        P("grp", "gz", "gx", "gy"),
        P("grp", "gz", "gx", "gy"),
        P(None, "gz", "gx", "gy"),
        P("gz", "gx", "gy"),
        P("gz", "gx", "gy"),
        P("gz", "gx", "gy"),
        P("grp", None, "gz", "gx", "gy"),
        P(),
        P(),
    )
    return jax.shard_map(
        shards,
        mesh=mesh,
        in_specs=placed,
        out_specs=(P("grp", "gz", "gx", "gy"), P("grp"), P("grp", "gz", "gx", "gy")),
        check_vma=False,
    )
```

```python
import functools
import math


import jax
import jax.numpy as jnp
from jax import lax
from jax.experimental import pallas as pl
from jax.experimental.pallas import tpu as pltpu
from jax.sharding import PartitionSpec as P

KMAX = 10
ITERS = 2


static_share = 0.6
ensemble_share = 0.4


def extended(cells, sides, width):
    for axis, dim in sides:
        count = lax.axis_size(axis)
        head = lax.slice_in_dim(cells, 0, width, axis=dim)
        tail = lax.slice_in_dim(cells, cells.shape[dim] - width, cells.shape[dim], axis=dim)
        cells = jnp.concatenate(
            [
                lax.ppermute(tail, axis, [(i, (i + 1) % count) for i in range(count)]),
                cells,
                lax.ppermute(head, axis, [((i + 1) % count, i) for i in range(count)]),
            ],
            axis=dim,
        )
    return cells


def level_mix(source, mixing):
    local_levels = source.shape[1]
    gathered = lax.all_gather(source, "gz", axis=1, tiled=True)
    own_rows = lax.dynamic_slice_in_dim(
        mixing, lax.axis_index("gz") * local_levels, local_levels, 1
    )
    return jnp.einsum("flk,fkxy->flxy", own_rows, gathered, precision=lax.Precision.HIGHEST)


def diffuse(source, padded, step_counts, halo_depth):
    current = source
    for segment in range(KMAX // halo_depth):
        current = extended(current, (("gx", 2), ("gy", 3)), halo_depth)
        for substep in range(halo_depth):
            number = segment * halo_depth + substep
            offset = KMAX - halo_depth + substep
            rows_now = current.shape[2]
            cols_now = current.shape[3]
            window = padded[:, :, offset : offset + rows_now, offset : offset + cols_now]
            east_kappa = window[0]
            north_kappa = window[1]
            wet_window = window[2]
            east_coef = east_kappa[:, :-1, :] * wet_window[:, :-1, :] * wet_window[:, 1:, :]
            flux_east = east_coef * (current[:, :, 1:, :] - current[:, :, :-1, :])
            div_east = (flux_east[:, :, 1:, :] - flux_east[:, :, :-1, :])[:, :, :, 1:-1]
            north_coef = north_kappa[:, :, :-1] * wet_window[:, :, :-1] * wet_window[:, :, 1:]
            flux_north = north_coef * (current[:, :, :, 1:] - current[:, :, :, :-1])
            div_north = (flux_north[:, :, :, 1:] - flux_north[:, :, :, :-1])[:, :, 1:-1, :]
            active = (step_counts > number).astype(jnp.float32)[:, None, None, None]
            current = current[:, :, 1:-1, 1:-1] + active * (div_east + div_north)
    return current


def both_sums(terms, partial_value):
    return lax.psum((terms, partial_value), ("gx", "gy", "gz"))


def squares(resid_field):
    return lax.psum(jnp.sum(resid_field * resid_field), ("gx", "gy", "gz"))


def shards_any(
    innovation,
    obs_precision,
    error_scale,
    kappa_x,
    kappa_y,
    sea_mask,
    members,
    vertical,
    diffusion_steps,
):
    wet_cells = sea_mask.astype(jnp.float32)
    coefficients = jnp.stack([kappa_x, kappa_y, wet_cells])
    padded = extended(coefficients, (("gx", 2), ("gy", 3)), KMAX)
    cols_dev = wet_cells.shape[2]
    y_position = (
        lax.axis_index("gy") * cols_dev + jnp.arange(cols_dev + 2 * KMAX, dtype=jnp.int32) - KMAX
    )
    inside = ((y_position >= 0) & (y_position < cols_dev * lax.axis_size("gy"))).astype(jnp.float32)
    padded = jnp.stack([padded[0], padded[1], padded[2] * inside[None, None, :]])
    halo_depth = 2
    transposed = jnp.swapaxes(vertical, 1, 2)
    sqrt_static = math.sqrt(static_share)
    ens_scale = math.sqrt(ensemble_share / (members.shape[0] - 1))

    def static_back(masked):
        return sqrt_static * diffuse(
            level_mix(error_scale * masked, transposed), padded, diffusion_steps, halo_depth
        )

    def ensemble_terms(masked):
        return jnp.einsum("mflxy,flxy->m", members, masked, precision=lax.Precision.HIGHEST)

    masked = wet_cells * (obs_precision * innovation)
    resid_field = static_back(masked)
    ens_sum, field_norm = both_sums(ensemble_terms(masked), jnp.sum(resid_field * resid_field))
    resid_weights = ens_scale * ens_sum
    norm_now = field_norm + jnp.sum(resid_weights * resid_weights)
    dir_field, dir_weights = (resid_field, resid_weights)
    control_field = jnp.zeros_like(resid_field)
    control_weights = jnp.zeros(resid_weights.shape, jnp.float32)
    for iteration in range(ITERS):
        static = error_scale * level_mix(
            diffuse(dir_field, padded, diffusion_steps, halo_depth), vertical
        )
        ensemble = jnp.einsum(
            "m,mflxy->flxy", dir_weights, members, precision=lax.Precision.HIGHEST
        )
        observed = wet_cells * (sqrt_static * static + ens_scale * ensemble)
        weighted = obs_precision * observed
        masked = wet_cells * weighted
        image_field = dir_field + static_back(masked)
        ens_sum, curve_part = both_sums(ensemble_terms(masked), jnp.sum(dir_field * image_field))
        image_weights = dir_weights + ens_scale * ens_sum
        curvature = curve_part + jnp.sum(dir_weights * image_weights)
        step_length = norm_now / curvature
        control_field = control_field + step_length * dir_field
        control_weights = control_weights + step_length * dir_weights
        resid_field = resid_field - step_length * image_field
        resid_weights = resid_weights - step_length * image_weights
        if iteration + 1 < ITERS:
            norm_next = squares(resid_field) + jnp.sum(resid_weights * resid_weights)
            ratio_next = norm_next / norm_now
            dir_field = resid_field + ratio_next * dir_field
            dir_weights = resid_weights + ratio_next * dir_weights
            norm_now = norm_next
    return (control_field, control_weights, resid_field)

ROWS = 16
WIN = 56
TILES = WIN // 8
NEAR_TILES = 5
LANES = 128
DEPTH = 2 * KMAX
GROUP = LANES // DEPTH
SUMS = 8
FETCHES = 4
AXES = ("gx", "gy", "gz")
VMEM = pl.BlockSpec(memory_space=pltpu.VMEM)
HBM = pl.BlockSpec(memory_space=pltpu.HBM)
SQRT_STATIC = math.sqrt(static_share)


def f32(*shape):
    return jax.ShapeDtypeStruct(shape, jnp.float32)


def call(kernel, outs, specs, args, scratch=(), grant=32):
    return pl.pallas_call(
        kernel,
        out_shape=outs,
        in_specs=specs,
        out_specs=[VMEM] * len(outs),
        scratch_shapes=list(scratch),
        compiler_params=pltpu.CompilerParams(vmem_limit_bytes=grant * 1024 * 1024),
    )(*args)


def lanes_of(shape):
    return lax.broadcasted_iota(jnp.int32, shape, len(shape) - 1)


def tile(ref, index, size=ROWS):
    return ref[index * size : (index + 1) * size, :]


def pack_edges(out_ref, planes, cols):
    first = jnp.where(lax.axis_index("gy") == 0, cols - DEPTH, 0)
    lane = lanes_of((ROWS, LANES))
    for group in range(-(-len(planes) // GROUP)):
        packed = jnp.zeros((ROWS, LANES), jnp.float32)
        for slot, plane in enumerate(planes[group * GROUP : (group + 1) * GROUP]):
            moved = pltpu.roll(plane, lax.rem(DEPTH * slot - first + LANES, LANES), 1)
            packed = jnp.where((lane >= DEPTH * slot) & (lane < DEPTH * (slot + 1)), moved, packed)
        out_ref[group * ROWS : (group + 1) * ROWS, :] = packed


def with_edge(own, edge_ref, index, cols):
    group, slot = divmod(index, GROUP)
    moved = pltpu.roll(tile(edge_ref, group), (cols - DEPTH * slot) % LANES, 1)
    return jnp.where(lanes_of(own.shape) < cols, own, moved)


def over_rows(values):
    return jnp.sum(values, axis=0, keepdims=True)


def whole(values):
    return jnp.sum(over_rows(values), axis=1, keepdims=True)


def on_diagonal(values):
    rows = lax.broadcasted_iota(jnp.int32, values.shape, 0)
    return over_rows(jnp.where(rows == lanes_of(values.shape), values, 0.0))


def off_diagonal(row, count):
    shape = (count, LANES)
    rows = lax.broadcasted_iota(jnp.int32, shape, 0)
    return spread(jnp.where(rows == lanes_of(shape), jnp.broadcast_to(row, shape), 0.0))


def spread(values):
    return jnp.broadcast_to(jnp.sum(values, axis=1, keepdims=True), values.shape)


def coefficient_planes(coef, sources, levels, cols):
    coef[...] = jnp.zeros(coef.shape, jnp.float32)
    for level in range(levels):
        for kind, source in enumerate(sources):
            at = (kind * levels + level) * ROWS
            coef[at : at + ROWS, :cols] = source[level].astype(jnp.float32)


def project(stack, at, totals, scale):
    for m, total in enumerate(totals):
        stack[at + m : at + m + 1, : total.shape[1]] = scale * over_rows(total)


def start(planes, levels, cols, count):
    ens_scale = math.sqrt(ensemble_share / (count - 1))
    base = planes * ROWS
    edge_rows = -(-(planes + 3 * levels) // GROUP) * ROWS

    def kernel(*refs):
        sources, (out_z, out_e, coef), copies, (weighted, stack, sems) = refs[:7], refs[7:10], refs[10:17], refs[17:]
        pairs = list(zip(sources[:6], copies[:6], strict=True))
        for part in range(FETCHES):
            rows = pl.ds(part * (count // FETCHES), count // FETCHES)
            pairs.append((sources[6].at[rows], copies[6].at[rows]))
        moves = [pltpu.make_async_copy(a, b, sems.at[i]) for i, (a, b) in enumerate(pairs)]
        for move in moves:
            move.start()
        innov, prec, scale, mask, kx, ky, members = copies
        out_z[...] = jnp.zeros(out_z.shape, jnp.float32)
        stack[...] = jnp.zeros(stack.shape, jnp.float32)
        for move in moves[:6]:
            move.wait()
        coefficient_planes(coef, (kx, ky, mask), levels, cols)
        for plane in range(planes):
            weighted[plane] = mask[plane % levels].astype(jnp.float32) * (prec[plane] * innov[plane])
            out_z[plane * ROWS : (plane + 1) * ROWS, :cols] = scale[plane] * weighted[plane]
        edges = [tile(out_z, plane) for plane in range(planes)]
        pack_edges(out_e, edges + [tile(coef, index) for index in range(3 * levels)], cols)
        each = count // FETCHES
        for part in range(FETCHES):
            moves[6 + part].wait()
            totals = [jnp.zeros((ROWS, cols), jnp.float32) for _ in range(each)]
            for plane in range(planes):
                for m in range(each):
                    totals[m] += members[part * each + m, plane] * weighted[plane]
            project(stack, part * each, totals, ens_scale)
        out_z[base : base + 1, :] = on_diagonal(spread(stack[...]))
        out_e[edge_rows:, :] = out_z[base:, :]

    outs = [f32(base + SUMS, LANES), f32(edge_rows + SUMS, LANES), f32(3 * levels * ROWS, LANES)]
    field, flat = (planes, ROWS, cols), (levels, ROWS, cols)
    kept = [(field, jnp.float32)] * 3 + [(flat, jnp.int32)] + [(flat, jnp.float32)] * 2 + [((count,) + field, jnp.float32)]
    scratch = [pltpu.VMEM(*one) for one in kept] + [pltpu.VMEM(field, jnp.float32), pltpu.VMEM((ROWS, LANES), jnp.float32)]
    scratch.append(pltpu.SemaphoreType.DMA((6 + FETCHES,)))
    return kernel, outs, scratch


def tables(vert, steps, _, out_vert, out_steps):
    out_vert[...] = vert[...]
    out_steps[...] = steps[...]


def ensemble_part(planes, cols, count):
    ens_scale = math.sqrt(ensemble_share / (count - 1))

    def kernel(weights, members, out):
        for plane in range(planes):
            total = jnp.zeros((ROWS, cols), jnp.float32)
            for m in range(count):
                total += weights[m : m + 1, :cols] * members[m, plane]
            out[plane] = ens_scale * total

    return kernel, [f32(planes, ROWS, cols)]


def observe(planes, levels, cols, count, with_weights):
    ens_scale = math.sqrt(ensemble_share / (count - 1))
    base = planes * ROWS
    edge_rows = -(-planes // GROUP) * ROWS

    def kernel(*refs):
        own, other, ensemble, sums, vert, prec, scale, mask = refs[:8]
        if with_weights:
            members, out_z, out_e, seen, stack = refs[8:]
        else:
            seen, out_z, out_e, now = refs[8:]
        out_z[...] = jnp.zeros(out_z.shape, jnp.float32)
        totals = [jnp.zeros((ROWS, cols), jnp.float32) for _ in range(count)]
        energy = jnp.zeros((ROWS, cols), jnp.float32)
        cross = jnp.zeros((ROWS, cols), jnp.float32)
        here = lax.axis_index("gz") * levels
        there = (1 - lax.axis_index("gz")) * levels
        for plane in range(planes):
            field, level = divmod(plane, levels)
            wet = mask[level].astype(jnp.float32)
            static = jnp.zeros((ROWS, cols), jnp.float32)
            for k in range(levels):
                row = (field * 2 * levels + here + level) * 2 * levels
                static += vert[pl.ds(row + here + k, 1), :cols] * tile(own, field * levels + k)[:, :cols]
                static += vert[pl.ds(row + there + k, 1), :cols] * tile(other, field * levels + k)[:, :cols]
            seen_now = wet * (SQRT_STATIC * (scale[plane] * static) + ensemble[plane])
            weighted = wet * (prec[plane] * seen_now)
            if with_weights:
                seen[plane] = seen_now
                energy += seen_now * weighted
                for m in range(count):
                    totals[m] += members[m, plane] * weighted
            else:
                now[plane] = seen_now
                before = seen[plane]
                energy += before * (prec[plane] * before)
                cross += before * weighted
            out_z[plane * ROWS : (plane + 1) * ROWS, :cols] = scale[plane] * weighted
        if with_weights:
            stack[:ROWS, :] = jnp.zeros((ROWS, LANES), jnp.float32)
            project(stack, 0, totals, ens_scale)
            stack[ROWS:, :] = sums[...]
            stack[ROWS : ROWS + 1, :cols] = over_rows(energy)
            out_z[base : base + 1, :] = on_diagonal(spread(stack[...]))
        else:
            out_z[base:, :] = sums[...]
            energy, cross = whole(energy), whole(cross)
            share = jnp.where(energy > 0.0, -cross / jnp.where(energy > 0.0, energy, 1.0), 0.0)
            rest = jnp.zeros((ROWS, cols), jnp.float32)
            left = jnp.zeros((ROWS, cols), jnp.float32)
            for plane in range(planes):
                before = seen[plane]
                gap = now[plane] + share * before
                rest += gap * (prec[plane] * gap)
                left += before * (prec[plane] * gap)
            place = (lax.axis_index("gx") * 2 + lax.axis_index("gy")) * 2 + lax.axis_index("gz")
            own_lane = lanes_of((1, LANES)) == place
            for index, value in enumerate((whole(rest), whole(left), share, energy)):
                out_z[base + index : base + index + 1, :] = jnp.where(own_lane, value, 0.0)
        pack_edges(out_e, [tile(out_z, plane) for plane in range(planes)], cols)
        out_e[edge_rows:, :] = out_z[base:, :]

    outs = [f32(base + SUMS, LANES), f32(edge_rows + SUMS, LANES)]
    if with_weights:
        return kernel, outs + [f32(planes, ROWS, cols)], [pltpu.VMEM((ROWS + SUMS, LANES), jnp.float32)]
    return kernel, outs, [pltpu.VMEM((planes, ROWS, cols), jnp.float32)]


def mix_back(first, far, planes, levels, cols):
    base = planes * ROWS
    coefs = 2 * levels if first else 0
    fields = planes // levels
    count = planes + coefs
    sent = -(-planes * KMAX // 8) * 8

    def kernel(*refs):
        if first:
            own, other, edge, edge_other, vert, raw, out_all, out_near = refs
        elif far:
            own, other, edge, edge_other, vert, out_all, out_near = refs
        else:
            own, other, edge, edge_other, vert, out_own, out_one, out_three, out_sums = refs
        here = lax.axis_index("gz") * levels
        there = (1 - lax.axis_index("gz")) * levels
        even = lax.rem(lax.axis_index("gx"), 2) == 0
        upper = lax.broadcasted_iota(jnp.int32, (8, LANES), 0) < 4

        def put(index, values):
            if far:
                out_all[index * ROWS : (index + 1) * ROWS, :] = values
                out_near[index * 8 : (index + 1) * 8, :] = jnp.where(upper, values[:8], values[8:])
            else:
                out_own[index * ROWS : (index + 1) * ROWS, :] = values
                head, end = values[:KMAX], values[ROWS - KMAX :]
                out_one[index * KMAX : (index + 1) * KMAX, :] = jnp.where(even, end, head)
                out_three[index * KMAX : (index + 1) * KMAX, :] = jnp.where(even, head, end)

        for field in range(fields):
            mine = [with_edge(tile(own, field * levels + l), edge, field * levels + l, cols) for l in range(levels)]
            theirs = [
                with_edge(tile(other, field * levels + l), edge_other, field * levels + l, cols) for l in range(levels)
            ]
            for k in range(levels):
                mixed = jnp.zeros((ROWS, LANES), jnp.float32)
                for l in range(levels):
                    block = field * 2 * levels
                    mixed += vert[pl.ds((block + here + l) * 2 * levels + here + k, 1), :] * mine[l]
                    mixed += vert[pl.ds((block + there + l) * 2 * levels + here + k, 1), :] * theirs[l]
                put(field * levels + k, mixed)
        packed = -(-(planes + (3 * levels if first else 0)) // GROUP) * ROWS
        total = (own[base:, :] + other[base:, :]) + (edge[packed:, :] + edge_other[packed:, :])
        if not far:
            out_sums[...] = total
            out_one[sent:, :] = total
            out_three[sent:, :] = total
            return
        at, near_at = count * ROWS, count * 8
        if first:
            last = jnp.where(lax.axis_index("gy") == 0, LANES - 1, cols - 1)
            lane = lanes_of((ROWS, LANES))
            bottom = lax.broadcasted_iota(jnp.int32, (ROWS, LANES), 0) == ROWS - 1
            for level in range(levels):
                kx, ky, wet = (
                    with_edge(tile(raw, kind * levels + level), edge, planes + kind * levels + level, cols) for kind in range(3)
                )
                put(planes + level, kx * wet * jnp.where(bottom, 1.0, pltpu.roll(wet, ROWS - 1, 0)))
                put(planes + levels + level, jnp.where(lane == last, 0.0, ky * wet * pltpu.roll(wet, LANES - 1, 1)))
                total = jnp.where(lax.broadcasted_iota(jnp.int32, total.shape, 0) == 1 + level, wet[:1], total)
        out_all[at:, :] = total
        out_near[near_at:, :] = total

    if not far:
        return kernel, [f32(base, LANES)] + [f32(sent + SUMS, LANES)] * 2 + [f32(SUMS, LANES)]
    return kernel, [f32(count * ROWS + SUMS, LANES), f32(count * 8 + SUMS, LANES)]


def is_even():
    return lax.rem(lax.axis_index("gx"), 2) == 0


def far_window(nat, index, own, first, near, third, slot):
    even = is_even()
    one, three = tile(first, slot), tile(third, slot)
    nat[index, 0:16, :] = tile(own, slot)
    nat[index, 16:32, :] = jnp.where(even, one, three)
    nat[index, 32:40, :] = tile(near, slot, 8)
    nat[index, 40:56, :] = jnp.where(even, three, one)


def shorten(nat, index):
    return jnp.concatenate([nat[index, 0:28, :], nat[index, 44:56, :]], axis=0)


def dealt(nat, index, tiles):
    return [nat[index, pl.ds(t, 8, stride=tiles), :] for t in range(tiles)]


def deal(buf, nat, index, tiles):
    for t, values in enumerate(dealt(nat, index, tiles)):
        buf[index, t * 8 : (t + 1) * 8, :] = values


def undeal(nat, buf, index, tiles):
    for t in range(tiles):
        nat[index, pl.ds(t, 8, stride=tiles), :] = buf[index, t * 8 : (t + 1) * 8, :]


def eight(ref, tiles, *index):
    return [ref[(*index, pl.ds(t * 8, 8), slice(None))] for t in range(tiles)]


def after(tiles):
    return tiles[1:] + [pltpu.roll(tiles[0], 7, 0)]


def run_steps(buf, spare, coef, steps, planes, levels, tiles):
    for number in range(KMAX):
        source, target = (buf, spare)[number % 2], (spare, buf)[number % 2]
        for level in range(levels):
            east, north, south = (eight(coef, tiles, kind, level) for kind in range(3))
            for field in range(planes // levels):
                plane = field * levels + level
                active = jnp.where(steps[field : field + 1, :] > float(number), 1.0, 0.0).astype(jnp.float32)
                u = eight(source, tiles, plane)
                flux_east = [c * (v - w) for c, v, w in zip(east, after(u), u, strict=True)]
                flux_west = [pltpu.roll(flux_east[-1], 1, 0)] + flux_east[:-1]
                for t in range(tiles):
                    to_north = north[t] * (pltpu.roll(u[t], LANES - 1, 1) - u[t])
                    to_south = south[t] * (pltpu.roll(u[t], 1, 1) - u[t])
                    change = (flux_east[t] - flux_west[t]) + (to_north + to_south)
                    target[plane, t * 8 : (t + 1) * 8, :] = u[t] + active * change


def own_sum(values, cols):
    return over_rows(jnp.where(lanes_of(values.shape) < cols, values, 0.0))


def window_scratch(planes):
    return [pltpu.VMEM((planes, WIN, LANES), jnp.float32)] * 2


def diffuse_own(out_g, field, buf, nat, coef, steps, planes, levels):
    for plane in range(planes):
        for t, values in enumerate(dealt(field, plane, NEAR_TILES)):
            buf[plane, t * 8 : (t + 1) * 8, :] = values
    run_steps(buf, nat, coef, steps, planes, levels, NEAR_TILES)
    for plane in range(planes):
        undeal(nat, buf, plane, NEAR_TILES)
        out_g[plane * ROWS : (plane + 1) * ROWS, :] = nat[plane, :ROWS, :]


def first_diffuse(planes, levels, cols):
    coefs = 2 * levels

    def kernel(own, first, near, third, steps, coef, coef_near, resid, weights, sums, out_g, buf, nat):
        even = is_even()
        at, near_at = (planes + coefs) * ROWS, (planes + coefs) * 8
        for index in range(coefs):
            far_window(nat, index, own, first, near, third, planes + index)
            if index < levels:
                row, near_row = at + 1 + index, near_at + 1 + index
                one, three = first[row : row + 1, :], third[row : row + 1, :]
                nat[index, 15:16, :] = nat[index, 15:16, :] * jnp.where(even, one, three)
                nat[index, 31:32, :] = nat[index, 31:32, :] * near[near_row : near_row + 1, :]
                nat[index, 39:40, :] = nat[index, 39:40, :] * jnp.where(even, three, one)
                nat[index, 55:56, :] = nat[index, 55:56, :] * own[row : row + 1, :]
            buf[index, : 8 * NEAR_TILES, :] = shorten(nat, index)
            kind, level = divmod(index, levels)
            for target, window, tiles in ((coef, nat, TILES), (coef_near, buf, NEAR_TILES)):
                for t, values in enumerate(dealt(window, index, tiles)):
                    target[kind, level, t * 8 : (t + 1) * 8, :] = values
                    if kind == 1:
                        target[2, level, t * 8 : (t + 1) * 8, :] = pltpu.roll(values, 1, 1)
        for plane in range(planes):
            far_window(nat, plane, own, first, near, third, plane)
            deal(buf, nat, plane, TILES)
        sent = slice(at, at + 1)
        total = (own[sent, :] + first[sent, :]) + (near[near_at : near_at + 1, :] + third[sent, :])
        weights[...] = off_diagonal(total, ROWS)
        run_steps(buf, nat, coef, steps, planes, levels, TILES)
        squares = jnp.zeros((ROWS, LANES), jnp.float32)
        for plane in range(planes):
            undeal(nat, buf, plane, TILES)
            value = SQRT_STATIC * shorten(nat, plane)
            resid[plane] = value
            squares += value[:ROWS] * value[:ROWS]
        sums[...] = jnp.zeros(sums.shape, jnp.float32)
        sums[4:5, :] = own_sum(squares, cols)
        diffuse_own(out_g, resid, buf, nat, coef_near, steps, planes, levels)

    outs = [
        f32(3, levels, WIN, LANES),
        f32(3, levels, 8 * NEAR_TILES, LANES),
        f32(planes, 8 * NEAR_TILES, LANES),
        f32(ROWS, LANES),
        f32(SUMS, LANES),
        f32(planes * ROWS, LANES),
    ]
    return kernel, outs, window_scratch(planes)


def second_diffuse(planes, levels, cols):
    def kernel(
        own, first, near, third, steps, coef, coef_near, resid, weights, image, new, new_w, sums, facts, out_g, buf, nat, field
    ):
        for plane in range(planes):
            far_window(nat, plane, own, first, near, third, plane)
            deal(buf, nat, plane, TILES)
        at, near_at = planes * ROWS, planes * 8
        sent = slice(at, at + 1)
        total = (own[sent, :] + first[sent, :]) + (near[near_at : near_at + 1, :] + third[sent, :])
        total = off_diagonal(total, ROWS + SUMS)
        energy = total[ROWS : ROWS + 1]
        rr = total[ROWS + 4 : ROWS + 5] + over_rows(weights[...] * weights[...])
        step = rr / (rr + energy)
        new_w[...] = weights[...] - step * (weights[...] + total[:ROWS])
        facts[...] = jnp.zeros(facts.shape, jnp.float32)
        facts[0:1, :] = rr
        facts[1:2, :] = step
        run_steps(buf, nat, coef, steps, planes, levels, TILES)
        squares = jnp.zeros((ROWS, LANES), jnp.float32)
        cross = jnp.zeros((ROWS, LANES), jnp.float32)
        for plane in range(planes):
            undeal(nat, buf, plane, TILES)
            direction = resid[plane]
            image_now = direction + SQRT_STATIC * shorten(nat, plane)
            value = direction - step * image_now
            field[plane] = value
            image[plane] = image_now[:ROWS]
            new[plane] = value[:ROWS]
            squares += value[:ROWS] * value[:ROWS]
            cross += value[:ROWS] * direction[:ROWS]
        sums[...] = jnp.zeros(sums.shape, jnp.float32)
        sums[4:5, :] = own_sum(squares, cols)
        sums[5:6, :] = own_sum(cross, cols)
        diffuse_own(out_g, field, buf, nat, coef_near, steps, planes, levels)

    block = f32(planes, ROWS, LANES)
    outs = [block, block, f32(ROWS, LANES), f32(SUMS, LANES), f32(SUMS, LANES), f32(planes * ROWS, LANES)]
    return kernel, outs, window_scratch(planes) + [pltpu.VMEM((planes, 8 * NEAR_TILES, LANES), jnp.float32)]


def last_diffuse(planes, levels, cols):
    def kernel(own, one, three, sums, steps, coef, out_g, out_sums, buf, nat):
        even = is_even()
        gap_rows = jnp.zeros((4, LANES), jnp.float32)
        for plane in range(planes):
            first, third = tile(one, plane, KMAX), tile(three, plane, KMAX)
            nat[plane, 0:16, :] = tile(own, plane)
            nat[plane, 16:26, :] = jnp.where(even, first, third)
            nat[plane, 26:30, :] = gap_rows
            nat[plane, 30:40, :] = jnp.where(even, third, first)
            deal(buf, nat, plane, NEAR_TILES)
        sent = one.shape[0] - SUMS
        out_sums[0] = sums[...] + one[sent:, :]
        out_sums[1] = three[sent:, :]
        run_steps(buf, nat, coef, steps, planes, levels, NEAR_TILES)
        for plane in range(planes):
            undeal(nat, buf, plane, NEAR_TILES)
            out_g[plane] = nat[plane, :ROWS, :]

    return kernel, [f32(planes, ROWS, LANES), f32(2, SUMS, LANES)], window_scratch(planes)


def finish(planes, cols):
    def kernel(diffused, sums, sums_two, resid, weights, image, new, new_w, facts, control, control_w, final):
        lanes = sums[0] + (sums_two[...] + sums[1])
        total = spread(lanes)
        rr, step = facts[0:1, :], facts[1:2, :]
        new_rr = total[4:5] + over_rows(new_w[...] * new_w[...])
        cross_rr = total[5:6] + over_rows(new_w[...] * weights[...])
        ratio = new_rr / rr
        gap = ratio - lanes[2:3]
        energy = spread(lanes[0:1] + gap * (2.0 * lanes[1:2] + gap * lanes[3:4]))
        squares = new_rr + ratio * (2.0 * cross_rr + ratio * rr)
        new_step = new_rr / (squares + energy)
        combined = step * weights[...] + new_step * (new_w[...] + ratio * weights[...])
        diagonal = lax.broadcasted_iota(jnp.int32, combined.shape, 0) == lanes_of(combined.shape)
        control_w[...] = over_rows(jnp.where(diagonal, combined, 0.0))[:, :ROWS]
        for plane in range(planes):
            direction, value = resid[plane, :ROWS, :], new[plane]
            new_direction = value + ratio * direction
            new_image = (value + SQRT_STATIC * diffused[plane]) + ratio * image[plane]
            control[plane] = (step * direction + new_step * new_direction)[:, :cols]
            final[plane] = (value - new_step * new_image)[:, :cols]

    return kernel, [f32(planes, ROWS, cols), f32(1, ROWS), f32(planes, ROWS, cols)]


def moved_to(values, x, y, z):
    sizes = [lax.axis_size(axis) for axis in AXES]
    here = [(a, b, c) for a in range(sizes[0]) for b in range(sizes[1]) for c in range(sizes[2])]
    number = {place: index for index, place in enumerate(here)}
    return lax.ppermute(values, AXES, [(number[a, b, c], number[a ^ x, b ^ y, c ^ z]) for a, b, c in here])


def mix_round(kernel_of, out_z, out_e, vert, raw=None):
    other = moved_to(out_z, 0, 0, 1)
    edge = moved_to(out_e, 0, 1, 0)
    edge_other = moved_to(out_e, 0, 1, 1)
    kernel, outs = kernel_of
    args = (out_z, other, edge, edge_other, vert)
    if raw is not None:
        args += (raw,)
    return call(kernel, outs, [VMEM] * len(args), args)


def far_round(own, near):
    return own, moved_to(own, 1, 0, 0), moved_to(near, 2, 0, 0), moved_to(own, 3, 0, 0)


def shards_small(
    innovation, obs_precision, error_scale, kappa_x, kappa_y, sea_mask, members, vertical, diffusion_steps
):
    fields, levels, rows, cols = innovation.shape
    count = members.shape[0]
    planes = fields * levels
    block = (planes, rows, cols)
    innov, prec, scale = (a.reshape(block) for a in (innovation, obs_precision, error_scale))
    ens = members.reshape((count,) + block)
    vert = jnp.broadcast_to(vertical.reshape(-1, 1), (vertical.size, LANES))
    steps = jnp.broadcast_to(diffusion_steps.astype(jnp.float32)[:, None], (fields, LANES))

    kernel, outs, scratch = start(planes, levels, cols, count)
    args = (innov, prec, scale, sea_mask, kappa_x, kappa_y, ens)
    args = [pltpu.with_memory_space_constraint(a, pltpu.HBM) for a in args]
    out_z, out_e, raw = call(kernel, outs, [HBM] * 7, args, scratch)
    vert, steps = call(tables, [f32(*vert.shape), f32(*steps.shape)], [VMEM] * 3, (vert, steps, out_e))
    parts = far_round(*mix_round(mix_back(True, True, planes, levels, cols), out_z, out_e, vert, raw))
    kernel, outs, scratch = first_diffuse(planes, levels, cols)
    coef, coef_near, resid, weights, sums, out_g = call(kernel, outs, [VMEM] * 5, (*parts, steps), scratch)

    kernel, outs = ensemble_part(planes, cols, count)
    (part,) = call(kernel, outs, [VMEM] * 2, (weights, ens))
    kernel, outs, scratch = observe(planes, levels, cols, count, True)
    args = (out_g, moved_to(out_g, 0, 0, 1), part, sums, vert, prec, scale, sea_mask, ens)
    out_z, out_e, seen = call(kernel, outs, [VMEM] * 9, args, scratch)
    parts = far_round(*mix_round(mix_back(False, True, planes, levels, cols), out_z, out_e, vert))
    kernel, outs, scratch = second_diffuse(planes, levels, cols)
    args = (*parts, steps, coef, coef_near, resid, weights)
    image, new, new_w, sums, facts, out_g = call(kernel, outs, [VMEM] * 9, args, scratch)

    kernel, outs = ensemble_part(planes, cols, count)
    (part,) = call(kernel, outs, [VMEM] * 2, (new_w, ens))
    kernel, outs, scratch = observe(planes, levels, cols, count, False)
    args = (out_g, moved_to(out_g, 0, 0, 1), part, sums, vert, prec, scale, sea_mask, seen)
    out_z, out_e = call(kernel, outs, [VMEM] * 9, args, scratch)
    own, one, three, sums = mix_round(mix_back(False, False, planes, levels, cols), out_z, out_e, vert)
    sums_two = moved_to(sums, 2, 0, 0)
    kernel, outs, scratch = last_diffuse(planes, levels, cols)
    args = (own, moved_to(one, 1, 0, 0), moved_to(three, 3, 0, 0), sums, steps, coef_near)
    diffused, sums = call(kernel, outs, [VMEM] * 6, args, scratch)
    kernel, outs = finish(planes, cols)
    args = (diffused, sums, sums_two, resid, weights, image, new, new_w, facts)
    control, control_w, final = call(kernel, outs, [VMEM] * 9, args)
    return control.reshape(innovation.shape), control_w.reshape(count), final.reshape(innovation.shape)


def shards(innovation, obs_precision, error_scale, kappa_x, kappa_y, sea_mask, members, vertical, diffusion_steps):
    arrays = (innovation, obs_precision, error_scale, kappa_x, kappa_y, sea_mask, members, vertical, diffusion_steps)
    sizes = tuple(lax.axis_size(axis) for axis in AXES)
    rows, cols = innovation.shape[2:]
    fits = rows == ROWS and members.shape[0] == ROWS and DEPTH <= cols <= LANES - DEPTH and ITERS == 2
    if sizes == (4, 2, 2) and fits:
        return shards_small(*arrays)
    return shards_any(*arrays)


def solution(mesh):
    placed = (
        P("grp", "gz", "gx", "gy"),
        P("grp", "gz", "gx", "gy"),
        P(None, "gz", "gx", "gy"),
        P("gz", "gx", "gy"),
        P("gz", "gx", "gy"),
        P("gz", "gx", "gy"),
        P("grp", None, "gz", "gx", "gy"),
        P(),
        P(),
    )
    return jax.shard_map(
        shards,
        mesh=mesh,
        in_specs=placed,
        out_specs=(P("grp", "gz", "gx", "gy"), P("grp"), P("grp", "gz", "gx", "gy")),
        check_vma=False,
    )
```

```python
import functools
import math


import jax
import jax.numpy as jnp
from jax import lax
from jax.experimental import pallas as pl
from jax.experimental.pallas import tpu as pltpu
from jax.sharding import PartitionSpec as P

KMAX = 10
ITERS = 2


static_share = 0.6
ensemble_share = 0.4


def extended(cells, sides, width):
    for axis, dim in sides:
        count = lax.axis_size(axis)
        head = lax.slice_in_dim(cells, 0, width, axis=dim)
        tail = lax.slice_in_dim(cells, cells.shape[dim] - width, cells.shape[dim], axis=dim)
        cells = jnp.concatenate(
            [
                lax.ppermute(tail, axis, [(i, (i + 1) % count) for i in range(count)]),
                cells,
                lax.ppermute(head, axis, [((i + 1) % count, i) for i in range(count)]),
            ],
            axis=dim,
        )
    return cells


def level_mix(source, mixing):
    local_levels = source.shape[1]
    gathered = lax.all_gather(source, "gz", axis=1, tiled=True)
    own_rows = lax.dynamic_slice_in_dim(
        mixing, lax.axis_index("gz") * local_levels, local_levels, 1
    )
    return jnp.einsum("flk,fkxy->flxy", own_rows, gathered, precision=lax.Precision.HIGHEST)


def diffuse(source, padded, step_counts, halo_depth):
    current = source
    for segment in range(KMAX // halo_depth):
        current = extended(current, (("gx", 2), ("gy", 3)), halo_depth)
        for substep in range(halo_depth):
            number = segment * halo_depth + substep
            offset = KMAX - halo_depth + substep
            rows_now = current.shape[2]
            cols_now = current.shape[3]
            window = padded[:, :, offset : offset + rows_now, offset : offset + cols_now]
            east_kappa = window[0]
            north_kappa = window[1]
            wet_window = window[2]
            east_coef = east_kappa[:, :-1, :] * wet_window[:, :-1, :] * wet_window[:, 1:, :]
            flux_east = east_coef * (current[:, :, 1:, :] - current[:, :, :-1, :])
            div_east = (flux_east[:, :, 1:, :] - flux_east[:, :, :-1, :])[:, :, :, 1:-1]
            north_coef = north_kappa[:, :, :-1] * wet_window[:, :, :-1] * wet_window[:, :, 1:]
            flux_north = north_coef * (current[:, :, :, 1:] - current[:, :, :, :-1])
            div_north = (flux_north[:, :, :, 1:] - flux_north[:, :, :, :-1])[:, :, 1:-1, :]
            active = (step_counts > number).astype(jnp.float32)[:, None, None, None]
            current = current[:, :, 1:-1, 1:-1] + active * (div_east + div_north)
    return current


def both_sums(terms, partial_value):
    return lax.psum((terms, partial_value), ("gx", "gy", "gz"))


def squares(resid_field):
    return lax.psum(jnp.sum(resid_field * resid_field), ("gx", "gy", "gz"))


def shards_any(
    innovation,
    obs_precision,
    error_scale,
    kappa_x,
    kappa_y,
    sea_mask,
    members,
    vertical,
    diffusion_steps,
):
    wet_cells = sea_mask.astype(jnp.float32)
    coefficients = jnp.stack([kappa_x, kappa_y, wet_cells])
    padded = extended(coefficients, (("gx", 2), ("gy", 3)), KMAX)
    cols_dev = wet_cells.shape[2]
    y_position = (
        lax.axis_index("gy") * cols_dev + jnp.arange(cols_dev + 2 * KMAX, dtype=jnp.int32) - KMAX
    )
    inside = ((y_position >= 0) & (y_position < cols_dev * lax.axis_size("gy"))).astype(jnp.float32)
    padded = jnp.stack([padded[0], padded[1], padded[2] * inside[None, None, :]])
    halo_depth = 2
    transposed = jnp.swapaxes(vertical, 1, 2)
    sqrt_static = math.sqrt(static_share)
    ens_scale = math.sqrt(ensemble_share / (members.shape[0] - 1))

    def static_back(masked):
        return sqrt_static * diffuse(
            level_mix(error_scale * masked, transposed), padded, diffusion_steps, halo_depth
        )

    def ensemble_terms(masked):
        return jnp.einsum("mflxy,flxy->m", members, masked, precision=lax.Precision.HIGHEST)

    masked = wet_cells * (obs_precision * innovation)
    resid_field = static_back(masked)
    ens_sum, field_norm = both_sums(ensemble_terms(masked), jnp.sum(resid_field * resid_field))
    resid_weights = ens_scale * ens_sum
    norm_now = field_norm + jnp.sum(resid_weights * resid_weights)
    dir_field, dir_weights = (resid_field, resid_weights)
    control_field = jnp.zeros_like(resid_field)
    control_weights = jnp.zeros(resid_weights.shape, jnp.float32)
    for iteration in range(ITERS):
        static = error_scale * level_mix(
            diffuse(dir_field, padded, diffusion_steps, halo_depth), vertical
        )
        ensemble = jnp.einsum(
            "m,mflxy->flxy", dir_weights, members, precision=lax.Precision.HIGHEST
        )
        observed = wet_cells * (sqrt_static * static + ens_scale * ensemble)
        weighted = obs_precision * observed
        masked = wet_cells * weighted
        image_field = dir_field + static_back(masked)
        ens_sum, curve_part = both_sums(ensemble_terms(masked), jnp.sum(dir_field * image_field))
        image_weights = dir_weights + ens_scale * ens_sum
        curvature = curve_part + jnp.sum(dir_weights * image_weights)
        step_length = norm_now / curvature
        control_field = control_field + step_length * dir_field
        control_weights = control_weights + step_length * dir_weights
        resid_field = resid_field - step_length * image_field
        resid_weights = resid_weights - step_length * image_weights
        if iteration + 1 < ITERS:
            norm_next = squares(resid_field) + jnp.sum(resid_weights * resid_weights)
            ratio_next = norm_next / norm_now
            dir_field = resid_field + ratio_next * dir_field
            dir_weights = resid_weights + ratio_next * dir_weights
            norm_now = norm_next
    return (control_field, control_weights, resid_field)

ROWS = 16
WIN = 56
TILES = WIN // 8
NEAR_TILES = 5
LANES = 128
DEPTH = 2 * KMAX
GROUP = LANES // DEPTH
SUMS = 8
FETCHES = 4
AXES = ("gx", "gy", "gz")
VMEM = pl.BlockSpec(memory_space=pltpu.VMEM)
HBM = pl.BlockSpec(memory_space=pltpu.HBM)
SQRT_STATIC = math.sqrt(static_share)


def f32(*shape):
    return jax.ShapeDtypeStruct(shape, jnp.float32)


def call(kernel, outs, specs, args, scratch=(), grant=32):
    return pl.pallas_call(
        kernel,
        out_shape=outs,
        in_specs=specs,
        out_specs=[VMEM] * len(outs),
        scratch_shapes=list(scratch),
        compiler_params=pltpu.CompilerParams(vmem_limit_bytes=grant * 1024 * 1024),
    )(*args)


def lanes_of(shape):
    return lax.broadcasted_iota(jnp.int32, shape, len(shape) - 1)


def tile(ref, index, size=ROWS):
    return ref[index * size : (index + 1) * size, :]


def pack_edges(out_ref, planes, cols):
    first = jnp.where(lax.axis_index("gy") == 0, cols - DEPTH, 0)
    lane = lanes_of((ROWS, LANES))
    for group in range(-(-len(planes) // GROUP)):
        packed = jnp.zeros((ROWS, LANES), jnp.float32)
        for slot, plane in enumerate(planes[group * GROUP : (group + 1) * GROUP]):
            moved = pltpu.roll(plane, lax.rem(DEPTH * slot - first + LANES, LANES), 1)
            packed = jnp.where((lane >= DEPTH * slot) & (lane < DEPTH * (slot + 1)), moved, packed)
        out_ref[group * ROWS : (group + 1) * ROWS, :] = packed


def with_edge(own, edge_ref, index, cols):
    group, slot = divmod(index, GROUP)
    moved = pltpu.roll(tile(edge_ref, group), (cols - DEPTH * slot) % LANES, 1)
    return jnp.where(lanes_of(own.shape) < cols, own, moved)


def over_rows(values):
    return jnp.sum(values, axis=0, keepdims=True)


def whole(values):
    return jnp.sum(over_rows(values), axis=1, keepdims=True)


def on_diagonal(values):
    rows = lax.broadcasted_iota(jnp.int32, values.shape, 0)
    return over_rows(jnp.where(rows == lanes_of(values.shape), values, 0.0))


def off_diagonal(row, count):
    shape = (count, LANES)
    rows = lax.broadcasted_iota(jnp.int32, shape, 0)
    return spread(jnp.where(rows == lanes_of(shape), jnp.broadcast_to(row, shape), 0.0))


def spread(values):
    return jnp.broadcast_to(jnp.sum(values, axis=1, keepdims=True), values.shape)


def coefficient_planes(coef, sources, levels, cols):
    coef[...] = jnp.zeros(coef.shape, jnp.float32)
    for level in range(levels):
        for kind, source in enumerate(sources):
            at = (kind * levels + level) * ROWS
            coef[at : at + ROWS, :cols] = source[level].astype(jnp.float32)


def project(stack, at, totals, scale):
    for m, total in enumerate(totals):
        stack[at + m : at + m + 1, : total.shape[1]] = scale * over_rows(total)


def start(planes, levels, cols, count):
    ens_scale = math.sqrt(ensemble_share / (count - 1))
    base = planes * ROWS
    edge_rows = -(-(planes + 3 * levels) // GROUP) * ROWS

    def kernel(*refs):
        sources, (out_z, out_e, coef), copies, (weighted, stack, sems) = refs[:7], refs[7:10], refs[10:17], refs[17:]
        pairs = list(zip(sources[:6], copies[:6], strict=True))
        for part in range(FETCHES):
            rows = pl.ds(part * (count // FETCHES), count // FETCHES)
            pairs.append((sources[6].at[rows], copies[6].at[rows]))
        moves = [pltpu.make_async_copy(a, b, sems.at[i]) for i, (a, b) in enumerate(pairs)]
        for move in moves:
            move.start()
        innov, prec, scale, mask, kx, ky, members = copies
        out_z[...] = jnp.zeros(out_z.shape, jnp.float32)
        stack[...] = jnp.zeros(stack.shape, jnp.float32)
        for move in moves[:6]:
            move.wait()
        coefficient_planes(coef, (kx, ky, mask), levels, cols)
        for plane in range(planes):
            weighted[plane] = mask[plane % levels].astype(jnp.float32) * (prec[plane] * innov[plane])
            out_z[plane * ROWS : (plane + 1) * ROWS, :cols] = scale[plane] * weighted[plane]
        edges = [tile(out_z, plane) for plane in range(planes)]
        pack_edges(out_e, edges + [tile(coef, index) for index in range(3 * levels)], cols)
        each = count // FETCHES
        for part in range(FETCHES):
            moves[6 + part].wait()
            totals = [jnp.zeros((ROWS, cols), jnp.float32) for _ in range(each)]
            for plane in range(planes):
                for m in range(each):
                    totals[m] += members[part * each + m, plane] * weighted[plane]
            project(stack, part * each, totals, ens_scale)
        out_z[base : base + 1, :] = on_diagonal(spread(stack[...]))
        out_e[edge_rows:, :] = out_z[base:, :]

    outs = [f32(base + SUMS, LANES), f32(edge_rows + SUMS, LANES), f32(3 * levels * ROWS, LANES)]
    field, flat = (planes, ROWS, cols), (levels, ROWS, cols)
    kept = [(field, jnp.float32)] * 3 + [(flat, jnp.int32)] + [(flat, jnp.float32)] * 2 + [((count,) + field, jnp.float32)]
    scratch = [pltpu.VMEM(*one) for one in kept] + [pltpu.VMEM(field, jnp.float32), pltpu.VMEM((ROWS, LANES), jnp.float32)]
    scratch.append(pltpu.SemaphoreType.DMA((6 + FETCHES,)))
    return kernel, outs, scratch


def tables(vert, steps, _, out_vert, out_steps):
    out_vert[...] = vert[...]
    out_steps[...] = steps[...]


def ensemble_part(planes, cols, count):
    ens_scale = math.sqrt(ensemble_share / (count - 1))

    def kernel(weights, members, out):
        for plane in range(planes):
            total = jnp.zeros((ROWS, cols), jnp.float32)
            for m in range(count):
                total += weights[m : m + 1, :cols] * members[m, plane]
            out[plane] = ens_scale * total

    return kernel, [f32(planes, ROWS, cols)]


def observe(planes, levels, cols, count, with_weights):
    ens_scale = math.sqrt(ensemble_share / (count - 1))
    base = planes * ROWS
    edge_rows = -(-planes // GROUP) * ROWS

    def kernel(*refs):
        own, other, ensemble, sums, vert, prec, scale, mask = refs[:8]
        if with_weights:
            members, out_z, out_e, seen, stack = refs[8:]
        else:
            seen, out_z, out_e, now = refs[8:]
        out_z[...] = jnp.zeros(out_z.shape, jnp.float32)
        totals = [jnp.zeros((ROWS, cols), jnp.float32) for _ in range(count)]
        energy = jnp.zeros((ROWS, cols), jnp.float32)
        cross = jnp.zeros((ROWS, cols), jnp.float32)
        here = lax.axis_index("gz") * levels
        there = (1 - lax.axis_index("gz")) * levels
        for plane in range(planes):
            field, level = divmod(plane, levels)
            wet = mask[level].astype(jnp.float32)
            static = jnp.zeros((ROWS, cols), jnp.float32)
            for k in range(levels):
                row = (field * 2 * levels + here + level) * 2 * levels
                static += vert[pl.ds(row + here + k, 1), :cols] * tile(own, field * levels + k)[:, :cols]
                static += vert[pl.ds(row + there + k, 1), :cols] * tile(other, field * levels + k)[:, :cols]
            seen_now = wet * (SQRT_STATIC * (scale[plane] * static) + ensemble[plane])
            weighted = wet * (prec[plane] * seen_now)
            if with_weights:
                seen[plane] = seen_now
                energy += seen_now * weighted
                for m in range(count):
                    totals[m] += members[m, plane] * weighted
            else:
                now[plane] = seen_now
                before = seen[plane]
                energy += before * (prec[plane] * before)
                cross += before * weighted
            out_z[plane * ROWS : (plane + 1) * ROWS, :cols] = scale[plane] * weighted
        if with_weights:
            stack[:ROWS, :] = jnp.zeros((ROWS, LANES), jnp.float32)
            project(stack, 0, totals, ens_scale)
            stack[ROWS:, :] = sums[...]
            stack[ROWS : ROWS + 1, :cols] = over_rows(energy)
            out_z[base : base + 1, :] = on_diagonal(spread(stack[...]))
        else:
            out_z[base:, :] = sums[...]
            energy, cross = whole(energy), whole(cross)
            share = jnp.where(energy > 0.0, -cross / jnp.where(energy > 0.0, energy, 1.0), 0.0)
            rest = jnp.zeros((ROWS, cols), jnp.float32)
            left = jnp.zeros((ROWS, cols), jnp.float32)
            for plane in range(planes):
                before = seen[plane]
                gap = now[plane] + share * before
                rest += gap * (prec[plane] * gap)
                left += before * (prec[plane] * gap)
            place = (lax.axis_index("gx") * 2 + lax.axis_index("gy")) * 2 + lax.axis_index("gz")
            own_lane = lanes_of((1, LANES)) == place
            for index, value in enumerate((whole(rest), whole(left), share, energy)):
                out_z[base + index : base + index + 1, :] = jnp.where(own_lane, value, 0.0)
        pack_edges(out_e, [tile(out_z, plane) for plane in range(planes)], cols)
        out_e[edge_rows:, :] = out_z[base:, :]

    outs = [f32(base + SUMS, LANES), f32(edge_rows + SUMS, LANES)]
    if with_weights:
        return kernel, outs + [f32(planes, ROWS, cols)], [pltpu.VMEM((ROWS + SUMS, LANES), jnp.float32)]
    return kernel, outs, [pltpu.VMEM((planes, ROWS, cols), jnp.float32)]


def mix_back(first, far, planes, levels, cols):
    base = planes * ROWS
    coefs = 2 * levels if first else 0
    fields = planes // levels
    count = planes + coefs
    sent = -(-planes * KMAX // 8) * 8

    def kernel(*refs):
        if first:
            own, other, edge, edge_other, vert, raw, out_all, out_near = refs
        elif far:
            own, other, edge, edge_other, vert, out_all, out_near = refs
        else:
            own, other, edge, edge_other, vert, out_own, out_one, out_three, out_sums = refs
        here = lax.axis_index("gz") * levels
        there = (1 - lax.axis_index("gz")) * levels
        even = lax.rem(lax.axis_index("gx"), 2) == 0
        upper = lax.broadcasted_iota(jnp.int32, (8, LANES), 0) < 4

        def put(index, values):
            if far:
                out_all[index * ROWS : (index + 1) * ROWS, :] = values
                out_near[index * 8 : (index + 1) * 8, :] = jnp.where(upper, values[:8], values[8:])
            else:
                out_own[index * ROWS : (index + 1) * ROWS, :] = values
                head, end = values[:KMAX], values[ROWS - KMAX :]
                out_one[index * KMAX : (index + 1) * KMAX, :] = jnp.where(even, end, head)
                out_three[index * KMAX : (index + 1) * KMAX, :] = jnp.where(even, head, end)

        for field in range(fields):
            mine = [with_edge(tile(own, field * levels + l), edge, field * levels + l, cols) for l in range(levels)]
            theirs = [
                with_edge(tile(other, field * levels + l), edge_other, field * levels + l, cols) for l in range(levels)
            ]
            for k in range(levels):
                mixed = jnp.zeros((ROWS, LANES), jnp.float32)
                for l in range(levels):
                    block = field * 2 * levels
                    mixed += vert[pl.ds((block + here + l) * 2 * levels + here + k, 1), :] * mine[l]
                    mixed += vert[pl.ds((block + there + l) * 2 * levels + here + k, 1), :] * theirs[l]
                put(field * levels + k, mixed)
        packed = -(-(planes + (3 * levels if first else 0)) // GROUP) * ROWS
        total = (own[base:, :] + other[base:, :]) + (edge[packed:, :] + edge_other[packed:, :])
        if not far:
            out_sums[...] = total
            out_one[sent:, :] = total
            out_three[sent:, :] = total
            return
        at, near_at = count * ROWS, count * 8
        if first:
            last = jnp.where(lax.axis_index("gy") == 0, LANES - 1, cols - 1)
            lane = lanes_of((ROWS, LANES))
            bottom = lax.broadcasted_iota(jnp.int32, (ROWS, LANES), 0) == ROWS - 1
            for level in range(levels):
                kx, ky, wet = (
                    with_edge(tile(raw, kind * levels + level), edge, planes + kind * levels + level, cols) for kind in range(3)
                )
                put(planes + level, kx * wet * jnp.where(bottom, 1.0, pltpu.roll(wet, ROWS - 1, 0)))
                put(planes + levels + level, jnp.where(lane == last, 0.0, ky * wet * pltpu.roll(wet, LANES - 1, 1)))
                total = jnp.where(lax.broadcasted_iota(jnp.int32, total.shape, 0) == 1 + level, wet[:1], total)
        out_all[at:, :] = total
        out_near[near_at:, :] = total

    if not far:
        return kernel, [f32(base, LANES)] + [f32(sent + SUMS, LANES)] * 2 + [f32(SUMS, LANES)]
    return kernel, [f32(count * ROWS + SUMS, LANES), f32(count * 8 + SUMS, LANES)]


def is_even():
    return lax.rem(lax.axis_index("gx"), 2) == 0


def far_window(nat, index, own, first, near, third, slot):
    even = is_even()
    one, three = tile(first, slot), tile(third, slot)
    nat[index, 0:16, :] = tile(own, slot)
    nat[index, 16:32, :] = jnp.where(even, one, three)
    nat[index, 32:40, :] = tile(near, slot, 8)
    nat[index, 40:56, :] = jnp.where(even, three, one)


def shorten(nat, index):
    return jnp.concatenate([nat[index, 0:28, :], nat[index, 44:56, :]], axis=0)


def dealt(nat, index, tiles):
    return [nat[index, pl.ds(t, 8, stride=tiles), :] for t in range(tiles)]


def deal(buf, nat, index, tiles):
    for t, values in enumerate(dealt(nat, index, tiles)):
        buf[index, t * 8 : (t + 1) * 8, :] = values


def undeal(nat, buf, index, tiles):
    for t in range(tiles):
        nat[index, pl.ds(t, 8, stride=tiles), :] = buf[index, t * 8 : (t + 1) * 8, :]


def eight(ref, tiles, *index):
    return [ref[(*index, pl.ds(t * 8, 8), slice(None))] for t in range(tiles)]


def after(tiles):
    return tiles[1:] + [pltpu.roll(tiles[0], 7, 0)]


def run_steps(buf, spare, coef, steps, planes, levels, tiles):
    for number in range(KMAX):
        source, target = (buf, spare)[number % 2], (spare, buf)[number % 2]
        for level in range(levels):
            east, north, south = (eight(coef, tiles, kind, level) for kind in range(3))
            for field in range(planes // levels):
                plane = field * levels + level
                active = jnp.where(steps[field : field + 1, :] > float(number), 1.0, 0.0).astype(jnp.float32)
                u = eight(source, tiles, plane)
                flux_east = [c * (v - w) for c, v, w in zip(east, after(u), u, strict=True)]
                flux_west = [pltpu.roll(flux_east[-1], 1, 0)] + flux_east[:-1]
                for t in range(tiles):
                    to_north = north[t] * (pltpu.roll(u[t], LANES - 1, 1) - u[t])
                    to_south = south[t] * (pltpu.roll(u[t], 1, 1) - u[t])
                    change = (flux_east[t] - flux_west[t]) + (to_north + to_south)
                    target[plane, t * 8 : (t + 1) * 8, :] = u[t] + active * change


def own_sum(values, cols):
    return over_rows(jnp.where(lanes_of(values.shape) < cols, values, 0.0))


def window_scratch(planes):
    return [pltpu.VMEM((planes, WIN, LANES), jnp.float32)] * 2


def diffuse_own(out_g, field, buf, nat, coef, steps, planes, levels):
    for plane in range(planes):
        for t, values in enumerate(dealt(field, plane, NEAR_TILES)):
            buf[plane, t * 8 : (t + 1) * 8, :] = values
    run_steps(buf, nat, coef, steps, planes, levels, NEAR_TILES)
    for plane in range(planes):
        undeal(nat, buf, plane, NEAR_TILES)
        out_g[plane * ROWS : (plane + 1) * ROWS, :] = nat[plane, :ROWS, :]


def first_diffuse(planes, levels, cols):
    coefs = 2 * levels

    def kernel(own, first, near, third, steps, coef, coef_near, resid, weights, sums, out_g, buf, nat):
        even = is_even()
        at, near_at = (planes + coefs) * ROWS, (planes + coefs) * 8
        for index in range(coefs):
            far_window(nat, index, own, first, near, third, planes + index)
            if index < levels:
                row, near_row = at + 1 + index, near_at + 1 + index
                one, three = first[row : row + 1, :], third[row : row + 1, :]
                nat[index, 15:16, :] = nat[index, 15:16, :] * jnp.where(even, one, three)
                nat[index, 31:32, :] = nat[index, 31:32, :] * near[near_row : near_row + 1, :]
                nat[index, 39:40, :] = nat[index, 39:40, :] * jnp.where(even, three, one)
                nat[index, 55:56, :] = nat[index, 55:56, :] * own[row : row + 1, :]
            buf[index, : 8 * NEAR_TILES, :] = shorten(nat, index)
            kind, level = divmod(index, levels)
            for target, window, tiles in ((coef, nat, TILES), (coef_near, buf, NEAR_TILES)):
                for t, values in enumerate(dealt(window, index, tiles)):
                    target[kind, level, t * 8 : (t + 1) * 8, :] = values
                    if kind == 1:
                        target[2, level, t * 8 : (t + 1) * 8, :] = pltpu.roll(values, 1, 1)
        for plane in range(planes):
            far_window(nat, plane, own, first, near, third, plane)
            deal(buf, nat, plane, TILES)
        sent = slice(at, at + 1)
        total = (own[sent, :] + first[sent, :]) + (near[near_at : near_at + 1, :] + third[sent, :])
        weights[...] = off_diagonal(total, ROWS)
        run_steps(buf, nat, coef, steps, planes, levels, TILES)
        squares = jnp.zeros((ROWS, LANES), jnp.float32)
        for plane in range(planes):
            undeal(nat, buf, plane, TILES)
            value = SQRT_STATIC * shorten(nat, plane)
            resid[plane] = value
            squares += value[:ROWS] * value[:ROWS]
        sums[...] = jnp.zeros(sums.shape, jnp.float32)
        sums[4:5, :] = own_sum(squares, cols)
        diffuse_own(out_g, resid, buf, nat, coef_near, steps, planes, levels)

    outs = [
        f32(3, levels, WIN, LANES),
        f32(3, levels, 8 * NEAR_TILES, LANES),
        f32(planes, 8 * NEAR_TILES, LANES),
        f32(ROWS, LANES),
        f32(SUMS, LANES),
        f32(planes * ROWS, LANES),
    ]
    return kernel, outs, window_scratch(planes)


def second_diffuse(planes, levels, cols):
    def kernel(
        own, first, near, third, steps, coef, coef_near, resid, weights, image, new, new_w, sums, facts, out_g, buf, nat, field
    ):
        for plane in range(planes):
            far_window(nat, plane, own, first, near, third, plane)
            deal(buf, nat, plane, TILES)
        at, near_at = planes * ROWS, planes * 8
        sent = slice(at, at + 1)
        total = (own[sent, :] + first[sent, :]) + (near[near_at : near_at + 1, :] + third[sent, :])
        total = off_diagonal(total, ROWS + SUMS)
        energy = total[ROWS : ROWS + 1]
        rr = total[ROWS + 4 : ROWS + 5] + over_rows(weights[...] * weights[...])
        step = rr / (rr + energy)
        new_w[...] = weights[...] - step * (weights[...] + total[:ROWS])
        facts[...] = jnp.zeros(facts.shape, jnp.float32)
        facts[0:1, :] = rr
        facts[1:2, :] = step
        run_steps(buf, nat, coef, steps, planes, levels, TILES)
        squares = jnp.zeros((ROWS, LANES), jnp.float32)
        cross = jnp.zeros((ROWS, LANES), jnp.float32)
        for plane in range(planes):
            undeal(nat, buf, plane, TILES)
            direction = resid[plane]
            image_now = direction + SQRT_STATIC * shorten(nat, plane)
            value = direction - step * image_now
            field[plane] = value
            image[plane] = image_now[:ROWS]
            new[plane] = value[:ROWS]
            squares += value[:ROWS] * value[:ROWS]
            cross += value[:ROWS] * direction[:ROWS]
        sums[...] = jnp.zeros(sums.shape, jnp.float32)
        sums[4:5, :] = own_sum(squares, cols)
        sums[5:6, :] = own_sum(cross, cols)
        diffuse_own(out_g, field, buf, nat, coef_near, steps, planes, levels)

    block = f32(planes, ROWS, LANES)
    outs = [block, block, f32(ROWS, LANES), f32(SUMS, LANES), f32(SUMS, LANES), f32(planes * ROWS, LANES)]
    return kernel, outs, window_scratch(planes) + [pltpu.VMEM((planes, 8 * NEAR_TILES, LANES), jnp.float32)]


def last_diffuse(planes, levels, cols):
    def kernel(own, three, one, sums, steps, coef, out_g, out_sums, buf, nat):
        even = is_even()
        gap_rows = jnp.zeros((4, LANES), jnp.float32)
        for plane in range(planes):
            first, third = tile(one, plane, KMAX), tile(three, plane, KMAX)
            nat[plane, 0:16, :] = tile(own, plane)
            nat[plane, 16:26, :] = jnp.where(even, first, third)
            nat[plane, 26:30, :] = gap_rows
            nat[plane, 30:40, :] = jnp.where(even, third, first)
            deal(buf, nat, plane, NEAR_TILES)
        sent = one.shape[0] - SUMS
        out_sums[0] = sums[...] + one[sent:, :]
        out_sums[1] = three[sent:, :]
        run_steps(buf, nat, coef, steps, planes, levels, NEAR_TILES)
        for plane in range(planes):
            undeal(nat, buf, plane, NEAR_TILES)
            out_g[plane] = nat[plane, :ROWS, :]

    return kernel, [f32(planes, ROWS, LANES), f32(2, SUMS, LANES)], window_scratch(planes)


def finish(planes, cols):
    def kernel(diffused, sums, sums_two, resid, weights, image, new, new_w, facts, control, control_w, final):
        lanes = sums[0] + (sums_two[...] + sums[1])
        total = spread(lanes)
        rr, step = facts[0:1, :], facts[1:2, :]
        new_rr = total[4:5] + over_rows(new_w[...] * new_w[...])
        cross_rr = total[5:6] + over_rows(new_w[...] * weights[...])
        ratio = new_rr / rr
        gap = ratio - lanes[2:3]
        energy = spread(lanes[0:1] + gap * (2.0 * lanes[1:2] + gap * lanes[3:4]))
        squares = new_rr + ratio * (2.0 * cross_rr + ratio * rr)
        new_step = new_rr / (squares + energy)
        combined = step * weights[...] + new_step * (new_w[...] + ratio * weights[...])
        diagonal = lax.broadcasted_iota(jnp.int32, combined.shape, 0) == lanes_of(combined.shape)
        control_w[...] = over_rows(jnp.where(diagonal, combined, 0.0))[:, :ROWS]
        for plane in range(planes):
            direction, value = resid[plane, :ROWS, :], new[plane]
            new_direction = value + ratio * direction
            new_image = (value + SQRT_STATIC * diffused[plane]) + ratio * image[plane]
            control[plane] = (step * direction + new_step * new_direction)[:, :cols]
            final[plane] = (value - new_step * new_image)[:, :cols]

    return kernel, [f32(planes, ROWS, cols), f32(1, ROWS), f32(planes, ROWS, cols)]


def moved_to(values, x, y, z):
    sizes = [lax.axis_size(axis) for axis in AXES]
    here = [(a, b, c) for a in range(sizes[0]) for b in range(sizes[1]) for c in range(sizes[2])]
    number = {place: index for index, place in enumerate(here)}
    return lax.ppermute(values, AXES, [(number[a, b, c], number[a ^ x, b ^ y, c ^ z]) for a, b, c in here])


def mix_round(kernel_of, out_z, out_e, vert, raw=None):
    other = moved_to(out_z, 0, 0, 1)
    edge = moved_to(out_e, 0, 1, 0)
    edge_other = moved_to(out_e, 0, 1, 1)
    kernel, outs = kernel_of
    args = (out_z, other, edge, edge_other, vert)
    if raw is not None:
        args += (raw,)
    return call(kernel, outs, [VMEM] * len(args), args)


def far_round(own, near):
    return own, moved_to(own, 1, 0, 0), moved_to(near, 2, 0, 0), moved_to(own, 3, 0, 0)


def shards_small(
    innovation, obs_precision, error_scale, kappa_x, kappa_y, sea_mask, members, vertical, diffusion_steps
):
    fields, levels, rows, cols = innovation.shape
    count = members.shape[0]
    planes = fields * levels
    block = (planes, rows, cols)
    innov, prec, scale = (a.reshape(block) for a in (innovation, obs_precision, error_scale))
    ens = members.reshape((count,) + block)
    vert = jnp.broadcast_to(vertical.reshape(-1, 1), (vertical.size, LANES))
    steps = jnp.broadcast_to(diffusion_steps.astype(jnp.float32)[:, None], (fields, LANES))

    kernel, outs, scratch = start(planes, levels, cols, count)
    args = (innov, prec, scale, sea_mask, kappa_x, kappa_y, ens)
    args = [pltpu.with_memory_space_constraint(a, pltpu.HBM) for a in args]
    out_z, out_e, raw = call(kernel, outs, [HBM] * 7, args, scratch)
    vert, steps = call(tables, [f32(*vert.shape), f32(*steps.shape)], [VMEM] * 3, (vert, steps, out_e))
    parts = far_round(*mix_round(mix_back(True, True, planes, levels, cols), out_z, out_e, vert, raw))
    kernel, outs, scratch = first_diffuse(planes, levels, cols)
    coef, coef_near, resid, weights, sums, out_g = call(kernel, outs, [VMEM] * 5, (*parts, steps), scratch)

    kernel, outs = ensemble_part(planes, cols, count)
    (part,) = call(kernel, outs, [VMEM] * 2, (weights, ens))
    kernel, outs, scratch = observe(planes, levels, cols, count, True)
    args = (out_g, moved_to(out_g, 0, 0, 1), part, sums, vert, prec, scale, sea_mask, ens)
    out_z, out_e, seen = call(kernel, outs, [VMEM] * 9, args, scratch)
    parts = far_round(*mix_round(mix_back(False, True, planes, levels, cols), out_z, out_e, vert))
    kernel, outs, scratch = second_diffuse(planes, levels, cols)
    args = (*parts, steps, coef, coef_near, resid, weights)
    image, new, new_w, sums, facts, out_g = call(kernel, outs, [VMEM] * 9, args, scratch)

    kernel, outs = ensemble_part(planes, cols, count)
    (part,) = call(kernel, outs, [VMEM] * 2, (new_w, ens))
    kernel, outs, scratch = observe(planes, levels, cols, count, False)
    args = (out_g, moved_to(out_g, 0, 0, 1), part, sums, vert, prec, scale, sea_mask, seen)
    out_z, out_e = call(kernel, outs, [VMEM] * 9, args, scratch)
    own, one, three, sums = mix_round(mix_back(False, False, planes, levels, cols), out_z, out_e, vert)
    sums_two = moved_to(sums, 2, 0, 0)
    kernel, outs, scratch = last_diffuse(planes, levels, cols)
    args = (own, moved_to(three, 3, 0, 0), moved_to(one, 1, 0, 0), sums, steps, coef_near)
    diffused, sums = call(kernel, outs, [VMEM] * 6, args, scratch)
    kernel, outs = finish(planes, cols)
    args = (diffused, sums, sums_two, resid, weights, image, new, new_w, facts)
    control, control_w, final = call(kernel, outs, [VMEM] * 9, args)
    return control.reshape(innovation.shape), control_w.reshape(count), final.reshape(innovation.shape)


def shards(innovation, obs_precision, error_scale, kappa_x, kappa_y, sea_mask, members, vertical, diffusion_steps):
    arrays = (innovation, obs_precision, error_scale, kappa_x, kappa_y, sea_mask, members, vertical, diffusion_steps)
    sizes = tuple(lax.axis_size(axis) for axis in AXES)
    rows, cols = innovation.shape[2:]
    fits = rows == ROWS and members.shape[0] == ROWS and DEPTH <= cols <= LANES - DEPTH and ITERS == 2
    if sizes == (4, 2, 2) and fits:
        return shards_small(*arrays)
    return shards_any(*arrays)


def solution(mesh):
    placed = (
        P("grp", "gz", "gx", "gy"),
        P("grp", "gz", "gx", "gy"),
        P(None, "gz", "gx", "gy"),
        P("gz", "gx", "gy"),
        P("gz", "gx", "gy"),
        P("gz", "gx", "gy"),
        P("grp", None, "gz", "gx", "gy"),
        P(),
        P(),
    )
    return jax.shard_map(
        shards,
        mesh=mesh,
        in_specs=placed,
        out_specs=(P("grp", "gz", "gx", "gy"), P("grp"), P("grp", "gz", "gx", "gy")),
        check_vma=False,
    )
```
